32 devices in a mesh: head: 2 (over core), blk: 16 (over z, y, x).
Axes of the slice: x: 2, y: 2, z: 4, core: 2. Of those that a mesh axis runs over, the one named last changes fastest.
Arguments:
- hidden: bfloat16 [4096, 1024], P(('blk', 'head')), may hold values from -6 to 6
- adapter_index: int32 [4096], P(('blk', 'head')), may hold values from 0 to 7
- first_gain: bfloat16 [1024], P(('head', 'blk')), may hold values from 0.5 to 1.5
- first_bias: bfloat16 [1024], P(('head', 'blk')), may hold values from -1.25 to 1.25
- triple_weight: bfloat16 [1024, 3072], P(('head', 'blk')), may hold values from -0.1875 to 0.1875
- triple_bias: bfloat16 [3072], P(('head', 'blk')), may hold values from -1.25 to 1.25
- mixer_weight: bfloat16 [1024, 1024], P(('head', 'blk')), may hold values from -6 to 6
- mixer_bias: bfloat16 [1024], P(('head', 'blk')), may hold values from -1.25 to 1.25
- second_gain: bfloat16 [1024], P(('head', 'blk')), may hold values from 0.5 to 1.5
- second_bias: bfloat16 [1024], P(('head', 'blk')), may hold values from -1.25 to 1.25
- expand_weight: bfloat16 [1024, 4096], P(('head', 'blk')), may hold values from -0.1875 to 0.1875
- expand_bias: bfloat16 [4096], P(('head', 'blk')), may hold values from -1.75 to 1.75
- reduce_weight: bfloat16 [4096, 1024], P(('head', 'blk')), may hold values from -0.09375 to 0.09375
- reduce_bias: bfloat16 [1024], P(('head', 'blk')), may hold values from -1.25 to 1.25
- triple_down: bfloat16 [8, 1024, 16], replicated, may hold values from -0.1875 to 0.1875
- triple_up: bfloat16 [8, 16, 3072], replicated, may hold values from -0.75 to 0.75
- mixer_down: bfloat16 [8, 1024, 16], replicated, may hold values from -6 to 6
- mixer_up: bfloat16 [8, 16, 1024], replicated, may hold values from -0.75 to 0.75
- expand_down: bfloat16 [8, 1024, 16], replicated, may hold values from -0.1875 to 0.1875
- expand_up: bfloat16 [8, 16, 4096], replicated, may hold values from -0.75 to 0.75
- reduce_down: bfloat16 [8, 4096, 16], replicated, may hold values from -0.09375 to 0.09375
- reduce_up: bfloat16 [8, 16, 1024], replicated, may hold values from -0.75 to 0.75
- cotangent: bfloat16 [4096, 1024], P(('blk', 'head')), may hold values from -6 to 6
Outputs:
- layer_out: bfloat16 [4096, 1024], P(('blk', 'head'))
- hidden_grad: bfloat16 [4096, 1024], P(('blk', 'head'))
- triple_down_grad: float32 [8, 1024, 16], replicated
- triple_up_grad: float32 [8, 16, 3072], replicated
- mixer_down_grad: float32 [8, 1024, 16], replicated
- mixer_up_grad: float32 [8, 16, 1024], replicated
- expand_down_grad: float32 [8, 1024, 16], replicated
- expand_up_grad: float32 [8, 16, 4096], replicated
- reduce_down_grad: float32 [8, 4096, 16], replicated
- reduce_up_grad: float32 [8, 16, 1024], replicated
The draws below stay inside these ranges and needn't reach their ends.
All inputs are finite; a program needn't handle non-finite values.
Results may differ from the reference program's by a relative error of at most 0.018.
Values may be sent and summed in bfloat16 or wider, within the bound.
A program may use at most 384 MiB of HBM per device.

```python
import math
import jax
import jax.numpy as jnp
from jax import lax

WIDTH = 1024
HEADS = 16
HEAD_DIM = 64
INNER = 4096
RANK = 16
ADAPTERS = 8
BLOCK = 256
SEQ = 4096


def place_ends(values, key, least, top_value):
    place = [jax.random.randint(jax.random.fold_in(key, axis), (), 0, length) for axis, length in enumerate(values.shape)]
    widest = values.shape.index(max(values.shape))
    neighbour = place[:widest] + [(place[widest] + 1) % values.shape[widest]] + place[widest + 1:]
    return values.at[tuple(place)].set(least).at[tuple(neighbour)].set(top_value)


def block_levels(key, dims, pieces, low, top_value):
    gain, own = 1.0, jax.random.fold_in(key, 6)
    for axis_at, parts in pieces:
        draws = jnp.exp(jax.random.uniform(jax.random.fold_in(own, axis_at), (parts,), jnp.float32, low / len(pieces), top_value / len(pieces)))
        gain = gain * jnp.repeat(draws, dims[axis_at] // parts).reshape([-1 if axis == axis_at else 1 for axis in range(len(dims))])
    return gain


def noise(own_key, shape, deviation, limit, cuts=(), held_as=jnp.bfloat16):
    loudness = block_levels(own_key, shape, cuts, -0.22, 0.18) if cuts else 1.0
    values = jax.random.normal(own_key, shape, jnp.float32) * deviation * loudness
    return jnp.minimum(jnp.maximum(values, -limit), limit).astype(held_as)


def setup_inputs(seed: int = 0) -> dict:
    splits = jax.random.split(jax.random.key(seed), 24)
    hidden = noise(splits[0], (SEQ, WIDTH), 1.0, 6.0, ((0, 32),))
    adapter_index = place_ends(jax.random.randint(splits[1], (SEQ,), 0, ADAPTERS), jax.random.fold_in(splits[1], 1), 0, ADAPTERS - 1).astype(jnp.int32)
    first_gain = jnp.clip(1.0 + 0.1 * jax.random.normal(splits[2], (WIDTH,), jnp.float32), 0.5, 1.5).astype(jnp.bfloat16)
    first_bias = noise(splits[3], (WIDTH,), 0.2, 1.25, ((0, 32),))
    triple_weight = noise(splits[4], (WIDTH, 3 * WIDTH), WIDTH ** -0.5, 0.1875, ((0, 32),))
    triple_bias = noise(splits[5], (3 * WIDTH,), 0.2, 1.25, ((0, 32),))
    mixer_weight = noise(splits[6], (WIDTH, WIDTH), 1.0, 6.0, ((0, 32),))
    mixer_bias = noise(splits[7], (WIDTH,), 0.2, 1.25, ((0, 32),))
    second_gain = jnp.clip(1.0 + 0.1 * jax.random.normal(splits[8], (WIDTH,), jnp.float32), 0.5, 1.5).astype(jnp.bfloat16)
    second_bias = noise(splits[9], (WIDTH,), 0.2, 1.25, ((0, 32),))
    expand_weight = noise(splits[10], (WIDTH, INNER), WIDTH ** -0.5, 0.1875, ((0, 32),))
    expand_bias = noise(splits[11], (INNER,), 0.3, 1.75, ((0, 32),))
    reduce_weight = noise(splits[12], (INNER, WIDTH), INNER ** -0.5, 0.09375, ((0, 32),))
    reduce_bias = noise(splits[13], (WIDTH,), 0.2, 1.25, ((0, 32),))
    triple_down = noise(splits[14], (ADAPTERS, WIDTH, RANK), WIDTH ** -0.5, 0.1875)
    triple_up = noise(splits[15], (ADAPTERS, RANK, 3 * WIDTH), (4 * RANK) ** -0.5, 0.75)
    mixer_down = noise(splits[16], (ADAPTERS, WIDTH, RANK), 1.0, 6.0)
    mixer_up = noise(splits[17], (ADAPTERS, RANK, WIDTH), (4 * RANK) ** -0.5, 0.75)
    expand_down = noise(splits[18], (ADAPTERS, WIDTH, RANK), WIDTH ** -0.5, 0.1875)
    expand_up = noise(splits[19], (ADAPTERS, RANK, INNER), (4 * RANK) ** -0.5, 0.75)
    reduce_down = noise(splits[20], (ADAPTERS, INNER, RANK), INNER ** -0.5, 0.09375)
    reduce_up = noise(splits[21], (ADAPTERS, RANK, WIDTH), (4 * RANK) ** -0.5, 0.75)
    cotangent = noise(splits[22], (SEQ, WIDTH), 1.0, 6.0, ((0, 32),))
    return {"hidden": hidden, "adapter_index": adapter_index, "first_gain": first_gain, "first_bias": first_bias, "triple_weight": triple_weight, "triple_bias": triple_bias, "mixer_weight": mixer_weight, "mixer_bias": mixer_bias, "second_gain": second_gain, "second_bias": second_bias, "expand_weight": expand_weight, "expand_bias": expand_bias, "reduce_weight": reduce_weight, "reduce_bias": reduce_bias, "triple_down": triple_down, "triple_up": triple_up, "mixer_down": mixer_down, "mixer_up": mixer_up, "expand_down": expand_down, "expand_up": expand_up, "reduce_down": reduce_down, "reduce_up": reduce_up, "cotangent": cotangent}


@jax.custom_vjp
def low(v):
    return lax.optimization_barrier(v.astype(jnp.bfloat16)).astype(jnp.float32)

@jax.custom_vjp
def low_back(v):
    return v

def low_keep(v):
    return (low(v), None)

def low_pass(kept, grad):
    return (grad,)

def back_keep(v):
    return (v, None)

def back_low(kept, grad):
    return (low(grad),)
low.defvjp(low_keep, low_pass)
low_back.defvjp(back_keep, back_low)
EPSILON = 1e-05
HIGHEST = lax.Precision.HIGHEST

def product(left, right):
    return jnp.dot(left, right, precision=HIGHEST, preferred_element_type=jnp.float32)

def layer_norm(stream, scales, offset):
    average = lax.optimization_barrier(jnp.mean(stream, axis=-1, keepdims=True))
    centred = stream - average
    variance = lax.optimization_barrier(jnp.mean(centred * centred, axis=-1, keepdims=True))
    return centred * lax.rsqrt(variance + EPSILON) * scales + offset

def selector(adapter_index):
    column = jnp.arange(ADAPTERS * RANK, dtype=jnp.int32) // RANK
    return (adapter_index[:, None] == column[None, :]).astype(jnp.float32)

def flat_down(factor):
    return jnp.transpose(factor, (1, 0, 2)).reshape(factor.shape[1], ADAPTERS * RANK)

def flat_up(factor):
    return factor.reshape(ADAPTERS * RANK, factor.shape[2])

def projected(source, weight, offset, down, upward, selection):
    low_rank = low(low_back(selection * product(source, flat_down(down))))
    return product(source, weight) + offset + product(low_rank, flat_up(upward))

def attention(joint):
    queries = joint[:, :WIDTH].reshape(SEQ, HEADS, HEAD_DIM)
    keys_all = joint[:, WIDTH:2 * WIDTH].reshape(SEQ, HEADS, HEAD_DIM)
    values_all = joint[:, 2 * WIDTH:].reshape(SEQ, HEADS, HEAD_DIM)
    positions = jnp.arange(SEQ, dtype=jnp.int32)
    block_rows = math.gcd(SEQ, 512)
    factor = 1.0 / math.sqrt(HEAD_DIM)

    def attend(packet):
        query_rows, query_places = packet
        scores = low_back(jnp.einsum('qhd,khd->qhk', query_rows, keys_all, precision=HIGHEST) * factor)
        allowed = (positions // BLOCK)[None, None, :] <= (query_places // BLOCK)[:, None, None]
        powers = jnp.where(allowed, jnp.exp(scores), 0.0)
        numerator = low_back(jnp.einsum('qhk,khd->qhd', low(powers), values_all, precision=HIGHEST))
        denominator = low_back(lax.optimization_barrier(jnp.sum(powers, axis=-1)))
        return numerator / denominator[:, :, None]
    blocks = SEQ // block_rows
    attended = lax.map(jax.checkpoint(attend), (queries.reshape(blocks, block_rows, HEADS, HEAD_DIM), positions.reshape(blocks, block_rows)))
    return attended.reshape(SEQ, WIDTH)

def reference(hidden, adapter_index, first_gain, first_bias, triple_weight, triple_bias, mixer_weight, mixer_bias, second_gain, second_bias, expand_weight, expand_bias, reduce_weight, reduce_bias, triple_down, triple_up, mixer_down, mixer_up, expand_down, expand_up, reduce_down, reduce_up, cotangent):

    def widen(array):
        return array.astype(jnp.float32)
    selection = selector(adapter_index)

    def forward(stream, triple_down, triple_up, mixer_down, mixer_up, expand_down, expand_up, reduce_down, reduce_up):
        first_normed = low(layer_norm(stream, widen(first_gain), widen(first_bias)))
        joint = low(low_back(projected(first_normed, widen(triple_weight), widen(triple_bias), triple_down, triple_up, selection)))
        attended = low(low_back(attention(joint)))
        residual = stream + low_back(projected(attended, widen(mixer_weight), widen(mixer_bias), mixer_down, mixer_up, selection))
        second_normed = low(layer_norm(residual, widen(second_gain), widen(second_bias)))
        expanded = low_back(projected(second_normed, widen(expand_weight), widen(expand_bias), expand_down, expand_up, selection))
        activated = low(low_back(jax.nn.gelu(expanded, approximate=True)))
        return residual + projected(activated, widen(reduce_weight), widen(reduce_bias), reduce_down, reduce_up, selection)
    result, pullback = jax.vjp(forward, widen(hidden), widen(triple_down), widen(triple_up), widen(mixer_down), widen(mixer_up), widen(expand_down), widen(expand_up), widen(reduce_down), widen(reduce_up))
    gradients = pullback(widen(cotangent))
    return (result.astype(jnp.bfloat16), gradients[0].astype(jnp.bfloat16), gradients[1], gradients[2], gradients[3], gradients[4], gradients[5], gradients[6], gradients[7], gradients[8])
```

```python
import functools
import math

import jax
import jax.numpy as jnp
from jax import lax
from jax.experimental import pallas as pl
from jax.experimental.pallas import tpu as pltpu
from jax.sharding import PartitionSpec as P

WIDTH = 1024
HEADS = 16
HEAD_DIM = 64
RANK = 16
ADAPTERS = 8
BLOCK = 256


EPSILON = 1e-05


def product(left, right):
    return jnp.dot(left, right, preferred_element_type=jnp.float32)


def by_transpose(left, right):
    return lax.dot_general(
        left, right, (((1,), (1,)), ((), ())), preferred_element_type=jnp.float32
    )


def transpose_by(left, right):
    return lax.dot_general(
        left, right, (((0,), (0,)), ((), ())), preferred_element_type=jnp.float32
    )


def layer_norm(stream, scales, offset):
    average = jnp.mean(stream, axis=-1, keepdims=True)
    centred = stream - average
    variance = jnp.mean(centred * centred, axis=-1, keepdims=True)
    return centred * lax.rsqrt(variance + EPSILON) * scales + offset


def selector(adapter_index):
    column = jnp.arange(ADAPTERS * RANK, dtype=jnp.int32) // RANK
    return (adapter_index[:, None] == column[None, :]).astype(jnp.float32)


def flat_down(factor):
    return jnp.transpose(factor, (1, 0, 2)).reshape(factor.shape[1], ADAPTERS * RANK)


def flat_up(factor):
    return factor.reshape(ADAPTERS * RANK, factor.shape[2])


def unflat_down(gradient):
    return jnp.transpose(gradient.reshape(gradient.shape[0], ADAPTERS, RANK), (1, 0, 2))


def unflat_up(gradient):
    return gradient.reshape(ADAPTERS, RANK, gradient.shape[1])


def projected(source, weight, offset, down_flat, up_flat, selection):
    low_rank = (selection * product(source, down_flat)).astype(jnp.bfloat16)
    return (
        product(source, weight) + offset.astype(jnp.float32) + product(low_rank, up_flat),
        low_rank,
    )


def adapter_grads(source, low_rank, out_grad, down_flat, up_flat, selection):
    rank_grad = (selection * by_transpose(out_grad, up_flat)).astype(jnp.bfloat16)
    down_grad = transpose_by(source, rank_grad)
    up_grad = transpose_by(low_rank, out_grad)
    return (down_grad, up_grad, by_transpose(rank_grad, down_flat))


def score_block(queries, keys_block):
    return jnp.einsum("qhd,khd->qhk", queries, keys_block, preferred_element_type=jnp.float32) * (
        1.0 / math.sqrt(HEAD_DIM)
    )


def cut_rows(arrays, trailing):
    length = arrays[0].shape[0]
    block_rows = math.gcd(length, 512)
    repeats = length // block_rows
    shaped = tuple(
        (
            array.reshape((repeats, block_rows) + shape_tail)
            for array, shape_tail in zip(arrays, trailing)
        )
    )
    firsts = jnp.arange(repeats, dtype=jnp.int32) * block_rows
    return (shaped, firsts, block_rows)


def forward_fold(queries, query_places, locate, totals, portion):
    head_count = queries.shape[1]
    query_block = query_places // BLOCK
    last_block = jnp.max(query_block)
    shaped, firsts, block_rows = cut_rows(portion, ((head_count, HEAD_DIM), (head_count, HEAD_DIM)))

    def forward_visiting(carried, packet):
        keys_block, values_block, first_row = packet
        key_places = locate(first_row, block_rows)

        def forward_compute(running):
            numerator, denominator = running
            allowed = (key_places // BLOCK)[None, None, :] <= query_block[:, None, None]
            powers = jnp.where(allowed, jnp.exp(score_block(queries, keys_block)), 0.0)
            numerator = numerator + jnp.einsum(
                "qhk,khd->qhd",
                powers.astype(jnp.bfloat16),
                values_block,
                preferred_element_type=jnp.float32,
            )
            return (numerator, denominator + jnp.sum(powers, axis=-1))

        skipped = jnp.min(key_places) // BLOCK > last_block
        return (lax.cond(skipped, lambda running: running, forward_compute, carried), None)

    return lax.scan(forward_visiting, totals, shaped + (firsts,))[0]


def query_grad_fold(queries, query_places, locate, numer_grad, denom_grad, totals, portion):
    head_count = queries.shape[1]
    query_block = query_places // BLOCK
    last_block = jnp.max(query_block)
    shaped, firsts, block_rows = cut_rows(portion, ((head_count, HEAD_DIM), (head_count, HEAD_DIM)))

    def query_visiting(carried, packet):
        keys_block, values_block, first_row = packet
        key_places = locate(first_row, block_rows)

        def query_compute(running):
            allowed = (key_places // BLOCK)[None, None, :] <= query_block[:, None, None]
            powers = jnp.where(allowed, jnp.exp(score_block(queries, keys_block)), 0.0)
            prob_grad = jnp.einsum(
                "qhd,khd->qhk", numer_grad, values_block, preferred_element_type=jnp.float32
            )
            score_grad = (powers * (prob_grad + denom_grad[:, :, None])).astype(jnp.bfloat16)
            return running + jnp.einsum(
                "qhk,khd->qhd", score_grad, keys_block, preferred_element_type=jnp.float32
            )

        skipped = jnp.min(key_places) // BLOCK > last_block
        return (lax.cond(skipped, lambda running: running, query_compute, carried), None)

    return lax.scan(query_visiting, totals, shaped + (firsts,))[0]


def key_grad_fold(keys_here, values_here, key_places, locate, totals, portion):
    head_count = keys_here.shape[1]
    key_block = key_places // BLOCK
    first_block = jnp.min(key_block)
    shaped, firsts, block_rows = cut_rows(
        portion, ((head_count, HEAD_DIM), (head_count, HEAD_DIM), (head_count,))
    )

    def key_visiting(carried, packet):
        query_rows, numer_rows, denom_rows, first_row = packet
        query_places = locate(first_row, block_rows)

        def key_compute(running):
            keys_grad, values_grad = running
            allowed = key_block[None, None, :] <= (query_places // BLOCK)[:, None, None]
            powers = jnp.where(allowed, jnp.exp(score_block(query_rows, keys_here)), 0.0)
            prob_grad = jnp.einsum(
                "qhd,khd->qhk", numer_rows, values_here, preferred_element_type=jnp.float32
            )
            score_grad = (powers * (prob_grad + denom_rows.astype(jnp.float32)[:, :, None])).astype(
                jnp.bfloat16
            )
            keys_grad = keys_grad + jnp.einsum(
                "qhk,qhd->khd", score_grad, query_rows, preferred_element_type=jnp.float32
            )
            values_grad = values_grad + jnp.einsum(
                "qhk,qhd->khd",
                powers.astype(jnp.bfloat16),
                numer_rows,
                preferred_element_type=jnp.float32,
            )
            return (keys_grad, values_grad)

        skipped = jnp.max(query_places) // BLOCK < first_block
        return (lax.cond(skipped, lambda running: running, key_compute, carried), None)

    return lax.scan(key_visiting, totals, shaped + (firsts,))[0]


def local(
    hidden,
    adapter_index,
    first_gain,
    first_bias,
    triple_weight,
    triple_bias,
    mixer_weight,
    mixer_bias,
    second_gain,
    second_bias,
    expand_weight,
    expand_bias,
    reduce_weight,
    reduce_bias,
    triple_down,
    triple_up,
    mixer_down,
    mixer_up,
    expand_down,
    expand_up,
    reduce_down,
    reduce_up,
    cotangent,
):
    gathered = (
        lax.all_gather(first_gain, ("head", "blk"), axis=0, tiled=True),
        lax.all_gather(first_bias, ("head", "blk"), axis=0, tiled=True),
        lax.all_gather(triple_weight, ("head", "blk"), axis=0, tiled=True),
        lax.all_gather(triple_bias, ("head", "blk"), axis=0, tiled=True),
        lax.all_gather(mixer_weight, ("head", "blk"), axis=0, tiled=True),
        lax.all_gather(mixer_bias, ("head", "blk"), axis=0, tiled=True),
        lax.all_gather(second_gain, ("head", "blk"), axis=0, tiled=True),
        lax.all_gather(second_bias, ("head", "blk"), axis=0, tiled=True),
        lax.all_gather(expand_weight, ("head", "blk"), axis=0, tiled=True),
        lax.all_gather(expand_bias, ("head", "blk"), axis=0, tiled=True),
        lax.all_gather(reduce_weight, ("head", "blk"), axis=0, tiled=True),
        lax.all_gather(reduce_bias, ("head", "blk"), axis=0, tiled=True),
    )
    (
        gain_one,
        bias_one,
        weight_triple,
        bias_triple,
        weight_mixer,
        bias_mixer,
        gain_two,
        bias_two,
        weight_expand,
        bias_expand,
        weight_reduce,
        bias_reduce,
    ) = gathered
    token_count = hidden.shape[0]
    head_ways = lax.axis_size("head")
    cycle_ways = lax.axis_size("blk")
    selection = selector(adapter_index)
    down_triple = flat_down(triple_down)
    upward_triple = flat_up(triple_up)
    down_mixer = flat_down(mixer_down)
    upward_mixer = flat_up(mixer_up)
    down_expand = flat_down(expand_down)
    upward_expand = flat_up(expand_up)
    down_reduce = flat_down(reduce_down)
    upward_reduce = flat_up(reduce_up)
    stream = hidden.astype(jnp.float32)

    def first_norm(values_in):
        return layer_norm(values_in, gain_one.astype(jnp.float32), bias_one.astype(jnp.float32))

    def second_norm(values_in):
        return layer_norm(values_in, gain_two.astype(jnp.float32), bias_two.astype(jnp.float32))

    first_normed = first_norm(stream).astype(jnp.bfloat16)
    joint, rank_triple = projected(
        first_normed, weight_triple, bias_triple, down_triple, upward_triple, selection
    )
    joint = joint.astype(jnp.bfloat16)
    parts = joint.reshape(token_count, 3, HEADS, HEAD_DIM)
    own_shard = lax.axis_index("blk") * head_ways + lax.axis_index("head")
    query_places = own_shard * token_count + jnp.arange(token_count, dtype=jnp.int32)

    def locate(first_row, length):
        rows_here = first_row + jnp.arange(length, dtype=jnp.int32)
        shard_index = rows_here // token_count
        return (
            shard_index % cycle_ways * head_ways + shard_index // cycle_ways
        ) * token_count + rows_here % token_count

    queries = parts[:, 0]
    keys_here = parts[:, 1]
    values_here = parts[:, 2]
    head_count = queries.shape[1]
    flat_keys = keys_here.reshape(token_count, head_count * HEAD_DIM)
    flat_values = values_here.reshape(token_count, head_count * HEAD_DIM)
    zeros_rows = jnp.zeros((token_count, head_count, HEAD_DIM), jnp.float32)
    payload = (flat_keys, flat_values)
    numerator, denominator = forward_fold(
        queries,
        query_places,
        locate,
        (zeros_rows, jnp.zeros((token_count, head_count), jnp.float32)),
        (
            lax.all_gather(payload[0], ("head", "blk"), axis=0, tiled=True),
            lax.all_gather(payload[1], ("head", "blk"), axis=0, tiled=True),
        ),
    )
    attended = numerator / denominator[:, :, None]
    attended_low = attended.astype(jnp.bfloat16).reshape(token_count, WIDTH)
    mixed, rank_mixer = projected(
        attended_low, weight_mixer, bias_mixer, down_mixer, upward_mixer, selection
    )
    residual = stream + mixed
    second_normed = second_norm(residual).astype(jnp.bfloat16)
    expanded, rank_expand = projected(
        second_normed, weight_expand, bias_expand, down_expand, upward_expand, selection
    )
    activated = jax.nn.gelu(expanded, approximate=True).astype(jnp.bfloat16)
    reduced, rank_reduce = projected(
        activated, weight_reduce, bias_reduce, down_reduce, upward_reduce, selection
    )
    layer_out = (residual + reduced).astype(jnp.bfloat16)
    reduce_down_grad, reduce_up_grad, through_reduce = adapter_grads(
        activated, rank_reduce, cotangent, down_reduce, upward_reduce, selection
    )
    activated_grad = (by_transpose(cotangent, weight_reduce) + through_reduce).astype(jnp.bfloat16)
    gelu_back = jax.vjp(lambda values_in: jax.nn.gelu(values_in, approximate=True), expanded)[1]
    expanded_grad = gelu_back(activated_grad.astype(jnp.float32))[0].astype(jnp.bfloat16)
    expand_down_grad, expand_up_grad, through_expand = adapter_grads(
        second_normed, rank_expand, expanded_grad, down_expand, upward_expand, selection
    )
    normed_grad = by_transpose(expanded_grad, weight_expand) + through_expand
    second_back = jax.vjp(second_norm, residual)[1]
    residual_grad = cotangent.astype(jnp.float32) + second_back(normed_grad)[0]
    mixed_grad = residual_grad.astype(jnp.bfloat16)
    mixer_down_grad, mixer_up_grad, through_mixer = adapter_grads(
        attended_low, rank_mixer, mixed_grad, down_mixer, upward_mixer, selection
    )
    attended_grad = (by_transpose(mixed_grad, weight_mixer) + through_mixer).astype(jnp.bfloat16)
    output_grad = attended_grad.reshape(token_count, HEADS, HEAD_DIM).astype(jnp.float32)
    numer_grad = (output_grad / denominator[:, :, None]).astype(jnp.bfloat16)
    denom_grad = (-jnp.sum(output_grad * attended, axis=-1) / denominator).astype(jnp.bfloat16)
    payload = (flat_keys, flat_values)
    query_grad = query_grad_fold(
        queries,
        query_places,
        locate,
        numer_grad,
        denom_grad.astype(jnp.float32),
        zeros_rows,
        (
            lax.all_gather(payload[0], ("head", "blk"), axis=0, tiled=True),
            lax.all_gather(payload[1], ("head", "blk"), axis=0, tiled=True),
        ),
    )
    payload = (
        queries.reshape(token_count, head_count * HEAD_DIM),
        numer_grad.reshape(token_count, head_count * HEAD_DIM),
        denom_grad,
    )
    keys_grad, values_grad = key_grad_fold(
        keys_here,
        values_here,
        query_places,
        locate,
        (zeros_rows, zeros_rows),
        (
            lax.all_gather(payload[0], ("head", "blk"), axis=0, tiled=True),
            lax.all_gather(payload[1], ("head", "blk"), axis=0, tiled=True),
            lax.all_gather(payload[2], ("head", "blk"), axis=0, tiled=True),
        ),
    )
    factor = 1.0 / math.sqrt(HEAD_DIM)
    joint_grad = jnp.stack([query_grad * factor, keys_grad * factor, values_grad], axis=1).astype(
        jnp.bfloat16
    )
    joint_tokens = joint_grad.reshape(token_count, 3 * WIDTH)
    triple_down_grad, triple_up_grad, through_triple = adapter_grads(
        first_normed, rank_triple, joint_tokens, down_triple, upward_triple, selection
    )
    normed_one_grad = by_transpose(joint_tokens, weight_triple) + through_triple
    first_back = jax.vjp(first_norm, stream)[1]
    hidden_grad = (residual_grad + first_back(normed_one_grad)[0]).astype(jnp.bfloat16)
    summed = lax.psum(
        (
            triple_down_grad,
            triple_up_grad,
            mixer_down_grad,
            mixer_up_grad,
            expand_down_grad,
            expand_up_grad,
            reduce_down_grad,
            reduce_up_grad,
        ),
        ("head", "blk"),
    )
    return (
        layer_out,
        hidden_grad,
        unflat_down(summed[0]),
        unflat_up(summed[1]),
        unflat_down(summed[2]),
        unflat_up(summed[3]),
        unflat_down(summed[4]),
        unflat_up(summed[5]),
        unflat_down(summed[6]),
        unflat_up(summed[7]),
    )


MESH = pl.DeviceIdType.MESH
CHIPS = 16
ROWS = 128
LIMIT = 60 * 1024 * 1024


class Links:
    def __init__(self):
        self.h = lax.axis_index("head")
        self.b = lax.axis_index("blk")
        self.o = 1 - self.h
        self.sent = []
        x = lax.rem(self.b, 2)
        y = lax.rem(self.b // 2, 2)
        self.xb = self.b + 1 - 2 * x
        self.yb = self.b + 2 - 4 * y
        self.db = self.xb + 2 - 4 * y

    def ahead(self, k):
        return lax.rem(self.b + k, CHIPS)

    def behind(self, k):
        return lax.rem(self.b + CHIPS - k, CHIPS)

    def greet(self):
        barrier = pltpu.get_barrier_semaphore()
        for k in range(1, CHIPS):
            pl.semaphore_signal(
                barrier, 1, device_id=(self.h, self.ahead(k)), device_id_type=MESH
            )
        pl.semaphore_signal(barrier, 1, device_id=(self.o, self.b), device_id_type=MESH)
        pl.semaphore_wait(barrier, CHIPS)

    def send(self, source, target, send_sem, recv_sem, device):
        copy = pltpu.make_async_remote_copy(
            src_ref=source,
            dst_ref=target,
            send_sem=send_sem,
            recv_sem=recv_sem,
            device_id=device,
            device_id_type=MESH,
        )
        copy.start()
        self.sent.append(copy)
        return copy

    def arrived(self, target, send_sem, recv_sem):
        pltpu.make_async_remote_copy(
            src_ref=target,
            dst_ref=target,
            send_sem=send_sem,
            recv_sem=recv_sem,
            device_id=(self.o, self.b),
            device_id_type=MESH,
        ).wait_recv()

    def settle(self):
        for copy in self.sent:
            copy.wait_send()
        self.sent = []


def half_mask(rows):
    return lax.broadcasted_iota(jnp.int32, (rows, 128), 1) < 64


def swap(tile):
    return pltpu.roll(tile, 64, 1)


def rows_at(ref, start, count):
    return ref.at[pl.ds(pl.multiple_of(start, 16), count), :]


class Gather:
    def __init__(self, links, number, slot, sems):
        self.links, self.p, self.slot = links, number, slot
        self.sems = sems

    def start(self):
        l = self.links
        self.own(0, l.b)
        return self

    def line(self, k):
        (zs, zr) = self.sems["z"]
        l = self.links
        piece = self.slot(l.h, l.b)
        l.send(piece, piece, zs.at[self.p, k], zr.at[self.p, k], (l.h, l.ahead(4 * k)))

    def own(self, j, chip):
        l = self.links
        piece = self.slot(l.h, chip)
        (xs, xr), (ys, yr) = (self.sems["x"], self.sems["y"])
        l.send(piece, piece, xs.at[self.p, j], xr.at[self.p, j], (l.h, l.xb))
        l.send(piece, piece, ys.at[self.p, j], yr.at[self.p, j], (l.h, l.yb))
        if j == 0:
            for k in range(1, 4):
                self.line(k)
        self.other(j, chip)

    def other(self, number, chip):
        l = self.links
        piece = self.slot(l.h, chip)
        (cs, cr) = self.sems["c"]
        l.send(piece, piece, cs.at[self.p, number], cr.at[self.p, number], (l.o, l.b))

    def from_line(self, j):
        l = self.links
        chip = l.behind(4 * j)
        (s, r) = self.sems["z"]
        l.arrived(self.slot(l.h, chip), s.at[self.p, j], r.at[self.p, j])
        self.own(j, chip)

    def shifted(self, base, j):
        return lax.rem(base + CHIPS - 4 * j, CHIPS)

    def from_side(self, axis, j):
        l = self.links
        chip = self.shifted(l.xb if axis == "x" else l.yb, j)
        (s, r) = self.sems[axis]
        piece = self.slot(l.h, chip)
        l.arrived(piece, s.at[self.p, j], r.at[self.p, j])
        if (j % 2 == 0) == (axis == "x"):
            (ds, dr) = self.sems["d"]
            target = l.yb if axis == "x" else l.xb
            l.send(piece, piece, ds.at[self.p, j], dr.at[self.p, j], (l.h, target))
        self.other((4 if axis == "x" else 8) + j, chip)

    def from_corner(self, j):
        l = self.links
        chip = self.shifted(l.db, j)
        (s, r) = self.sems["d"]
        l.arrived(self.slot(l.h, chip), s.at[self.p, j], r.at[self.p, j])
        self.other(12 + j, chip)

    def events(self):
        found = [self.start]
        for j in range(4):
            if j:
                found.append(functools.partial(self.from_line, j))
            found.append(functools.partial(self.from_side, "x", j))
            found.append(functools.partial(self.from_side, "y", j))
        for j in range(4):
            found.append(functools.partial(self.from_corner, j))
        return found

    def whole(self):
        l = self.links
        (s, r) = self.sems["c"]
        bases = (l.b, l.xb, l.yb, l.db)
        for number in range(16):
            chip = self.shifted(bases[number // 4], number % 4)
            l.arrived(self.slot(l.o, chip), s.at[self.p, number], r.at[self.p, number])


def shard_of(h, chip):
    return h * CHIPS + chip


def normalise(stream, gain, bias):
    average = jnp.mean(stream, axis=-1, keepdims=True)
    centred = stream - average
    variance = jnp.mean(centred * centred, axis=-1, keepdims=True)
    return centred * lax.rsqrt(variance + EPSILON) * gain + bias


PIECES = 13


def front_kernel(
    hidden, sel, small_sh, triple_sh, mixer_sh, reduce_sh, expand_sh, down_t, up_t,
    wt, wm, wr, we, vecs, bias_e, first_normed, rank_triple, kv, q, attden, attended,
    small, bias_t, send_kv, send_q, recv_q, ones_v, send_a, recv_a,
    lsem, zs, zr, xs, xr, ys, yr, ds, dr, cs, cr, ks, kr, qs, qr, fs, fr, as_, ar,
):
    l = Links()
    mine = shard_of(l.h, l.b)
    local_copies = [
        pltpu.make_async_copy(small_sh, rows_at(small, mine * 16, 16), lsem.at[0]),
        pltpu.make_async_copy(triple_sh, rows_at(wt, mine * 32, 32), lsem.at[1]),
        pltpu.make_async_copy(mixer_sh, rows_at(wm, mine * 32, 32), lsem.at[2]),
        pltpu.make_async_copy(reduce_sh, rows_at(wr, mine * 128, 128), lsem.at[3]),
        pltpu.make_async_copy(expand_sh, rows_at(we, mine * 32, 32), lsem.at[4]),
    ]
    for copy in local_copies:
        copy.start()
    l.greet()
    for copy in local_copies:
        copy.wait()
    sems = {"z": (zs, zr), "x": (xs, xr), "y": (ys, yr), "d": (ds, dr), "c": (cs, cr)}

    def columns(ref, at):
        return lambda h, chip: ref.at[
            pl.ds(pl.multiple_of(shard_of(h, chip) * 32, 32), 32), at : at + 1024
        ]

    def inner(ref, at):
        return lambda h, chip: ref.at[
            pl.ds(pl.multiple_of(shard_of(h, chip) * 128 + at, 32), 32), :
        ]

    slots = [lambda h, chip: rows_at(small, shard_of(h, chip) * 16, 16)]
    slots += [columns(wt, m * 1024) for m in range(3)]
    slots += [columns(wm, 0)]
    slots += [inner(wr, m * 32) for m in range(4)]
    slots += [columns(we, m * 1024) for m in range(4)]
    pieces = [Gather(l, n, slot, sems) for n, slot in enumerate(slots)]
    for piece in pieces[:4]:
        for event in piece.events():
            event()
    waiting = []
    for piece in pieces[4:]:
        waiting += piece.events()

    def pump(count):
        for _ in range(min(count, len(waiting))):
            waiting.pop(0)()

    waiting.pop(0)()
    pieces[0].whole()
    for g in range(8):
        tile = jnp.zeros((16, 128), jnp.float32)
        for n in range(4):
            at = (4 * g + n) * 16
            tile = tile + small[at : at + 16, :].astype(jnp.float32)
        vecs[:, g * 128 : (g + 1) * 128] = tile
        for n in range(3):
            at = (g * 3 + n) * 128
            bias_t[0:1, at : at + 128] = tile[6 + n : 7 + n, :]
        for n in range(4):
            at = (g * 4 + n) * 128
            bias_e[0:1, at : at + 128] = tile[9 + n : 10 + n, :]
    normed = normalise(hidden[...].astype(jnp.float32), vecs[0:1, :], vecs[1:2, :])
    first_normed[...] = normed.astype(jnp.bfloat16)
    rank_triple[...] = (sel[...] * by_transpose(first_normed[...], down_t[...])).astype(
        jnp.bfloat16
    )
    for piece in pieces[1:4]:
        piece.whole()
    low = half_mask(128)
    low64 = half_mask(64)
    for step in range(4):

        def joint(part):
            at = part * 1024 + step * 256
            tile = (
                product(first_normed[...], wt[:, at : at + 256])
                + bias_t[0:1, at : at + 256]
                + product(rank_triple[...], up_t[:, at : at + 256])
            )
            return tile[:, :128], tile[:, 128:]

        for n, (qt, kt, vt) in enumerate(zip(joint(0), joint(1), joint(2))):
            c = step * 4 + n * 2
            bf = jnp.bfloat16
            send_kv[c * 128 : c * 128 + 128, :] = jnp.where(low, kt, swap(vt)).astype(bf)
            send_kv[c * 128 + 128 : c * 128 + 256, :] = jnp.where(low, swap(kt), vt).astype(bf)
            qt = qt.astype(bf).astype(jnp.float32) * 0.125
            turned = swap(qt)
            send_q[c * 64 : c * 64 + 64, :] = jnp.where(low64, qt[:64], turned[64:]).astype(bf)
            send_q[c * 64 + 64 : c * 64 + 128, :] = jnp.where(
                low64, turned[:64], qt[64:]
            ).astype(bf)
    own = l.b * 256 + l.h * 128

    def kv_at(chip, h):
        return rows_at(kv, chip * 256 + h * 128, 128)

    for k in range(1, CHIPS):
        t = l.ahead(k)
        l.send(rows_at(send_kv, t * 128, 128), kv_at(l.b, l.h), ks.at[k], kr.at[k], (l.h, t))
    for k in range(1, CHIPS):
        t = l.ahead(k)
        l.send(rows_at(send_q, t * 64, 64), rows_at(recv_q, l.b * 64, 64), qs.at[k], qr.at[k], (l.h, t))
    kv[pl.ds(pl.multiple_of(own, 128), 128), :] = send_kv[pl.ds(pl.multiple_of(l.b * 128, 128), 128), :]
    recv_q[pl.ds(pl.multiple_of(l.b * 64, 64), 64), :] = send_q[pl.ds(pl.multiple_of(l.b * 64, 64), 64), :]
    l.send(kv_at(l.b, l.h), kv_at(l.b, l.h), fs.at[0], fr.at[0], (l.o, l.b))
    for k in range(1, CHIPS):
        c = l.behind(k)
        l.arrived(kv_at(c, l.h), ks.at[k], kr.at[k])
        l.send(kv_at(c, l.h), kv_at(c, l.h), fs.at[k], fr.at[k], (l.o, l.b))
        pump(2)
    for k in range(1, CHIPS):
        l.arrived(rows_at(recv_q, l.behind(k) * 64, 64), qs.at[k], qr.at[k])
        pump(1)
    for k in range(CHIPS):
        l.arrived(kv_at(l.behind(k), l.o), fs.at[k], fr.at[k])
    for n in range(CHIPS):
        tile = recv_q[n * 64 : n * 64 + 64, :].astype(jnp.float32)
        q[n * 128 : n * 128 + 64, :] = jnp.where(low64, tile, 0.0).astype(jnp.bfloat16)
        q[n * 128 + 64 : n * 128 + 128, :] = jnp.where(low64, swap(tile), 0.0).astype(jnp.bfloat16)
        tile = kv[n * 256 : n * 256 + 256, :].astype(jnp.float32)
        ones_v[n * 256 : n * 256 + 256, :] = jnp.where(half_mask(256), 1.0, tile).astype(jnp.bfloat16)
    for i in range(8):
        queries = q[i * 256 : (i + 1) * 256, :]

        def fold(jj, total, masked=False):
            at = pl.ds(pl.multiple_of(jj * 512, 512), 512)
            powers = jnp.exp(by_transpose(queries, kv[at, :]))
            if masked:
                row = lax.broadcasted_iota(jnp.int32, (256, 512), 0)
                column = lax.broadcasted_iota(jnp.int32, (256, 512), 1)
                powers = jnp.where((row >= 128) | (column < 256), powers, 0.0)
            return total + product(powers.astype(jnp.bfloat16), ones_v[at, :])

        total = fold(i, jnp.zeros((256, 128), jnp.float32), True)
        if i:
            total = lax.fori_loop(0, i, fold, total)
        share = total / swap(total)
        attden[i * 256 : (i + 1) * 256, :] = jnp.where(half_mask(256), total, share)
        for n in range(2):
            t = 2 * i + n
            part = share[n * 128 : n * 128 + 128]
            packed = jnp.where(low64, swap(part[64:]), part[:64]).astype(jnp.bfloat16)
            send_a[t * 64 : t * 64 + 64, :] = packed
        pump(10)
    for k in range(1, CHIPS):
        t = l.ahead(k)
        l.send(rows_at(send_a, t * 64, 64), rows_at(recv_a, l.b * 64, 64), as_.at[k], ar.at[k], (l.h, t))
    recv_a[pl.ds(pl.multiple_of(l.b * 64, 64), 64), :] = send_a[pl.ds(pl.multiple_of(l.b * 64, 64), 64), :]
    pump(1000)
    for k in range(1, CHIPS):
        l.arrived(rows_at(recv_a, l.behind(k) * 64, 64), as_.at[k], ar.at[k])
    for p in range(8):
        one = recv_a[p * 128 : p * 128 + 64, :].astype(jnp.float32)
        two = recv_a[p * 128 + 64 : p * 128 + 128, :].astype(jnp.float32)
        at = p * 128
        attended[0:64, at : at + 128] = jnp.where(low64, swap(one), two).astype(jnp.bfloat16)
        attended[64:128, at : at + 128] = jnp.where(low64, one, swap(two)).astype(jnp.bfloat16)
    for piece in pieces[4:]:
        piece.whole()
    l.settle()


def front(hidden, sel, small_sh, triple_sh, mixer_sh, reduce_sh, expand_sh, down_t, up_t):
    bf, f4 = jnp.bfloat16, jnp.float32
    vmem = pl.BlockSpec(memory_space=pltpu.VMEM)
    hbm = pl.BlockSpec(memory_space=pl.ANY)
    shape = jax.ShapeDtypeStruct
    dma = pltpu.SemaphoreType.DMA
    return pl.pallas_call(
        front_kernel,
        name="front",
        in_specs=[vmem, vmem, hbm, hbm, hbm, hbm, hbm, vmem, vmem],
        out_shape=[
            shape((1024, 3072), bf),
            shape((1024, 1024), bf),
            shape((4096, 1024), bf),
            shape((1024, 4096), bf),
            shape((16, 1024), f4),
            shape((1, 4096), f4),
            shape((128, 1024), bf),
            shape((128, 128), bf),
            shape((4096, 128), bf),
            shape((2048, 128), bf),
            shape((2048, 128), f4),
            shape((128, 1024), bf),
        ],
        out_specs=[vmem] * 12,
        scratch_shapes=[
            pltpu.VMEM((512, 128), bf),
            pltpu.VMEM((1, 3072), f4),
            pltpu.VMEM((2048, 128), bf),
            pltpu.VMEM((1024, 128), bf),
            pltpu.VMEM((1024, 128), bf),
            pltpu.VMEM((4096, 128), bf),
            pltpu.VMEM((1024, 128), bf),
            pltpu.VMEM((1024, 128), bf),
            dma((5,)),
            dma((PIECES, 4)), dma((PIECES, 4)),
            dma((PIECES, 4)), dma((PIECES, 4)),
            dma((PIECES, 4)), dma((PIECES, 4)),
            dma((PIECES, 4)), dma((PIECES, 4)),
            dma((PIECES, 16)), dma((PIECES, 16)),
            dma((16,)), dma((16,)),
            dma((16,)), dma((16,)),
            dma((16,)), dma((16,)),
            dma((16,)), dma((16,)),
        ],
        compiler_params=pltpu.CompilerParams(
            collective_id=0, has_side_effects=True, vmem_limit_bytes=LIMIT
        ),
    )(hidden, sel, small_sh, triple_sh, mixer_sh, reduce_sh, expand_sh, down_t, up_t)


def back_kernel(
    kv, q, attden, agrad,
    joint_grad,
    send_g, recv_g, qd, qz, dz, kz, vz, k_t, ddrow, dq_t, part, recv_part, send_kv, send_q, recv_kv, recv_q,
    gs, gr, es, er, ks, kr, qs, qr,
):
    bf, f4 = jnp.bfloat16, jnp.float32
    l = Links()
    low, low64 = half_mask(128), half_mask(64)
    l.greet()
    for p in range(8):
        tile = agrad[:, p * 128 : (p + 1) * 128].astype(f4)
        turned = swap(tile)
        send_g[p * 128 : p * 128 + 64, :] = jnp.where(low64, tile[64:], turned[:64]).astype(bf)
        send_g[p * 128 + 64 : p * 128 + 128, :] = jnp.where(low64, turned[64:], tile[:64]).astype(bf)
    for k in range(1, CHIPS):
        t = l.ahead(k)
        l.send(rows_at(send_g, t * 64, 64), rows_at(recv_g, l.b * 64, 64), gs.at[k], gr.at[k], (l.h, t))
    recv_g[pl.ds(pl.multiple_of(l.b * 64, 64), 64), :] = send_g[pl.ds(pl.multiple_of(l.b * 64, 64), 64), :]
    for n in range(CHIPS):
        tile = kv[n * 256 : n * 256 + 256, :].astype(f4)
        wide = half_mask(256)
        kz[n * 256 : n * 256 + 256, :] = jnp.where(wide, tile, 0.0).astype(bf)
        vz[n * 256 : n * 256 + 256, :] = jnp.where(wide, 0.0, tile).astype(bf)
        k_t[:, n * 256 : n * 256 + 256] = tile.T[:64, :].astype(bf)
    dq_t[...] = jnp.zeros_like(dq_t)
    for k in range(1, CHIPS):
        l.arrived(rows_at(recv_g, l.behind(k) * 64, 64), gs.at[k], gr.at[k])
    for n in range(CHIPS):
        at = n * 128
        g = recv_g[n * 64 : n * 64 + 64, :].astype(f4)
        both = attden[at : at + 128, :]
        grad = jnp.concatenate([g, swap(g)], axis=0)
        numer = jnp.where(low, 0.0, grad / swap(both))
        numer_low = numer.astype(bf)
        dz[at : at + 128, :] = numer_low
        held = q[at : at + 128, :]
        qz[at : at + 128, :] = held
        qd[at : at + 128, :] = jnp.where(low, held.astype(f4), numer_low.astype(f4)).astype(bf)
        term = jnp.where(low, 0.0, numer * both)
        row = -jnp.sum(term.T, axis=0, keepdims=True)
        ddrow[0:1, at : at + 128] = row.astype(bf).astype(f4)

    def exchange(jj):
        for n in range(2):
            t = 2 * jj + n
            l.send(
                rows_at(part, t * 256 + l.o * 128, 128), rows_at(recv_part, t * 128, 128),
                es.at[t], er.at[t], (l.o, l.b),
            )

    def finish(jj):
        for n in range(2):
            t = 2 * jj + n
            l.arrived(rows_at(recv_part, t * 128, 128), es.at[t], er.at[t])
            here = part[pl.ds(pl.multiple_of(t * 256 + l.h * 128, 128), 128), :]
            send_kv[t * 128 : t * 128 + 128, :] = (here + recv_part[t * 128 : t * 128 + 128, :]).astype(bf)
            y = dq_t[:, t * 128 : t * 128 + 128].T * 0.125
            send_q[t * 64 : t * 64 + 64, :] = jnp.where(low64, y[:64], swap(y[64:])).astype(bf)

    for jj in range(8):
        keys = slice(jj * 512, jj * 512 + 512)

        def fold(i, total, masked=False):
            at = pl.ds(pl.multiple_of(i * 256, 256), 256)
            both = qd[at, :]
            powers = jnp.exp(by_transpose(kz[keys, :], both))
            if masked:
                row = lax.broadcasted_iota(jnp.int32, (512, 256), 0)
                column = lax.broadcasted_iota(jnp.int32, (512, 256), 1)
                powers = jnp.where((row < 256) | (column >= 128), powers, 0.0)
            prob = by_transpose(vz[keys, :], both) + ddrow[0:1, at]
            score = (powers * prob).astype(bf)
            dq_t[0:64, at] += product(k_t[:, keys], score)
            return total + product(score, qz[at, :]) + product(powers.astype(bf), dz[at, :])

        total = fold(jj, jnp.zeros((512, 128), f4), True)
        if jj < 7:
            total = lax.fori_loop(jj + 1, 8, fold, total)
        part[keys, :] = total
        exchange(jj)
        if jj:
            finish(jj - 1)
    finish(7)
    for k in range(1, CHIPS):
        t = l.ahead(k)
        l.send(rows_at(send_kv, t * 128, 128), rows_at(recv_kv, l.b * 128, 128), ks.at[k], kr.at[k], (l.h, t))
        l.send(rows_at(send_q, t * 64, 64), rows_at(recv_q, l.b * 64, 64), qs.at[k], qr.at[k], (l.h, t))
    recv_kv[pl.ds(pl.multiple_of(l.b * 128, 128), 128), :] = send_kv[pl.ds(pl.multiple_of(l.b * 128, 128), 128), :]
    recv_q[pl.ds(pl.multiple_of(l.b * 64, 64), 64), :] = send_q[pl.ds(pl.multiple_of(l.b * 64, 64), 64), :]
    for k in range(1, CHIPS):
        l.arrived(rows_at(recv_kv, l.behind(k) * 128, 128), ks.at[k], kr.at[k])
        l.arrived(rows_at(recv_q, l.behind(k) * 64, 64), qs.at[k], qr.at[k])
    for p in range(8):
        at = p * 128
        one = recv_q[p * 128 : p * 128 + 64, :].astype(f4)
        two = recv_q[p * 128 + 64 : p * 128 + 128, :].astype(f4)
        joint_grad[0:64, at : at + 128] = jnp.where(low64, one, swap(two)).astype(bf)
        joint_grad[64:128, at : at + 128] = jnp.where(low64, swap(one), two).astype(bf)
        one = recv_kv[p * 256 : p * 256 + 128, :].astype(f4)
        two = recv_kv[p * 256 + 128 : p * 256 + 256, :].astype(f4)
        joint_grad[:, 1024 + at : 1152 + at] = jnp.where(low, one, swap(two)).astype(bf)
        joint_grad[:, 2048 + at : 2176 + at] = jnp.where(low, swap(one), two).astype(bf)
    l.settle()


def back(kv, q, attden, agrad):
    bf, f4 = jnp.bfloat16, jnp.float32
    vmem = pl.BlockSpec(memory_space=pltpu.VMEM)
    dma = pltpu.SemaphoreType.DMA
    return pl.pallas_call(
        back_kernel,
        name="back",
        in_specs=[vmem] * 4,
        out_shape=jax.ShapeDtypeStruct((128, 3072), bf),
        out_specs=vmem,
        scratch_shapes=[
            pltpu.VMEM((1024, 128), bf), pltpu.VMEM((1024, 128), bf),
            pltpu.VMEM((2048, 128), bf), pltpu.VMEM((2048, 128), bf), pltpu.VMEM((2048, 128), bf),
            pltpu.VMEM((4096, 128), bf), pltpu.VMEM((4096, 128), bf), pltpu.VMEM((64, 4096), bf),
            pltpu.VMEM((1, 2048), f4), pltpu.VMEM((128, 2048), f4),
            pltpu.VMEM((4096, 128), f4), pltpu.VMEM((2048, 128), f4),
            pltpu.VMEM((2048, 128), bf), pltpu.VMEM((1024, 128), bf),
            pltpu.VMEM((2048, 128), bf), pltpu.VMEM((1024, 128), bf),
            dma((16,)), dma((16,)), dma((16,)), dma((16,)),
            dma((16,)), dma((16,)), dma((16,)), dma((16,)),
        ],
        compiler_params=pltpu.CompilerParams(
            collective_id=1, has_side_effects=True, vmem_limit_bytes=LIMIT
        ),
    )(kv, q, attden, agrad)


def small_block(blocks, triple_bias, expand_bias):
    place = lax.rem(shard_of(lax.axis_index("head"), lax.axis_index("blk")), 4)
    lane = jnp.arange(128, dtype=jnp.int32)[None, :]
    six = jnp.where(lane // 32 == place, jnp.tile(jnp.stack(blocks), (1, 4)), 0)
    wide = jnp.arange(384, dtype=jnp.int32)
    three = jnp.where(wide // 96 == place, jnp.tile(triple_bias, 4), 0).reshape(3, 128)
    row = jnp.arange(4, dtype=jnp.int32)[:, None]
    four = jnp.where(row == place, expand_bias[None, :], 0)
    return jnp.concatenate([six, three, four, jnp.zeros((3, 128), jnp.bfloat16)], axis=0).astype(jnp.bfloat16)


def local_fast(
    hidden, adapter_index, first_gain, first_bias, triple_weight, triple_bias, mixer_weight, mixer_bias,
    second_gain, second_bias, expand_weight, expand_bias, reduce_weight, reduce_bias, triple_down, triple_up,
    mixer_down, mixer_up, expand_down, expand_up, reduce_down, reduce_up, cotangent,
):
    selection = selector(adapter_index)

    def turned(factor):
        return jnp.transpose(factor, (0, 2, 1)).reshape(ADAPTERS * RANK, factor.shape[1])

    small_sh = small_block(
        [first_gain, first_bias, mixer_bias, second_gain, second_bias, reduce_bias], triple_bias, expand_bias
    )
    down_t, up_t = turned(triple_down), flat_up(triple_up)
    (wt, wm, wr, we, vecs, bias_e, first_normed, rank_triple, kv, q, attden, attended_low) = front(
        hidden, selection, small_sh, triple_weight, mixer_weight, reduce_weight, expand_weight, down_t, up_t
    )
    stream = hidden.astype(jnp.float32)
    gain_one, bias_one, bias_m, gain_two, bias_two, bias_r = [vecs[n] for n in range(6)]
    down_m, up_m = turned(mixer_down), flat_up(mixer_up)
    down_e, up_e = turned(expand_down), flat_up(expand_up)
    down_r, up_r = turned(reduce_down), flat_up(reduce_up)

    def first_norm(values_in):
        return layer_norm(values_in, gain_one, bias_one)

    def second_norm(values_in):
        return layer_norm(values_in, gain_two, bias_two)

    def forward(source, weight, offset, down, up):
        low_rank = (selection * by_transpose(source, down)).astype(jnp.bfloat16)
        return product(source, weight) + offset + product(low_rank, up), low_rank

    def backward(source, low_rank, out_grad, down, up):
        rank_grad = (selection * by_transpose(out_grad, up)).astype(jnp.bfloat16)
        return transpose_by(rank_grad, source), transpose_by(low_rank, out_grad), product(rank_grad, down)

    mixed, rank_mixer = forward(attended_low, wm, bias_m, down_m, up_m)
    residual = stream + mixed
    second_normed = second_norm(residual).astype(jnp.bfloat16)
    expanded, rank_expand = forward(second_normed, we, bias_e[0], down_e, up_e)
    activated = jax.nn.gelu(expanded, approximate=True).astype(jnp.bfloat16)
    reduced, rank_reduce = forward(activated, wr, bias_r, down_r, up_r)
    layer_out = (residual + reduced).astype(jnp.bfloat16)
    reduce_down_grad, reduce_up_grad, through = backward(activated, rank_reduce, cotangent, down_r, up_r)
    activated_grad = (by_transpose(cotangent, wr) + through).astype(jnp.bfloat16)
    gelu_back = jax.vjp(lambda values_in: jax.nn.gelu(values_in, approximate=True), expanded)[1]
    expanded_grad = gelu_back(activated_grad.astype(jnp.float32))[0].astype(jnp.bfloat16)
    expand_down_grad, expand_up_grad, through = backward(second_normed, rank_expand, expanded_grad, down_e, up_e)
    normed_grad = by_transpose(expanded_grad, we) + through
    residual_grad = cotangent.astype(jnp.float32) + jax.vjp(second_norm, residual)[1](normed_grad)[0]
    mixed_grad = residual_grad.astype(jnp.bfloat16)
    mixer_down_grad, mixer_up_grad, through = backward(attended_low, rank_mixer, mixed_grad, down_m, up_m)
    attended_grad = (by_transpose(mixed_grad, wm) + through).astype(jnp.bfloat16)
    joint_tokens = back(kv, q, attden, attended_grad)
    triple_down_grad, triple_up_grad, through = backward(first_normed, rank_triple, joint_tokens, down_t, up_t)
    normed_one_grad = by_transpose(joint_tokens, wt) + through
    hidden_grad = (residual_grad + jax.vjp(first_norm, stream)[1](normed_one_grad)[0]).astype(jnp.bfloat16)
    summed = lax.psum(
        (
            triple_down_grad, triple_up_grad, mixer_down_grad, mixer_up_grad,
            expand_down_grad, expand_up_grad, reduce_down_grad, reduce_up_grad,
        ),
        ("head", "blk"),
    )

    def down_out(gradient):
        return jnp.transpose(gradient.reshape(ADAPTERS, RANK, gradient.shape[1]), (0, 2, 1))

    return (
        layer_out,
        hidden_grad,
        down_out(summed[0]),
        unflat_up(summed[1]),
        down_out(summed[2]),
        unflat_up(summed[3]),
        down_out(summed[4]),
        unflat_up(summed[5]),
        down_out(summed[6]),
        unflat_up(summed[7]),
    )


def solution(mesh):
    placed = (
        P(("blk", "head"), None),
        P(("blk", "head")),
        P(("head", "blk")),
        P(("head", "blk")),
        P(("head", "blk"), None),
        P(("head", "blk")),
        P(("head", "blk"), None),
        P(("head", "blk")),
        P(("head", "blk")),
        P(("head", "blk")),
        P(("head", "blk"), None),
        P(("head", "blk")),
        P(("head", "blk"), None),
        P(("head", "blk")),
        P(),
        P(),
        P(),
        P(),
        P(),
        P(),
        P(),
        P(),
        P(("blk", "head"), None),
    )
    fits = tuple(mesh.shape[name] for name in ("head", "blk")) == (2, CHIPS)
    return jax.shard_map(
        local_fast if fits else local,
        mesh=mesh,
        in_specs=placed,
        out_specs=(
            P(("blk", "head"), None),
            P(("blk", "head"), None),
            P(),
            P(),
            P(),
            P(),
            P(),
            P(),
            P(),
            P(),
        ),
        check_vma=False,
    )
```

```python
import functools
import math
import types

import jax
import jax.numpy as jnp
from jax import lax
from jax.experimental import pallas as pl
from jax.experimental.pallas import tpu as pltpu
from jax.sharding import PartitionSpec as P

WIDTH = 1024
HEADS = 16
HEAD_DIM = 64
RANK = 16
ADAPTERS = 8
BLOCK = 256


EPSILON = 1e-05


def product(left, right):
    return jnp.dot(left, right, preferred_element_type=jnp.float32)


def by_transpose(left, right):
    return lax.dot_general(
        left, right, (((1,), (1,)), ((), ())), preferred_element_type=jnp.float32
    )


def transpose_by(left, right):
    return lax.dot_general(
        left, right, (((0,), (0,)), ((), ())), preferred_element_type=jnp.float32
    )


def layer_norm(stream, scales, offset):
    average = jnp.mean(stream, axis=-1, keepdims=True)
    centred = stream - average
    variance = jnp.mean(centred * centred, axis=-1, keepdims=True)
    return centred * lax.rsqrt(variance + EPSILON) * scales + offset


def selector(adapter_index):
    column = jnp.arange(ADAPTERS * RANK, dtype=jnp.int32) // RANK
    return (adapter_index[:, None] == column[None, :]).astype(jnp.float32)


def flat_down(factor):
    return jnp.transpose(factor, (1, 0, 2)).reshape(factor.shape[1], ADAPTERS * RANK)


def flat_up(factor):
    return factor.reshape(ADAPTERS * RANK, factor.shape[2])


def unflat_down(gradient):
    return jnp.transpose(gradient.reshape(gradient.shape[0], ADAPTERS, RANK), (1, 0, 2))


def unflat_up(gradient):
    return gradient.reshape(ADAPTERS, RANK, gradient.shape[1])


def projected(source, weight, offset, down_flat, up_flat, selection):
    low_rank = (selection * product(source, down_flat)).astype(jnp.bfloat16)
    return (
        product(source, weight) + offset.astype(jnp.float32) + product(low_rank, up_flat),
        low_rank,
    )


def adapter_grads(source, low_rank, out_grad, down_flat, up_flat, selection):
    rank_grad = (selection * by_transpose(out_grad, up_flat)).astype(jnp.bfloat16)
    down_grad = transpose_by(source, rank_grad)
    up_grad = transpose_by(low_rank, out_grad)
    return (down_grad, up_grad, by_transpose(rank_grad, down_flat))


def score_block(queries, keys_block):
    return jnp.einsum("qhd,khd->qhk", queries, keys_block, preferred_element_type=jnp.float32) * (
        1.0 / math.sqrt(HEAD_DIM)
    )


def cut_rows(arrays, trailing):
    length = arrays[0].shape[0]
    block_rows = math.gcd(length, 512)
    repeats = length // block_rows
    shaped = tuple(
        (
            array.reshape((repeats, block_rows) + shape_tail)
            for array, shape_tail in zip(arrays, trailing)
        )
    )
    firsts = jnp.arange(repeats, dtype=jnp.int32) * block_rows
    return (shaped, firsts, block_rows)


def forward_fold(queries, query_places, locate, totals, portion):
    head_count = queries.shape[1]
    query_block = query_places // BLOCK
    last_block = jnp.max(query_block)
    shaped, firsts, block_rows = cut_rows(portion, ((head_count, HEAD_DIM), (head_count, HEAD_DIM)))

    def forward_visiting(carried, packet):
        keys_block, values_block, first_row = packet
        key_places = locate(first_row, block_rows)

        def forward_compute(running):
            numerator, denominator = running
            allowed = (key_places // BLOCK)[None, None, :] <= query_block[:, None, None]
            powers = jnp.where(allowed, jnp.exp(score_block(queries, keys_block)), 0.0)
            numerator = numerator + jnp.einsum(
                "qhk,khd->qhd",
                powers.astype(jnp.bfloat16),
                values_block,
                preferred_element_type=jnp.float32,
            )
            return (numerator, denominator + jnp.sum(powers, axis=-1))

        skipped = jnp.min(key_places) // BLOCK > last_block
        return (lax.cond(skipped, lambda running: running, forward_compute, carried), None)

    return lax.scan(forward_visiting, totals, shaped + (firsts,))[0]


def query_grad_fold(queries, query_places, locate, numer_grad, denom_grad, totals, portion):
    head_count = queries.shape[1]
    query_block = query_places // BLOCK
    last_block = jnp.max(query_block)
    shaped, firsts, block_rows = cut_rows(portion, ((head_count, HEAD_DIM), (head_count, HEAD_DIM)))

    def query_visiting(carried, packet):
        keys_block, values_block, first_row = packet
        key_places = locate(first_row, block_rows)

        def query_compute(running):
            allowed = (key_places // BLOCK)[None, None, :] <= query_block[:, None, None]
            powers = jnp.where(allowed, jnp.exp(score_block(queries, keys_block)), 0.0)
            prob_grad = jnp.einsum(
                "qhd,khd->qhk", numer_grad, values_block, preferred_element_type=jnp.float32
            )
            score_grad = (powers * (prob_grad + denom_grad[:, :, None])).astype(jnp.bfloat16)
            return running + jnp.einsum(
                "qhk,khd->qhd", score_grad, keys_block, preferred_element_type=jnp.float32
            )

        skipped = jnp.min(key_places) // BLOCK > last_block
        return (lax.cond(skipped, lambda running: running, query_compute, carried), None)

    return lax.scan(query_visiting, totals, shaped + (firsts,))[0]


def key_grad_fold(keys_here, values_here, key_places, locate, totals, portion):
    head_count = keys_here.shape[1]
    key_block = key_places // BLOCK
    first_block = jnp.min(key_block)
    shaped, firsts, block_rows = cut_rows(
        portion, ((head_count, HEAD_DIM), (head_count, HEAD_DIM), (head_count,))
    )

    def key_visiting(carried, packet):
        query_rows, numer_rows, denom_rows, first_row = packet
        query_places = locate(first_row, block_rows)

        def key_compute(running):
            keys_grad, values_grad = running
            allowed = key_block[None, None, :] <= (query_places // BLOCK)[:, None, None]
            powers = jnp.where(allowed, jnp.exp(score_block(query_rows, keys_here)), 0.0)
            prob_grad = jnp.einsum(
                "qhd,khd->qhk", numer_rows, values_here, preferred_element_type=jnp.float32
            )
            score_grad = (powers * (prob_grad + denom_rows.astype(jnp.float32)[:, :, None])).astype(
                jnp.bfloat16
            )
            keys_grad = keys_grad + jnp.einsum(
                "qhk,qhd->khd", score_grad, query_rows, preferred_element_type=jnp.float32
            )
            values_grad = values_grad + jnp.einsum(
                "qhk,qhd->khd",
                powers.astype(jnp.bfloat16),
                numer_rows,
                preferred_element_type=jnp.float32,
            )
            return (keys_grad, values_grad)

        skipped = jnp.max(query_places) // BLOCK < first_block
        return (lax.cond(skipped, lambda running: running, key_compute, carried), None)

    return lax.scan(key_visiting, totals, shaped + (firsts,))[0]


def local(
    hidden,
    adapter_index,
    first_gain,
    first_bias,
    triple_weight,
    triple_bias,
    mixer_weight,
    mixer_bias,
    second_gain,
    second_bias,
    expand_weight,
    expand_bias,
    reduce_weight,
    reduce_bias,
    triple_down,
    triple_up,
    mixer_down,
    mixer_up,
    expand_down,
    expand_up,
    reduce_down,
    reduce_up,
    cotangent,
):
    gathered = (
        lax.all_gather(first_gain, ("head", "blk"), axis=0, tiled=True),
        lax.all_gather(first_bias, ("head", "blk"), axis=0, tiled=True),
        lax.all_gather(triple_weight, ("head", "blk"), axis=0, tiled=True),
        lax.all_gather(triple_bias, ("head", "blk"), axis=0, tiled=True),
        lax.all_gather(mixer_weight, ("head", "blk"), axis=0, tiled=True),
        lax.all_gather(mixer_bias, ("head", "blk"), axis=0, tiled=True),
        lax.all_gather(second_gain, ("head", "blk"), axis=0, tiled=True),
        lax.all_gather(second_bias, ("head", "blk"), axis=0, tiled=True),
        lax.all_gather(expand_weight, ("head", "blk"), axis=0, tiled=True),
        lax.all_gather(expand_bias, ("head", "blk"), axis=0, tiled=True),
        lax.all_gather(reduce_weight, ("head", "blk"), axis=0, tiled=True),
        lax.all_gather(reduce_bias, ("head", "blk"), axis=0, tiled=True),
    )
    (
        gain_one,
        bias_one,
        weight_triple,
        bias_triple,
        weight_mixer,
        bias_mixer,
        gain_two,
        bias_two,
        weight_expand,
        bias_expand,
        weight_reduce,
        bias_reduce,
    ) = gathered
    token_count = hidden.shape[0]
    head_ways = lax.axis_size("head")
    cycle_ways = lax.axis_size("blk")
    selection = selector(adapter_index)
    down_triple = flat_down(triple_down)
    upward_triple = flat_up(triple_up)
    down_mixer = flat_down(mixer_down)
    upward_mixer = flat_up(mixer_up)
    down_expand = flat_down(expand_down)
    upward_expand = flat_up(expand_up)
    down_reduce = flat_down(reduce_down)
    upward_reduce = flat_up(reduce_up)
    stream = hidden.astype(jnp.float32)

    def first_norm(values_in):
        return layer_norm(values_in, gain_one.astype(jnp.float32), bias_one.astype(jnp.float32))

    def second_norm(values_in):
        return layer_norm(values_in, gain_two.astype(jnp.float32), bias_two.astype(jnp.float32))

    first_normed = first_norm(stream).astype(jnp.bfloat16)
    joint, rank_triple = projected(
        first_normed, weight_triple, bias_triple, down_triple, upward_triple, selection
    )
    joint = joint.astype(jnp.bfloat16)
    parts = joint.reshape(token_count, 3, HEADS, HEAD_DIM)
    own_shard = lax.axis_index("blk") * head_ways + lax.axis_index("head")
    query_places = own_shard * token_count + jnp.arange(token_count, dtype=jnp.int32)

    def locate(first_row, length):
        rows_here = first_row + jnp.arange(length, dtype=jnp.int32)
        shard_index = rows_here // token_count
        return (
            shard_index % cycle_ways * head_ways + shard_index // cycle_ways
        ) * token_count + rows_here % token_count

    queries = parts[:, 0]
    keys_here = parts[:, 1]
    values_here = parts[:, 2]
    head_count = queries.shape[1]
    flat_keys = keys_here.reshape(token_count, head_count * HEAD_DIM)
    flat_values = values_here.reshape(token_count, head_count * HEAD_DIM)
    zeros_rows = jnp.zeros((token_count, head_count, HEAD_DIM), jnp.float32)
    payload = (flat_keys, flat_values)
    numerator, denominator = forward_fold(
        queries,
        query_places,
        locate,
        (zeros_rows, jnp.zeros((token_count, head_count), jnp.float32)),
        (
            lax.all_gather(payload[0], ("head", "blk"), axis=0, tiled=True),
            lax.all_gather(payload[1], ("head", "blk"), axis=0, tiled=True),
        ),
    )
    attended = numerator / denominator[:, :, None]
    attended_low = attended.astype(jnp.bfloat16).reshape(token_count, WIDTH)
    mixed, rank_mixer = projected(
        attended_low, weight_mixer, bias_mixer, down_mixer, upward_mixer, selection
    )
    residual = stream + mixed
    second_normed = second_norm(residual).astype(jnp.bfloat16)
    expanded, rank_expand = projected(
        second_normed, weight_expand, bias_expand, down_expand, upward_expand, selection
    )
    activated = jax.nn.gelu(expanded, approximate=True).astype(jnp.bfloat16)
    reduced, rank_reduce = projected(
        activated, weight_reduce, bias_reduce, down_reduce, upward_reduce, selection
    )
    layer_out = (residual + reduced).astype(jnp.bfloat16)
    reduce_down_grad, reduce_up_grad, through_reduce = adapter_grads(
        activated, rank_reduce, cotangent, down_reduce, upward_reduce, selection
    )
    activated_grad = (by_transpose(cotangent, weight_reduce) + through_reduce).astype(jnp.bfloat16)
    gelu_back = jax.vjp(lambda values_in: jax.nn.gelu(values_in, approximate=True), expanded)[1]
    expanded_grad = gelu_back(activated_grad.astype(jnp.float32))[0].astype(jnp.bfloat16)
    expand_down_grad, expand_up_grad, through_expand = adapter_grads(
        second_normed, rank_expand, expanded_grad, down_expand, upward_expand, selection
    )
    normed_grad = by_transpose(expanded_grad, weight_expand) + through_expand
    second_back = jax.vjp(second_norm, residual)[1]
    residual_grad = cotangent.astype(jnp.float32) + second_back(normed_grad)[0]
    mixed_grad = residual_grad.astype(jnp.bfloat16)
    mixer_down_grad, mixer_up_grad, through_mixer = adapter_grads(
        attended_low, rank_mixer, mixed_grad, down_mixer, upward_mixer, selection
    )
    attended_grad = (by_transpose(mixed_grad, weight_mixer) + through_mixer).astype(jnp.bfloat16)
    output_grad = attended_grad.reshape(token_count, HEADS, HEAD_DIM).astype(jnp.float32)
    numer_grad = (output_grad / denominator[:, :, None]).astype(jnp.bfloat16)
    denom_grad = (-jnp.sum(output_grad * attended, axis=-1) / denominator).astype(jnp.bfloat16)
    payload = (flat_keys, flat_values)
    query_grad = query_grad_fold(
        queries,
        query_places,
        locate,
        numer_grad,
        denom_grad.astype(jnp.float32),
        zeros_rows,
        (
            lax.all_gather(payload[0], ("head", "blk"), axis=0, tiled=True),
            lax.all_gather(payload[1], ("head", "blk"), axis=0, tiled=True),
        ),
    )
    payload = (
        queries.reshape(token_count, head_count * HEAD_DIM),
        numer_grad.reshape(token_count, head_count * HEAD_DIM),
        denom_grad,
    )
    keys_grad, values_grad = key_grad_fold(
        keys_here,
        values_here,
        query_places,
        locate,
        (zeros_rows, zeros_rows),
        (
            lax.all_gather(payload[0], ("head", "blk"), axis=0, tiled=True),
            lax.all_gather(payload[1], ("head", "blk"), axis=0, tiled=True),
            lax.all_gather(payload[2], ("head", "blk"), axis=0, tiled=True),
        ),
    )
    factor = 1.0 / math.sqrt(HEAD_DIM)
    joint_grad = jnp.stack([query_grad * factor, keys_grad * factor, values_grad], axis=1).astype(
        jnp.bfloat16
    )
    joint_tokens = joint_grad.reshape(token_count, 3 * WIDTH)
    triple_down_grad, triple_up_grad, through_triple = adapter_grads(
        first_normed, rank_triple, joint_tokens, down_triple, upward_triple, selection
    )
    normed_one_grad = by_transpose(joint_tokens, weight_triple) + through_triple
    first_back = jax.vjp(first_norm, stream)[1]
    hidden_grad = (residual_grad + first_back(normed_one_grad)[0]).astype(jnp.bfloat16)
    summed = lax.psum(
        (
            triple_down_grad,
            triple_up_grad,
            mixer_down_grad,
            mixer_up_grad,
            expand_down_grad,
            expand_up_grad,
            reduce_down_grad,
            reduce_up_grad,
        ),
        ("head", "blk"),
    )
    return (
        layer_out,
        hidden_grad,
        unflat_down(summed[0]),
        unflat_up(summed[1]),
        unflat_down(summed[2]),
        unflat_up(summed[3]),
        unflat_down(summed[4]),
        unflat_up(summed[5]),
        unflat_down(summed[6]),
        unflat_up(summed[7]),
    )


MESH = pl.DeviceIdType.MESH
CHIPS = 16
LIMIT = 62 * 1024 * 1024 - 512 * 1024
BF = jnp.bfloat16
F4 = jnp.float32


ALONG = ((0, 1, 2, 3), (1, 0, 2, 3), (2, 1, 3, 0), (3, 2, 1, 0))


class Links:
    def __init__(self):
        self.h = lax.axis_index("head")
        self.b = lax.axis_index("blk")
        self.o = 1 - self.h
        self.sent = []
        self.x = lax.rem(self.b, 2)
        self.y = lax.rem(self.b // 2, 2)
        self.z = self.b // 4
        self.xb = self.b + 1 - 2 * self.x
        self.yb = self.b + 2 - 4 * self.y
        self.db = self.xb + 2 - 4 * self.y
        self.columns = [lax.rem(chip, 4) for chip in (self.b, self.xb, self.yb, self.db)]

    def nth(self, n):
        return sum(jnp.where(self.z == z, table[n], 0) for z, table in enumerate(ALONG))

    def at_line(self, z):
        return lax.rem(self.b, 4) + 4 * z

    def along(self, piece, sems, index):
        for k, wanted in ((1, self.z < 3), (3, self.z > 0), (2, None)):
            where = (piece, piece, sems, index + (self.z,), (self.h, self.ahead(4 * k)))
            if wanted is None:
                self.send(*where)
            else:
                self.send_if(wanted, *where)

    def pass_on(self, piece, z, sems, index):
        wanted = (self.z == 2) & (z == 0) | (self.z == 1) & (z == 3)
        chip = self.columns[0] + 4 * (3 - z)
        self.send_if(wanted, piece, piece, sems, index + (z,), (self.h, chip))

    def ahead(self, k):
        return lax.rem(self.b + k, CHIPS)

    def behind(self, k):
        return lax.rem(self.b + CHIPS - k, CHIPS)

    def greet(self):
        barrier = pltpu.get_barrier_semaphore()
        for k in range(1, CHIPS):
            pl.semaphore_signal(
                barrier, 1, device_id=(self.h, self.ahead(k)), device_id_type=MESH
            )
        pl.semaphore_signal(barrier, 1, device_id=(self.o, self.b), device_id_type=MESH)

    def met(self):
        pl.semaphore_wait(pltpu.get_barrier_semaphore(), CHIPS)

    def copy(self, source, target, sems, at, device):
        return pltpu.make_async_remote_copy(
            src_ref=source,
            dst_ref=target,
            send_sem=sems[0].at[at],
            recv_sem=sems[1].at[at],
            device_id=device,
            device_id_type=MESH,
        )

    def send(self, source, target, sems, at, device):
        copy = self.copy(source, target, sems, at, device)
        copy.start()
        self.sent.append((None, copy))

    def send_if(self, wanted, *where):
        copy = self.copy(*where)
        pl.when(wanted)(copy.start)
        self.sent.append((wanted, copy))

    def arrived(self, target, sems, at):
        self.copy(target, target, sems, at, (self.o, self.b)).wait_recv()

    def settle(self):
        for wanted, copy in self.sent:
            if wanted is None:
                copy.wait_send()
            else:
                pl.when(wanted)(copy.wait_send)
        self.sent = []


class Exchange:
    def __init__(self, links, source, target, rows, sems, slot=None):
        self.links, self.source, self.target = links, source, target
        self.rows, self.sems = rows, sems
        self.slot = slot or (lambda chip: rows_at(target, chip * rows, rows))

    def send(self, t):
        l = self.links

        @pl.when(l.b != t)
        def _():
            l.copy(
                rows_at(self.source, t * self.rows, self.rows),
                self.slot(l.b), self.sems, lax.rem(t + CHIPS - l.b, CHIPS), (l.h, t),
            ).start()

    def own(self):
        l = self.links
        copy = pltpu.make_async_copy(
            rows_at(self.source, l.b * self.rows, self.rows), self.slot(l.b), self.sems[0].at[0]
        )
        copy.start()
        copy.wait()

    def wait(self, k):
        self.links.arrived(self.slot(self.links.behind(k)), self.sems, k)

    def settle(self):
        for k in range(1, CHIPS):
            l = self.links
            part = rows_at(self.source, l.ahead(k) * self.rows, self.rows)
            l.copy(part, part, self.sems, k, (l.h, l.ahead(k))).wait_send()


def half_mask(rows):
    return lax.broadcasted_iota(jnp.int32, (rows, 128), 1) < 64


def swap(tile):
    return pltpu.roll(tile, 64, 1)


def rows_at(ref, start, count):
    return ref.at[pl.ds(pl.multiple_of(start, 16), count), :]


class Gather:
    def __init__(self, links, number, slot, sems):
        self.links, self.p, self.slot = links, number, slot
        self.sems = sems

    def send(self, axis, n, chip, device):
        piece = self.slot(self.links.h, chip)
        self.links.send(piece, piece, self.sems[axis], (self.p, n), device)

    def chip(self, side, n):
        return side + 4 * self.links.nth(n)

    def own(self, n):
        l = self.links
        chip = self.chip(l.columns[0], n)
        if n:
            l.pass_on(self.slot(l.h, chip), l.nth(n), self.sems["z"], (self.p,))
        else:
            l.along(self.slot(l.h, chip), self.sems["z"], (self.p,))
        self.send("x", n, chip, (l.h, l.xb))
        self.send("y", n, chip, (l.h, l.yb))
        self.send("c", n, chip, (l.o, l.b))

    def from_line(self, n):
        l = self.links
        chip = self.chip(l.columns[0], n)
        l.arrived(self.slot(l.h, chip), self.sems["z"], (self.p, l.nth(n)))
        self.own(n)

    def arrived(self, axis, n, chip):
        self.links.arrived(self.slot(self.links.h, chip), self.sems[axis], (self.p, n))

    def from_side(self, axis, n):
        l = self.links
        chip = self.chip(l.columns[1 if axis == "x" else 2], n)
        self.arrived(axis, n, chip)
        if (n % 2 == 0) == (axis == "x"):
            self.send("d", n, chip, (l.h, l.yb if axis == "x" else l.xb))
        self.send("c", (4 if axis == "x" else 8) + n, chip, (l.o, l.b))

    def from_corner(self, n):
        l = self.links
        chip = self.chip(l.columns[3], n)
        self.arrived("d", n, chip)
        self.send("c", 12 + n, chip, (l.o, l.b))

    def stages(self):
        part = functools.partial
        return [
            [part(self.own, 0)],
            [part(self.from_line, 1), part(self.from_side, "x", 0), part(self.from_side, "y", 0), part(self.from_line, 2)],
            [part(self.from_side, axis, 1) for axis in "xy"]
            + [part(self.from_line, 3)]
            + [part(self.from_side, axis, n) for n in (2, 3) for axis in "xy"],
            [part(self.from_corner, n) for n in range(4)],
        ]

    def whole(self):
        l = self.links
        for number in range(16):
            chip = self.chip(l.columns[number // 4], number % 4)
            l.arrived(self.slot(l.o, chip), self.sems["c"], (self.p, number))


class RowSlice:
    def __init__(self, links, ref, sems):
        self.links, self.ref = links, ref
        self.line_sems, self.core_sems = sems

    def slot(self, h, z):
        return rows_at(self.ref, (h * 4 + z) * 128, 128)

    def core(self, k, z):
        l = self.links
        l.send(self.slot(l.h, z), self.slot(l.h, z), self.core_sems, k, (l.o, l.b))

    def own(self, n):
        l = self.links
        z = l.nth(n)
        if n:
            l.pass_on(self.slot(l.h, z), z, self.line_sems, ())
        else:
            l.along(self.slot(l.h, z), self.line_sems, ())
        self.core(n, z)

    def from_line(self, n):
        l = self.links
        z = l.nth(n)
        l.arrived(self.slot(l.h, z), self.line_sems, (z,))
        self.own(n)

    def stages(self):
        part = functools.partial
        return [[part(self.own, 0)], [part(self.from_line, 1)], [part(self.from_line, 2)], [part(self.from_line, 3)]]

    def whole(self):
        l = self.links
        for n in range(4):
            l.arrived(self.slot(l.o, l.nth(n)), self.core_sems, n)


class ColumnSlice:
    def __init__(self, links, ref, stage, sems):
        self.links, self.ref, self.stage = links, ref, stage
        self.plane_sems, self.line_sems, self.core_sems = sems

    def chip(self, j, n):
        return self.links.columns[j] + 4 * self.links.nth(n)

    def slot(self, h, chip):
        return rows_at(self.ref, shard_of(h, chip) * 32, 32)

    def own(self, j, n):
        l = self.links
        piece = self.slot(l.h, self.chip(j, n))
        if n:
            l.pass_on(piece, l.nth(n), self.line_sems, (j,))
        else:
            l.along(piece, self.line_sems, (j,))
        l.send(piece, piece, self.core_sems, (j, n), (l.o, l.b))

    def start(self):
        l = self.links
        for j, chip in enumerate((l.b, l.xb, l.yb, l.db)):
            if j:
                l.send(rows_at(self.stage, j * 32, 32), self.slot(l.h, l.b), self.plane_sems, j, (l.h, chip))

    def from_plane(self, j):
        self.links.arrived(self.slot(self.links.h, self.chip(j, 0)), self.plane_sems, j)
        self.own(j, 0)

    def from_line(self, j, n):
        l = self.links
        l.arrived(self.slot(l.h, self.chip(j, n)), self.line_sems, (j, l.nth(n)))
        self.own(j, n)

    def stages(self):
        part = functools.partial
        return [
            [self.start],
            [part(self.own, 0, 0)] + [part(self.from_plane, j) for j in range(1, 4)],
            [part(self.from_line, j, n) for n in range(1, 4) for j in range(4)],
        ]

    def whole(self):
        l = self.links
        for j in range(4):
            for n in range(4):
                l.arrived(self.slot(l.o, self.chip(j, n)), self.core_sems, (j, n))


def ordered(stages, lag):
    events = []
    deepest = max(len(stage) for stage in stages)
    for tick in range(len(stages) * lag + deepest):
        for n, stage in enumerate(stages):
            if 0 <= tick - n * lag < len(stage):
                events += stage[tick - n * lag]
    return events


class Reduce:
    def __init__(self, links, g, out, base, width, bufs, sems):
        self.l, self.g, self.out, self.base, self.sems = links, g, out, base, sems
        self.by_core, self.by_side, self.by_turn, self.by_line = bufs
        self.half, self.p = width // 2, width // 4
        l = links
        self.mine = base + l.h * self.half
        p = self.p
        self.keep1 = (self.mine + l.x * (p // 2), self.mine + p + l.y * (p // 2))
        self.give1 = (self.mine + (1 - l.x) * (p // 2), self.mine + p + (1 - l.y) * (p // 2))
        self.keep2 = (self.keep1[0] + l.y * (p // 4), self.keep1[1] + l.x * (p // 4))
        self.give2 = (self.keep1[0] + (1 - l.y) * (p // 4), self.keep1[1] + (1 - l.x) * (p // 4))

    def at(self, start, width):
        return self.g.at[:, pl.ds(pl.multiple_of(start, 128), width)]

    def out_at(self, start, width):
        return self.out.at[:, pl.ds(pl.multiple_of(start, 128), width)]

    def chunk(self, z):
        first, second = self.keep2
        return first * (1 - z // 2) + second * (z // 2) + lax.rem(z, 2) * (self.p // 8)

    def add(self, start, width, others, final=False):
        tile = 384 if width % 384 == 0 else 128
        for n in range(width // tile):
            here = pl.ds(pl.multiple_of(start + n * tile, 128), tile)
            total = self.g[:, here].astype(F4)
            for other in others:
                total = total + other[:, n * tile : (n + 1) * tile].astype(F4)
            (self.out if final else self.g)[:, here] = total.astype(BF)

    def steps(self):
        l, p = self.l, self.p
        sides, turns = (l.xb, l.yb), (l.yb, l.xb)

        def cores():
            away = self.base + l.o * self.half
            l.send(self.at(away, self.half), self.by_core, self.sems, 0, (l.o, l.b))

        def side():
            l.arrived(self.by_core, self.sems, 0)
            for n in range(2):
                self.add(self.give1[n], p // 2, [self.by_core.at[:, pl.ds(pl.multiple_of(self.give1[n] - self.mine, 128), p // 2)]])
                l.send(self.at(self.give1[n], p // 2), self.by_side.at[n], self.sems, 1 + n, (l.h, sides[n]))
            for n in range(2):
                self.add(self.keep1[n], p // 2, [self.by_core.at[:, pl.ds(pl.multiple_of(self.keep1[n] - self.mine, 128), p // 2)]])

        def turn():
            for n in range(2):
                l.arrived(self.by_side.at[n], self.sems, 1 + n)
                self.add(self.keep1[n], p // 2, [self.by_side.at[n]])
                l.send(self.at(self.give2[n], p // 4), self.by_turn.at[n], self.sems, 3 + n, (l.h, turns[n]))

        def line():
            for n in range(2):
                l.arrived(self.by_turn.at[n], self.sems, 3 + n)
                self.add(self.keep2[n], p // 4, [self.by_turn.at[n]])
            for k in range(1, 4):
                away = self.chunk(lax.rem(l.z + k, 4))
                l.send(self.at(away, p // 8), self.by_line.at[k - 1], self.sems, 4 + k, (l.h, l.ahead(4 * k)))

        def line_back():
            for k in range(1, 4):
                l.arrived(self.by_line.at[k - 1], self.sems, 4 + k)
            self.add(self.chunk(l.z), p // 8, [self.by_line.at[k] for k in range(3)], True)
            here = self.out_at(self.chunk(l.z), p // 8)
            for k in range(1, 4):
                l.send(here, here, self.sems, 7 + k, (l.h, l.ahead(4 * k)))

        def turn_back():
            for k in range(1, 4):
                l.arrived(self.out_at(self.chunk(lax.rem(l.z + 4 - k, 4)), p // 8), self.sems, 7 + k)
            for n in range(2):
                here = self.out_at(self.keep2[n], p // 4)
                l.send(here, here, self.sems, 11 + n, (l.h, turns[n]))

        def side_back():
            for n in range(2):
                l.arrived(self.out_at(self.give2[n], p // 4), self.sems, 11 + n)
                here = self.out_at(self.keep1[n], p // 2)
                l.send(here, here, self.sems, 13 + n, (l.h, sides[n]))

        def cores_back():
            for n in range(2):
                l.arrived(self.out_at(self.give1[n], p // 2), self.sems, 13 + n)
            here = self.out_at(self.mine, self.half)
            l.send(here, here, self.sems, 15, (l.o, l.b))

        def done():
            l.arrived(self.out_at(self.base + l.o * self.half, self.half), self.sems, 15)

        return [cores, side, turn, line, line_back, turn_back, side_back, cores_back, done]


class SliceReduce:
    def __init__(self, links, g, out, base, bufs, sems):
        self.l, self.g, self.out, self.base, self.sems = links, g, out, base, sems
        self.by_core, self.by_line = bufs

    def at(self, ref, start, width):
        return ref.at[:, pl.ds(pl.multiple_of(start, 128), width)]

    def steps(self):
        l = self.l
        chips = (l.b, l.xb, l.yb, l.db)
        places = [
            self.base + 2048 * (lax.rem(chip, 4)) for chip in chips
        ]

        def region(j, h, z=None):
            if z is None:
                return self.at(self.out, places[j] + h * 1024, 1024)
            return self.at(self.out, places[j] + h * 1024 + z * 256, 256)

        def cores():
            l.send(self.at(self.g, l.o * 1024, 1024), self.by_core, self.sems, 0, (l.o, l.b))

        def line():
            l.arrived(self.by_core, self.sems, 0)
            for n in range(4):
                here = pl.ds(pl.multiple_of(l.h * 1024 + n * 256, 128), 256)
                total = self.g[:, here].astype(F4) + self.by_core[:, n * 256 : (n + 1) * 256].astype(F4)
                self.g[:, here] = total.astype(BF)
            for k in range(1, 4):
                z = lax.rem(l.z + k, 4)
                l.send(self.at(self.g, l.h * 1024 + z * 256, 256), self.by_line.at[k - 1], self.sems, k, (l.h, l.ahead(4 * k)))

        def line_back():
            total = self.g[:, pl.ds(pl.multiple_of(l.h * 1024 + l.z * 256, 128), 256)].astype(F4)
            for k in range(1, 4):
                l.arrived(self.by_line.at[k - 1], self.sems, k)
                total = total + self.by_line[k - 1].astype(F4)
            self.out[:, pl.ds(pl.multiple_of(places[0] + l.h * 1024 + l.z * 256, 128), 256)] = total.astype(BF)
            for k in range(1, 4):
                l.send(region(0, l.h, l.z), region(0, l.h, l.z), self.sems, 3 + k, (l.h, l.ahead(4 * k)))

        def plane():
            for k in range(1, 4):
                l.arrived(region(0, l.h, lax.rem(l.z + 4 - k, 4)), self.sems, 3 + k)
            for j in range(1, 4):
                l.send(region(0, l.h), region(0, l.h), self.sems, 6 + j, (l.h, chips[j]))
            l.send(region(0, l.h), region(0, l.h), self.sems, 10, (l.o, l.b))

        def cores_back():
            for j in range(1, 4):
                l.arrived(region(j, l.h), self.sems, 6 + j)
                l.send(region(j, l.h), region(j, l.h), self.sems, 10 + j, (l.o, l.b))

        def done():
            for j in range(4):
                l.arrived(region(j, l.o), self.sems, 10 + j)

        return [cores, line, line_back, plane, cores_back, done]


def shard_of(h, chip):
    return h * CHIPS + chip


def centre(stream):
    average = jnp.mean(stream, axis=-1, keepdims=True)
    centred = stream - average
    variance = jnp.mean(centred * centred, axis=-1, keepdims=True)
    scale = lax.rsqrt(variance + EPSILON)
    return centred * scale, scale


def norm_back(stream, gain, grad):
    hat, scale = centre(stream)
    q = grad * gain
    return scale * (
        q - jnp.mean(q, axis=-1, keepdims=True) - hat * jnp.mean(q * hat, axis=-1, keepdims=True)
    )


def gelu_parts(u):
    cubic = 0.044715 * u * u
    slope = math.sqrt(2.0 / math.pi)
    t = jnp.tanh(slope * u * (1.0 + cubic))
    grown = 0.5 * (1.0 + t)
    return u * grown, grown + 0.5 * u * (1.0 - t * t) * slope * (1.0 + 3.0 * cubic)


PIECES = 5
MIXER_D, MIXER_U, EXPAND_D, REDUCE_U, TRIPLE_D, TRIPLE_U, SLICES, COLUMNS = (
    0, 1024, 2048, 3072, 4096, 5120, 8192, 16384,
)

INPUTS = (
    "hidden", "cot", "sel", "small_sh", "triple_sh", "mixer_sh", "reduce_sh", "expand_sh",
    "down_t", "up_t", "down_m", "up_m", "down_e", "up_e", "down_r", "up_r",
)
OUTPUTS = {"layer_out": ((128, 1024), BF), "hidden_grad": ((128, 1024), BF), "g": ((128, COLUMNS), BF)}
SCRATCH = {
    "wt": ((1024, 3072), BF), "wm": ((1024, 1024), BF), "wr": ((1024, 1024), BF), "we": ((1024, 1024), BF),
    "e_in": ((32, 4096), BF), "e_stage": ((128, 1024), BF), "up_es": ((128, 1024), BF), "down_rs": ((128, 1024), BF), "bias_es": ((1, 1024), F4),
    "small": ((512, 128), BF), "vecs": ((16, 1024), F4), "bias_t": ((1, 3072), F4), "bias_e": ((1, 4096), F4),
    "fn": ((128, 1024), BF), "rank_t": ((128, 128), BF), "kv": ((4096, 128), BF), "q": ((2048, 128), BF),
    "attden": ((2048, 128), F4), "attended": ((128, 1024), BF), "ones_v": ((4096, 128), BF),
    "send_kv": ((2048, 128), BF), "send_q": ((1024, 128), BF), "recv_q": ((1024, 128), BF),
    "send_a": ((1024, 128), BF), "recv_a": ((1024, 128), BF),
    "residual": ((128, 1024), F4), "sn_all": ((512, 1152), BF), "cot_all": ((512, 1152), BF),
    "act": ((512, 1024), BF), "agrad": ((512, 1024), BF), "ng_part": ((512, 1152), BF), "ng_recv": ((512, 1152), BF),
    "red_part": ((512, 1152), BF), "red_recv": ((512, 1152), BF),
    "send_g": ((1024, 128), BF), "recv_g": ((1024, 128), BF),
    "qd": ((2048, 128), BF), "dz": ((2048, 128), BF), "vz": ((4096, 128), BF),
    "k_t": ((64, 4096), BF), "ddrow": ((1, 2048), F4), "dq_t": ((128, 2048), F4), "part": ((4096, 128), F4),
    "recv_part": ((2048, 128), F4), "send_dkv": ((2048, 128), BF), "send_dq": ((1024, 128), BF),
    "recv_dkv": ((2048, 128), BF), "recv_dq": ((1024, 128), BF), "jg": ((128, 3072), BF),
"gp": ((128, SLICES), BF), "gs": ((128, 2048), BF), "slice_c": ((128, 1024), BF), "slice_l": ((3, 128, 256), BF),
    "early_c": ((128, 2048), BF), "early_1": ((2, 128, 512), BF), "early_2": ((2, 128, 256), BF), "early_3": ((3, 128, 128), BF),
    "late_c": ((128, 2048), BF), "late_1": ((2, 128, 512), BF), "late_2": ((2, 128, 256), BF), "late_3": ((3, 128, 128), BF),
}
SEMS = {
    "z": (PIECES, 4), "x": (PIECES, 4), "y": (PIECES, 4), "d": (PIECES, 4), "c": (PIECES, 16),
    "kv": (16,), "q": (16,), "f": (16,), "a": (16,), "g": (16,), "e": (16,), "dkv": (16,), "dq": (16,),
    "early": (16,), "late": (16,), "slice": (16,),
    "rz": (4,), "rc": (4,), "ep": (4,), "ez": (4, 4), "ec": (4, 4), "ct": (2, 4), "sn": (2, 4), "ng": (2, 4), "rd": (2, 4),
}


def layer_kernel(*refs):
    names = list(INPUTS) + list(OUTPUTS) + list(SCRATCH)
    r = types.SimpleNamespace(**dict(zip(names, refs)))
    rest = refs[len(names) :]
    local_sem = rest[0]
    sems = {name: (rest[1 + 2 * n], rest[2 + 2 * n]) for n, name in enumerate(SEMS)}
    l = Links()
    low, low64 = half_mask(128), half_mask(64)
    mine = shard_of(l.h, l.b)
    local_copies = [
        pltpu.make_async_copy(r.small_sh, rows_at(r.small, mine * 16, 16), local_sem.at[0]),
        pltpu.make_async_copy(r.triple_sh, rows_at(r.wt, mine * 32, 32), local_sem.at[1]),
        pltpu.make_async_copy(r.mixer_sh, rows_at(r.wm, mine * 32, 32), local_sem.at[2]),
        pltpu.make_async_copy(r.reduce_sh, rows_at(r.wr, (l.h * 4 + l.z) * 128, 128), local_sem.at[3]),
        pltpu.make_async_copy(r.expand_sh, r.e_in, local_sem.at[4]),
    ]
    for copy in local_copies:
        copy.start()
    l.greet()

    def columns(ref, at):
        return lambda h, chip: ref.at[
            pl.ds(pl.multiple_of(shard_of(h, chip) * 32, 32), 32), at : at + 1024
        ]

    slots = [lambda h, chip: rows_at(r.small, shard_of(h, chip) * 16, 16)]
    slots += [columns(r.wt, m * 1024) for m in range(3)]
    slots += [columns(r.wm, 0)]
    pieces = [Gather(l, n, slot, sems) for n, slot in enumerate(slots)]
    pieces.append(RowSlice(l, r.wr, (sems["rz"], sems["rc"])))
    pieces.append(ColumnSlice(l, r.we, r.e_stage, (sems["ep"], sems["ez"], sems["ec"])))
    places = [lax.rem(chip, 4) for chip in (l.b, l.xb, l.yb, l.db)]

    def block(j, i):
        return pl.ds(pl.multiple_of((i // 4 * 16 + places[j] + i % 4 * 4) * 128, 128), 128)

    for i in range(8):
        here = slice(i * 128, (i + 1) * 128)
        r.up_es[:, here] = r.up_e[:, block(0, i)]
        r.down_rs[:, here] = r.down_r[:, block(0, i)]
    for copy in local_copies:
        copy.wait()
    for i in range(8):
        here = slice(i * 128, (i + 1) * 128)
        r.we[pl.ds(pl.multiple_of(mine * 32, 32), 32), here] = r.e_in[:, block(0, i)]
        for j in range(1, 4):
            r.e_stage[j * 32 : (j + 1) * 32, here] = r.e_in[:, block(j, i)]
    l.met()
    stages = [piece.stages() for piece in pieces]
    events = [event for n in (0, 1, 2, 3, 6) for event in stages[n].pop(0)]
    stages[2][1] += stages[5].pop(0)
    events += ordered(stages[:4], 1)
    ends = {n: len(events) for n in range(4)}
    begun = len(events) + 1
    events += stages[4].pop(0)
    crossed = len(events) + 8
    events += [event for stage in stages[4] for event in stage]
    ends[4] = len(events)
    events += stages[6].pop(0)
    kicked = len(events)
    events += [event for stage in stages[5] for event in stage]
    ends[5] = len(events)
    events += [event for stage in stages[6] for event in stage]
    ends[6] = len(events)
    state = [0]

    def pump(count):
        until(state[0] + count)

    def until(end):
        end = min(end, len(events))
        while state[0] < end:
            events[state[0]]()
            state[0] += 1

    def need(first, last):
        until(ends[last])
        for n in range(first, last + 1):
            pieces[n].whole()

    until(ends[3] - 4)
    pieces[0].whole()
    for g in range(8):
        tile = jnp.zeros((16, 128), F4)
        for n in range(4):
            at = (4 * g + n) * 16
            tile = tile + r.small[at : at + 16, :].astype(F4)
        r.vecs[:, g * 128 : (g + 1) * 128] = tile
        for n in range(3):
            at = (g * 3 + n) * 128
            r.bias_t[0:1, at : at + 128] = tile[6 + n : 7 + n, :]
        for n in range(4):
            at = (g * 4 + n) * 128
            r.bias_e[0:1, at : at + 128] = tile[9 + n : 10 + n, :]
    gain_one, bias_one, bias_m, gain_two, bias_two, bias_r = [
        (lambda n=n: r.vecs[n : n + 1, :]) for n in range(6)
    ]
    hat, _ = centre(r.hidden[...].astype(F4))
    r.fn[...] = (hat * gain_one() + bias_one()).astype(BF)

    def rank(source, down):
        return (r.sel[...] * by_transpose(source, down)).astype(BF)

    r.rank_t[...] = rank(r.fn[...], r.down_t[...])
    need(1, 3)
    until(begun)

    own = l.b * 256 + l.h * 128

    def kv_at(chip, h):
        return rows_at(r.kv, chip * 256 + h * 128, 128)

    kv_out = Exchange(l, r.send_kv, r.kv, 128, sems["kv"], lambda chip: kv_at(chip, l.h))
    q_out = Exchange(l, r.send_q, r.recv_q, 64, sems["q"])
    for step in range(4):
        plane = lax.rem(l.z + 1 + step, 4)

        def joint(part):
            at = pl.ds(pl.multiple_of(part * 1024 + plane * 256, 256), 256)
            tile = (
                product(r.fn[...], r.wt[:, at]) + r.bias_t[0:1, at] + product(r.rank_t[...], r.up_t[:, at])
            )
            return tile[:, :128], tile[:, 128:]

        for n, (qt, kt, vt) in enumerate(zip(joint(0), joint(1), joint(2))):
            c = plane * 4 + n * 2
            send_kv, send_q = rows_at(r.send_kv, c * 128, 256), rows_at(r.send_q, c * 64, 128)
            send_kv[0:128, :] = jnp.where(low, kt, swap(vt)).astype(BF)
            send_kv[128:256, :] = jnp.where(low, swap(kt), vt).astype(BF)
            qt = qt.astype(BF).astype(F4) * 0.125
            turned = swap(qt)
            send_q[0:64, :] = jnp.where(low64, qt[:64], turned[64:]).astype(BF)
            send_q[64:128, :] = jnp.where(low64, turned[:64], qt[64:]).astype(BF)
        for n in range(4):
            kv_out.send(plane * 4 + n)
            q_out.send(plane * 4 + n)
    kv_out.own()
    q_out.own()
    until(crossed)
    rank_grad_r = rank(r.cot[...], r.up_r[...])
    for i in range(8):
        r.bias_es[0:1, i * 128 : (i + 1) * 128] = r.bias_e[0:1, block(0, i)]

    def to_plane(source, target, name, half, own):
        for j, chip in ((3, l.db), (1, l.xb), (2, l.yb)):
            part = rows_at(source, half * 256 + (0 if own else j * 64), 64)
            l.send(part, rows_at(target, half * 256 + j * 64, 64), sems[name], (half, j), (l.h, chip))

    def from_plane(target, name, half):
        for j in range(1, 4):
            l.arrived(rows_at(target, half * 256 + j * 64, 64), sems[name], (half, j))

    def keep_own(target, at, tile):
        target[0:64, at] = tile[:64]
        target[256:320, at] = tile[64:]

    all_columns, ranks = slice(0, 1024), slice(1024, 1152)
    keep_own(r.cot_all, all_columns, r.cot[...])
    keep_own(r.cot_all, ranks, rank_grad_r)
    l.send(kv_at(l.b, l.h), kv_at(l.b, l.h), sems["f"], 0, (l.o, l.b))
    for k in range(1, CHIPS):
        kv_out.wait(k)
        c = l.behind(k)
        l.send(kv_at(c, l.h), kv_at(c, l.h), sems["f"], k, (l.o, l.b))
        until(min(state[0] + 1, ends[4]))
    until(kicked)
    to_plane(r.cot_all, r.cot_all, "ct", 0, True)
    to_plane(r.cot_all, r.cot_all, "ct", 1, True)
    until(ends[5])
    for k in range(1, CHIPS):
        q_out.wait(k)
    for k in range(CHIPS):
        l.arrived(kv_at(l.behind(k), l.o), sems["f"], k)

    for n in range(CHIPS):
        tile = r.recv_q[n * 64 : n * 64 + 64, :].astype(F4)
        r.q[n * 128 : n * 128 + 64, :] = jnp.where(low64, tile, 0.0).astype(BF)
        r.q[n * 128 + 64 : n * 128 + 128, :] = jnp.where(low64, swap(tile), 0.0).astype(BF)
        tile = r.kv[n * 256 : n * 256 + 256, :].astype(F4)
        r.ones_v[n * 256 : n * 256 + 256, :] = jnp.where(half_mask(256), 1.0, tile).astype(BF)
    a_out = Exchange(l, r.send_a, r.recv_a, 64, sems["a"])
    for i in range(8):
        queries = r.q[i * 256 : (i + 1) * 256, :]

        def fold(jj, total, masked=False):
            at = pl.ds(pl.multiple_of(jj * 512, 512), 512)
            powers = jnp.exp(by_transpose(queries, r.kv[at, :]))
            if masked:
                row = lax.broadcasted_iota(jnp.int32, (256, 512), 0)
                column = lax.broadcasted_iota(jnp.int32, (256, 512), 1)
                powers = jnp.where((row >= 128) | (column < 256), powers, 0.0)
            return total + product(powers.astype(BF), r.ones_v[at, :])

        total = fold(i, jnp.zeros((256, 128), F4), True)
        if i:
            total = lax.fori_loop(0, i, fold, total)
        share = total / swap(total)
        r.attden[i * 256 : (i + 1) * 256, :] = jnp.where(half_mask(256), total, share)
        for n in range(2):
            t = 2 * i + n
            part = share[n * 128 : n * 128 + 128]
            packed = jnp.where(low64, swap(part[64:]), part[:64]).astype(BF)
            r.send_a[t * 64 : t * 64 + 64, :] = packed
            a_out.send(t)
    a_out.own()
    until(ends[6])
    need(4, 4)
    for k in range(1, CHIPS):
        a_out.wait(k)
    for p in range(8):
        one = r.recv_a[p * 128 : p * 128 + 64, :].astype(F4)
        two = r.recv_a[p * 128 + 64 : p * 128 + 128, :].astype(F4)
        at = p * 128
        r.attended[0:64, at : at + 128] = jnp.where(low64, swap(one), two).astype(BF)
        r.attended[64:128, at : at + 128] = jnp.where(low64, one, swap(two)).astype(BF)

    rank_m = rank(r.attended[...], r.down_m[...])
    r.residual[...] = (
        r.hidden[...].astype(F4)
        + product(r.attended[...], r.wm[...])
        + bias_m()
        + product(rank_m, r.up_m[...])
    )
    hat, _ = centre(r.residual[...])
    second_normed = (hat * gain_two() + bias_two()).astype(BF)
    rank_e = rank(second_normed, r.down_e[...])
    keep_own(r.sn_all, all_columns, second_normed)
    keep_own(r.sn_all, ranks, rank_e)
    to_plane(r.sn_all, r.sn_all, "sn", 0, True)
    to_plane(r.sn_all, r.sn_all, "sn", 1, True)

    def tile_at(n, width):
        return pl.ds(pl.multiple_of(n * width, width), width)

    need(5, 6)
    from_plane(r.cot_all, "ct", 0)
    from_plane(r.cot_all, "ct", 1)

    def grad_tile(n, carry):
        at = tile_at(n, 256)
        r.agrad[:, at] = (
            by_transpose(r.cot_all[:, :1024], r.wr[at, :]) + product(r.cot_all[:, 1024:], r.down_rs[:, at])
        ).astype(BF)
        return carry

    lax.fori_loop(0, 4, grad_tile, 0)
    for half in range(2):
        from_plane(r.sn_all, "sn", half)
        these = slice(half * 256, half * 256 + 256)

        def inner_tile(n, carry):
            at = tile_at(n, 256)
            expanded = (
                product(r.sn_all[these, :1024], r.we[:, at])
                + r.bias_es[0:1, at]
                + product(r.sn_all[these, 1024:], r.up_es[:, at])
            )
            value, slope = gelu_parts(expanded)
            r.act[these, at] = value.astype(BF)
            r.agrad[these, at] = (r.agrad[these, at].astype(F4) * slope).astype(BF)
            return carry

        lax.fori_loop(0, 4, inner_tile, 0)

        def normed_tile(n, carry):
            at = tile_at(n, 256)
            r.ng_part[these, at] = by_transpose(r.agrad[these, :], r.we[at, :]).astype(BF)
            return carry

        lax.fori_loop(0, 4, normed_tile, 0)
        r.ng_part[these, 1024:] = by_transpose(r.agrad[these, :], r.up_es[...]).astype(BF)
        to_plane(r.ng_part, r.ng_recv, "ng", half, False)
    def flipped(tile):
        return tile.astype(F4).T.astype(BF)

    def reduce_tile(n, carry):
        at = tile_at(n, 256)
        r.red_part[:, at] = product(r.act[...], r.wr[:, at]).astype(BF)
        return carry

    lax.fori_loop(0, 4, reduce_tile, 0)
    r.red_part[:, 1024:] = by_transpose(r.act[...], r.down_rs[...]).astype(BF)
    rank_e_t, rank_grad_r_t = flipped(r.sn_all[:, 1024:]), flipped(r.cot_all[:, 1024:])
    for n in range(4):
        at = slice(n * 256, (n + 1) * 256)
        for kind, tile in enumerate((product(rank_e_t, r.agrad[:, at]), product(rank_grad_r_t, r.act[:, at]))):
            for m in range(2):
                to = (n * 2 + m) * 256 + kind * 128
                r.gs[:, to : to + 128] = tile[:, m * 128 : (m + 1) * 128].astype(BF)
    sliced = SliceReduce(l, r.gs, r.g, SLICES, (r.slice_c, r.slice_l), sems["slice"]).steps()
    sliced.pop(0)()
    from_plane(r.ng_recv, "ng", 0)
    from_plane(r.ng_recv, "ng", 1)

    def plane_sum(part, received, at):
        halves = []
        for start in (0, 256):
            total = part[start : start + 64, at].astype(F4)
            for j in range(1, 4):
                total = total + received[start + j * 64 : start + j * 64 + 64, at].astype(F4)
            halves.append(total)
        return jnp.concatenate(halves, axis=0)

    rank_grad_e = (r.sel[...] * plane_sum(r.ng_part, r.ng_recv, ranks)).astype(BF)
    normed_grad = plane_sum(r.ng_part, r.ng_recv, all_columns) + product(rank_grad_e, r.down_e[...])
    back_two = norm_back(r.residual[...], gain_two(), normed_grad)
    residual_grad = r.cot[...].astype(F4) + back_two
    mixed_grad = residual_grad.astype(BF)
    rank_grad_m = rank(mixed_grad, r.up_m[...])
    g_out = Exchange(l, r.send_g, r.recv_g, 64, sems["g"])
    for step in range(4):
        plane = lax.rem(l.z + 1 + step, 4)
        at = pl.ds(pl.multiple_of(plane * 256, 256), 256)
        both = by_transpose(mixed_grad, r.wm[at, :]) + product(rank_grad_m, r.down_m[:, at])
        for n in range(2):
            tile = both[:, n * 128 : n * 128 + 128]
            turned = swap(tile)
            send_g = rows_at(r.send_g, (plane * 4 + n * 2) * 64, 128)
            send_g[0:64, :] = jnp.where(low64, tile[64:], turned[:64]).astype(BF)
            send_g[64:128, :] = jnp.where(low64, turned[64:], tile[:64]).astype(BF)
        for n in range(4):
            g_out.send(plane * 4 + n)
    g_out.own()

    to_plane(r.red_part, r.red_recv, "rd", 0, False)
    to_plane(r.red_part, r.red_recv, "rd", 1, False)

    def adapter(at, left, right, width):
        for n in range(width // 512):
            r.gp[:, at + n * 512 : at + (n + 1) * 512] = product(left, right[:, n * 512 : (n + 1) * 512]).astype(BF)

    adapter(MIXER_D, flipped(rank_grad_m), r.attended, 1024)
    adapter(MIXER_U, flipped(rank_m), mixed_grad, 1024)
    adapter(EXPAND_D, flipped(rank_grad_e), second_normed, 1024)
    early = Reduce(l, r.gp, r.g, 0, TRIPLE_D, (r.early_c, r.early_1, r.early_2, r.early_3), sems["early"]).steps()

    def finish_output():
        from_plane(r.red_recv, "rd", 0)
        from_plane(r.red_recv, "rd", 1)
        rank_r = (r.sel[...] * plane_sum(r.red_part, r.red_recv, ranks)).astype(BF)
        reduced = plane_sum(r.red_part, r.red_recv, all_columns)
        r.layer_out[...] = (r.residual[...] + reduced + bias_r() + product(rank_r, r.up_r[...])).astype(BF)
        adapter(REDUCE_U, flipped(rank_r), r.cot, 1024)
        r.residual[...] = residual_grad
        early.pop(0)()

    for n in range(CHIPS):
        tile = r.kv[n * 256 : n * 256 + 256, :].astype(F4)
        wide = half_mask(256)
        r.ones_v[n * 256 : n * 256 + 256, :] = jnp.where(wide, tile, 0.0).astype(BF)
        r.vz[n * 256 : n * 256 + 256, :] = jnp.where(wide, 0.0, tile).astype(BF)
        r.k_t[:, n * 256 : n * 256 + 256] = tile.T[:64, :].astype(BF)
    r.dq_t[...] = jnp.zeros((128, 2048), F4)
    for k in range(1, CHIPS):
        g_out.wait(k)
    for n in range(CHIPS):
        at = n * 128
        g = r.recv_g[n * 64 : n * 64 + 64, :].astype(F4)
        both = r.attden[at : at + 128, :]
        grad = jnp.concatenate([g, swap(g)], axis=0)
        numer = jnp.where(low, 0.0, grad / swap(both))
        numer_low = numer.astype(BF)
        r.dz[at : at + 128, :] = numer_low
        r.qd[at : at + 128, :] = jnp.where(
            low, r.q[at : at + 128, :].astype(F4), numer_low.astype(F4)
        ).astype(BF)
        term = jnp.where(low, 0.0, numer * both)
        row = -jnp.sum(term.T, axis=0, keepdims=True)
        r.ddrow[0:1, at : at + 128] = row.astype(BF).astype(F4)
    dkv_out = Exchange(l, r.send_dkv, r.recv_dkv, 128, sems["dkv"])
    dq_out = Exchange(l, r.send_dq, r.recv_dq, 64, sems["dq"])

    def exchange(jj):
        for n in range(2):
            t = 2 * jj + n
            l.send(rows_at(r.part, t * 256 + l.o * 128, 128), rows_at(r.recv_part, t * 128, 128), sems["e"], t, (l.o, l.b))

    def finish(jj):
        for n in range(2):
            t = 2 * jj + n
            l.arrived(rows_at(r.recv_part, t * 128, 128), sems["e"], t)
            here = r.part[pl.ds(pl.multiple_of(t * 256 + l.h * 128, 128), 128), :]
            r.send_dkv[t * 128 : t * 128 + 128, :] = (here + r.recv_part[t * 128 : t * 128 + 128, :]).astype(BF)
            y = r.dq_t[:, t * 128 : t * 128 + 128].T * 0.125
            r.send_dq[t * 64 : t * 64 + 64, :] = jnp.where(low64, y[:64], swap(y[64:])).astype(BF)
            dkv_out.send(t)
            dq_out.send(t)

    for jj in range(8):
        keys = slice(jj * 512, jj * 512 + 512)

        def fold_back(i, total, masked=False):
            at = tile_at(i, 256)
            both = r.qd[at, :]
            powers = jnp.exp(by_transpose(r.ones_v[keys, :], both))
            if masked:
                row = lax.broadcasted_iota(jnp.int32, (512, 256), 0)
                column = lax.broadcasted_iota(jnp.int32, (512, 256), 1)
                powers = jnp.where((row < 256) | (column >= 128), powers, 0.0)
            prob = by_transpose(r.vz[keys, :], both) + r.ddrow[0:1, at]
            score = (powers * prob).astype(BF)
            r.dq_t[0:64, at] += product(r.k_t[:, keys], score)
            return total + product(score, r.q[at, :]) + product(powers.astype(BF), r.dz[at, :])

        total = fold_back(jj, jnp.zeros((512, 128), F4), True)
        if jj < 7:
            total = lax.fori_loop(jj + 1, 8, fold_back, total)
        r.part[keys, :] = total
        exchange(jj)
        if jj:
            finish(jj - 1)
        if jj == 2:
            finish_output()
        for steps in {0: [sliced], 2: [sliced], 3: [early], 4: [sliced], 5: [early], 7: [early]}.get(jj, []):
            steps.pop(0)()
    finish(7)
    dkv_out.own()
    dq_out.own()
    for k in range(1, CHIPS):
        dkv_out.wait(k)
        dq_out.wait(k)
        if k % 5 == 0:
            early.pop(0)()
    for p in range(8):
        at = p * 128
        one = r.recv_dq[p * 128 : p * 128 + 64, :].astype(F4)
        two = r.recv_dq[p * 128 + 64 : p * 128 + 128, :].astype(F4)
        r.jg[0:64, at : at + 128] = jnp.where(low64, one, swap(two)).astype(BF)
        r.jg[64:128, at : at + 128] = jnp.where(low64, swap(one), two).astype(BF)
        one = r.recv_dkv[p * 256 : p * 256 + 128, :].astype(F4)
        two = r.recv_dkv[p * 256 + 128 : p * 256 + 256, :].astype(F4)
        r.jg[:, 1024 + at : 1152 + at] = jnp.where(low, one, swap(two)).astype(BF)
        r.jg[:, 2048 + at : 2176 + at] = jnp.where(low, swap(one), two).astype(BF)

    rank_grad_t = rank(r.jg[...], r.up_t[...])
    adapter(TRIPLE_D, flipped(rank_grad_t), r.fn, 1024)
    adapter(TRIPLE_U, flipped(r.rank_t[...]), r.jg, 3072)
    late = Reduce(l, r.gp, r.g, TRIPLE_D, SLICES - TRIPLE_D, (r.late_c, r.late_1, r.late_2, r.late_3), sems["late"]).steps()
    late.pop(0)()
    late.pop(0)()

    def triple_tile(n, carry):
        at = tile_at(n, 512)
        return carry + by_transpose(r.jg[:, at], r.wt[:, at])

    normed_grad = lax.fori_loop(0, 6, triple_tile, product(rank_grad_t, r.down_t[...]))
    back_one = norm_back(r.hidden[...].astype(F4), gain_one(), normed_grad)
    r.hidden_grad[...] = (r.residual[...] + back_one).astype(BF)
    while late or early or sliced:
        for rest in (late, early, sliced):
            if rest:
                rest.pop(0)()
    for out in (kv_out, q_out, a_out, g_out, dkv_out, dq_out):
        out.settle()
    l.settle()


def layer(*arrays):
    vmem = pl.BlockSpec(memory_space=pltpu.VMEM)
    hbm = pl.BlockSpec(memory_space=pl.ANY)
    dma = pltpu.SemaphoreType.DMA
    return pl.pallas_call(
        layer_kernel,
        name="layer",
        in_specs=[hbm if name.endswith("_sh") else vmem for name in INPUTS],
        out_shape=[jax.ShapeDtypeStruct(*OUTPUTS[name]) for name in OUTPUTS],
        out_specs=[vmem] * len(OUTPUTS),
        scratch_shapes=[pltpu.VMEM(*SCRATCH[name]) for name in SCRATCH]
        + [dma((5,))]
        + [dma(SEMS[name]) for name in SEMS for _ in range(2)],
        compiler_params=pltpu.CompilerParams(
            collective_id=0, has_side_effects=True, vmem_limit_bytes=LIMIT
        ),
    )(*arrays)


WRITTEN = (1024, 3072, 1024, 1024, 1024, 4096, 4096, 1024)


def write_kernel(layer_in, hidden_in, g, layer_out, hidden_out, td, tu, md, mu, ed, eu, rd, ru, low, high, in_sem, out_sem):
    passed = [
        pltpu.make_async_copy(layer_in, layer_out, out_sem.at[0]),
        pltpu.make_async_copy(hidden_in, hidden_out, out_sem.at[1]),
    ]
    reads = [
        pltpu.make_async_copy(
            g.at[:, n * 2048 : (n + 1) * 2048], low.at[:, n * 2048 : (n + 1) * 2048], in_sem.at[n]
        )
        for n in range(8)
    ]
    for copy in reads + passed:
        copy.start()
    writes = []

    def write(start, width, target, at):
        copy = pltpu.make_async_copy(
            high.at[:, start : start + width], target.at[:, at : at + width], out_sem.at[2 + len(writes)]
        )
        copy.start()
        writes.append(copy)

    whole = (
        (MIXER_D, 1024, md, 0), (MIXER_U, 1024, mu, 0), (EXPAND_D, 1024, ed, 0), (REDUCE_U, 1024, ru, 0),
        (TRIPLE_D, 1024, td, 0), (TRIPLE_U, 1024, tu, 0), (TRIPLE_U + 1024, 2048, tu, 1024),
    )
    done = 0
    for start, width, target, at in whole:
        while done * 2048 < start + width:
            reads[done].wait()
            done += 1
        high[:, start : start + width] = low[:, start : start + width].astype(F4)
        write(start, width, target, at)
    for n in range(done, 8):
        reads[n].wait()
    for h in range(2):
        for kind, target in enumerate((eu, rd)):
            to = SLICES + (h * 2 + kind) * 2048
            for z in range(4):
                for p in range(4):
                    source = SLICES + p * 2048 + h * 1024 + z * 256 + kind * 128
                    here = to + (z * 4 + p) * 128
                    high[:, here : here + 128] = low[:, source : source + 128].astype(F4)
            write(to, 2048, target, h * 2048)
    for copy in passed + writes:
        copy.wait()


def written(layer_out, hidden_grad, g):
    hbm = pl.BlockSpec(memory_space=pl.ANY)
    dma = pltpu.SemaphoreType.DMA
    return pl.pallas_call(
        write_kernel,
        name="written",
        in_specs=[hbm] * 3,
        out_shape=[jax.ShapeDtypeStruct((128, 1024), BF)] * 2 + [jax.ShapeDtypeStruct((128, width), F4) for width in WRITTEN],
        out_specs=[hbm] * 10,
        scratch_shapes=[pltpu.VMEM((128, COLUMNS), BF), pltpu.VMEM((128, COLUMNS), F4), dma((8,)), dma((16,))],
        compiler_params=pltpu.CompilerParams(vmem_limit_bytes=20 * 1024 * 1024),
    )(layer_out, hidden_grad, g)


def small_block(blocks, triple_bias, expand_bias):
    place = lax.rem(shard_of(lax.axis_index("head"), lax.axis_index("blk")), 4)
    lane = jnp.arange(128, dtype=jnp.int32)[None, :]
    six = jnp.where(lane // 32 == place, jnp.tile(jnp.stack(blocks), (1, 4)), 0)
    wide = jnp.arange(384, dtype=jnp.int32)
    three = jnp.where(wide // 96 == place, jnp.tile(triple_bias, 4), 0).reshape(3, 128)
    row = jnp.arange(4, dtype=jnp.int32)[:, None]
    four = jnp.where(row == place, expand_bias[None, :], 0)
    return jnp.concatenate([six, three, four, jnp.zeros((3, 128), BF)], axis=0).astype(BF)


def local_fast(
    hidden, adapter_index, first_gain, first_bias, triple_weight, triple_bias, mixer_weight, mixer_bias,
    second_gain, second_bias, expand_weight, expand_bias, reduce_weight, reduce_bias, triple_down, triple_up,
    mixer_down, mixer_up, expand_down, expand_up, reduce_down, reduce_up, cotangent,
):
    def turned(factor):
        return jnp.transpose(factor, (0, 2, 1)).reshape(ADAPTERS * RANK, factor.shape[1])

    small_sh = small_block(
        [first_gain, first_bias, mixer_bias, second_gain, second_bias, reduce_bias], triple_bias, expand_bias
    )
    layer_out, hidden_grad, g = layer(
        hidden, cotangent, selector(adapter_index), small_sh, triple_weight, mixer_weight, reduce_weight, expand_weight,
        turned(triple_down), flat_up(triple_up), turned(mixer_down), flat_up(mixer_up),
        turned(expand_down), flat_up(expand_up), turned(reduce_down), flat_up(reduce_up),
    )
    layer_out, hidden_grad, *grads = written(layer_out, hidden_grad, g)

    def down_out(part):
        return jnp.transpose(part.reshape(ADAPTERS, RANK, part.shape[1]), (0, 2, 1))

    def up_out(part):
        return part.reshape(ADAPTERS, RANK, part.shape[1])

    shaped = [down_out, up_out, down_out, up_out, down_out, up_out, down_out, up_out]
    return (layer_out, hidden_grad) + tuple(shape(part) for shape, part in zip(shaped, grads))


def solution(mesh):
    placed = (
        P(("blk", "head"), None),
        P(("blk", "head")),
        P(("head", "blk")),
        P(("head", "blk")),
        P(("head", "blk"), None),
        P(("head", "blk")),
        P(("head", "blk"), None),
        P(("head", "blk")),
        P(("head", "blk")),
        P(("head", "blk")),
        P(("head", "blk"), None),
        P(("head", "blk")),
        P(("head", "blk"), None),
        P(("head", "blk")),
        P(),
        P(),
        P(),
        P(),
        P(),
        P(),
        P(),
        P(),
        P(("blk", "head"), None),
    )
    fits = tuple(mesh.shape[name] for name in ("head", "blk")) == (2, CHIPS)
    return jax.shard_map(
        local_fast if fits else local,
        mesh=mesh,
        in_specs=placed,
        out_specs=(
            P(("blk", "head"), None),
            P(("blk", "head"), None),
            P(),
            P(),
            P(),
            P(),
            P(),
            P(),
            P(),
            P(),
        ),
        check_vma=False,
    )
```

```python
import functools
import math
import types

import jax
import jax.numpy as jnp
from jax import lax
from jax.experimental import pallas as pl
from jax.experimental.pallas import tpu as pltpu
from jax.sharding import PartitionSpec as P

WIDTH = 1024
HEADS = 16
HEAD_DIM = 64
RANK = 16
ADAPTERS = 8
BLOCK = 256


EPSILON = 1e-05


def product(left, right):
    return jnp.dot(left, right, preferred_element_type=jnp.float32)


def by_transpose(left, right):
    return lax.dot_general(
        left, right, (((1,), (1,)), ((), ())), preferred_element_type=jnp.float32
    )


def transpose_by(left, right):
    return lax.dot_general(
        left, right, (((0,), (0,)), ((), ())), preferred_element_type=jnp.float32
    )


def layer_norm(stream, scales, offset):
    average = jnp.mean(stream, axis=-1, keepdims=True)
    centred = stream - average
    variance = jnp.mean(centred * centred, axis=-1, keepdims=True)
    return centred * lax.rsqrt(variance + EPSILON) * scales + offset


def selector(adapter_index):
    column = jnp.arange(ADAPTERS * RANK, dtype=jnp.int32) // RANK
    return (adapter_index[:, None] == column[None, :]).astype(jnp.float32)


def flat_down(factor):
    return jnp.transpose(factor, (1, 0, 2)).reshape(factor.shape[1], ADAPTERS * RANK)


def flat_up(factor):
    return factor.reshape(ADAPTERS * RANK, factor.shape[2])


def unflat_down(gradient):
    return jnp.transpose(gradient.reshape(gradient.shape[0], ADAPTERS, RANK), (1, 0, 2))


def unflat_up(gradient):
    return gradient.reshape(ADAPTERS, RANK, gradient.shape[1])


def projected(source, weight, offset, down_flat, up_flat, selection):
    low_rank = (selection * product(source, down_flat)).astype(jnp.bfloat16)
    return (
        product(source, weight) + offset.astype(jnp.float32) + product(low_rank, up_flat),
        low_rank,
    )


def adapter_grads(source, low_rank, out_grad, down_flat, up_flat, selection):
    rank_grad = (selection * by_transpose(out_grad, up_flat)).astype(jnp.bfloat16)
    down_grad = transpose_by(source, rank_grad)
    up_grad = transpose_by(low_rank, out_grad)
    return (down_grad, up_grad, by_transpose(rank_grad, down_flat))


def score_block(queries, keys_block):
    return jnp.einsum("qhd,khd->qhk", queries, keys_block, preferred_element_type=jnp.float32) * (
        1.0 / math.sqrt(HEAD_DIM)
    )


def cut_rows(arrays, trailing):
    length = arrays[0].shape[0]
    block_rows = math.gcd(length, 512)
    repeats = length // block_rows
    shaped = tuple(
        (
            array.reshape((repeats, block_rows) + shape_tail)
            for array, shape_tail in zip(arrays, trailing)
        )
    )
    firsts = jnp.arange(repeats, dtype=jnp.int32) * block_rows
    return (shaped, firsts, block_rows)


def forward_fold(queries, query_places, locate, totals, portion):
    head_count = queries.shape[1]
    query_block = query_places // BLOCK
    last_block = jnp.max(query_block)
    shaped, firsts, block_rows = cut_rows(portion, ((head_count, HEAD_DIM), (head_count, HEAD_DIM)))

    def forward_visiting(carried, packet):
        keys_block, values_block, first_row = packet
        key_places = locate(first_row, block_rows)

        def forward_compute(running):
            numerator, denominator = running
            allowed = (key_places // BLOCK)[None, None, :] <= query_block[:, None, None]
            powers = jnp.where(allowed, jnp.exp(score_block(queries, keys_block)), 0.0)
            numerator = numerator + jnp.einsum(
                "qhk,khd->qhd",
                powers.astype(jnp.bfloat16),
                values_block,
                preferred_element_type=jnp.float32,
            )
            return (numerator, denominator + jnp.sum(powers, axis=-1))

        skipped = jnp.min(key_places) // BLOCK > last_block
        return (lax.cond(skipped, lambda running: running, forward_compute, carried), None)

    return lax.scan(forward_visiting, totals, shaped + (firsts,))[0]


def query_grad_fold(queries, query_places, locate, numer_grad, denom_grad, totals, portion):
    head_count = queries.shape[1]
    query_block = query_places // BLOCK
    last_block = jnp.max(query_block)
    shaped, firsts, block_rows = cut_rows(portion, ((head_count, HEAD_DIM), (head_count, HEAD_DIM)))

    def query_visiting(carried, packet):
        keys_block, values_block, first_row = packet
        key_places = locate(first_row, block_rows)

        def query_compute(running):
            allowed = (key_places // BLOCK)[None, None, :] <= query_block[:, None, None]
            powers = jnp.where(allowed, jnp.exp(score_block(queries, keys_block)), 0.0)
            prob_grad = jnp.einsum(
                "qhd,khd->qhk", numer_grad, values_block, preferred_element_type=jnp.float32
            )
            score_grad = (powers * (prob_grad + denom_grad[:, :, None])).astype(jnp.bfloat16)
            return running + jnp.einsum(
                "qhk,khd->qhd", score_grad, keys_block, preferred_element_type=jnp.float32
            )

        skipped = jnp.min(key_places) // BLOCK > last_block
        return (lax.cond(skipped, lambda running: running, query_compute, carried), None)

    return lax.scan(query_visiting, totals, shaped + (firsts,))[0]


def key_grad_fold(keys_here, values_here, key_places, locate, totals, portion):
    head_count = keys_here.shape[1]
    key_block = key_places // BLOCK
    first_block = jnp.min(key_block)
    shaped, firsts, block_rows = cut_rows(
        portion, ((head_count, HEAD_DIM), (head_count, HEAD_DIM), (head_count,))
    )

    def key_visiting(carried, packet):
        query_rows, numer_rows, denom_rows, first_row = packet
        query_places = locate(first_row, block_rows)

        def key_compute(running):
            keys_grad, values_grad = running
            allowed = key_block[None, None, :] <= (query_places // BLOCK)[:, None, None]
            powers = jnp.where(allowed, jnp.exp(score_block(query_rows, keys_here)), 0.0)
            prob_grad = jnp.einsum(
                "qhd,khd->qhk", numer_rows, values_here, preferred_element_type=jnp.float32
            )
            score_grad = (powers * (prob_grad + denom_rows.astype(jnp.float32)[:, :, None])).astype(
                jnp.bfloat16
            )
            keys_grad = keys_grad + jnp.einsum(
                "qhk,qhd->khd", score_grad, query_rows, preferred_element_type=jnp.float32
            )
            values_grad = values_grad + jnp.einsum(
                "qhk,qhd->khd",
                powers.astype(jnp.bfloat16),
                numer_rows,
                preferred_element_type=jnp.float32,
            )
            return (keys_grad, values_grad)

        skipped = jnp.max(query_places) // BLOCK < first_block
        return (lax.cond(skipped, lambda running: running, key_compute, carried), None)

    return lax.scan(key_visiting, totals, shaped + (firsts,))[0]


def local(
    hidden,
    adapter_index,
    first_gain,
    first_bias,
    triple_weight,
    triple_bias,
    mixer_weight,
    mixer_bias,
    second_gain,
    second_bias,
    expand_weight,
    expand_bias,
    reduce_weight,
    reduce_bias,
    triple_down,
    triple_up,
    mixer_down,
    mixer_up,
    expand_down,
    expand_up,
    reduce_down,
    reduce_up,
    cotangent,
):
    gathered = (
        lax.all_gather(first_gain, ("head", "blk"), axis=0, tiled=True),
        lax.all_gather(first_bias, ("head", "blk"), axis=0, tiled=True),
        lax.all_gather(triple_weight, ("head", "blk"), axis=0, tiled=True),
        lax.all_gather(triple_bias, ("head", "blk"), axis=0, tiled=True),
        lax.all_gather(mixer_weight, ("head", "blk"), axis=0, tiled=True),
        lax.all_gather(mixer_bias, ("head", "blk"), axis=0, tiled=True),
        lax.all_gather(second_gain, ("head", "blk"), axis=0, tiled=True),
        lax.all_gather(second_bias, ("head", "blk"), axis=0, tiled=True),
        lax.all_gather(expand_weight, ("head", "blk"), axis=0, tiled=True),
        lax.all_gather(expand_bias, ("head", "blk"), axis=0, tiled=True),
        lax.all_gather(reduce_weight, ("head", "blk"), axis=0, tiled=True),
        lax.all_gather(reduce_bias, ("head", "blk"), axis=0, tiled=True),
    )
    (
        gain_one,
        bias_one,
        weight_triple,
        bias_triple,
        weight_mixer,
        bias_mixer,
        gain_two,
        bias_two,
        weight_expand,
        bias_expand,
        weight_reduce,
        bias_reduce,
    ) = gathered
    token_count = hidden.shape[0]
    head_ways = lax.axis_size("head")
    cycle_ways = lax.axis_size("blk")
    selection = selector(adapter_index)
    down_triple = flat_down(triple_down)
    upward_triple = flat_up(triple_up)
    down_mixer = flat_down(mixer_down)
    upward_mixer = flat_up(mixer_up)
    down_expand = flat_down(expand_down)
    upward_expand = flat_up(expand_up)
    down_reduce = flat_down(reduce_down)
    upward_reduce = flat_up(reduce_up)
    stream = hidden.astype(jnp.float32)

    def first_norm(values_in):
        return layer_norm(values_in, gain_one.astype(jnp.float32), bias_one.astype(jnp.float32))

    def second_norm(values_in):
        return layer_norm(values_in, gain_two.astype(jnp.float32), bias_two.astype(jnp.float32))

    first_normed = first_norm(stream).astype(jnp.bfloat16)
    joint, rank_triple = projected(
        first_normed, weight_triple, bias_triple, down_triple, upward_triple, selection
    )
    joint = joint.astype(jnp.bfloat16)
    parts = joint.reshape(token_count, 3, HEADS, HEAD_DIM)
    own_shard = lax.axis_index("blk") * head_ways + lax.axis_index("head")
    query_places = own_shard * token_count + jnp.arange(token_count, dtype=jnp.int32)

    def locate(first_row, length):
        rows_here = first_row + jnp.arange(length, dtype=jnp.int32)
        shard_index = rows_here // token_count
        return (
            shard_index % cycle_ways * head_ways + shard_index // cycle_ways
        ) * token_count + rows_here % token_count

    queries = parts[:, 0]
    keys_here = parts[:, 1]
    values_here = parts[:, 2]
    head_count = queries.shape[1]
    flat_keys = keys_here.reshape(token_count, head_count * HEAD_DIM)
    flat_values = values_here.reshape(token_count, head_count * HEAD_DIM)
    zeros_rows = jnp.zeros((token_count, head_count, HEAD_DIM), jnp.float32)
    payload = (flat_keys, flat_values)
    numerator, denominator = forward_fold(
        queries,
        query_places,
        locate,
        (zeros_rows, jnp.zeros((token_count, head_count), jnp.float32)),
        (
            lax.all_gather(payload[0], ("head", "blk"), axis=0, tiled=True),
            lax.all_gather(payload[1], ("head", "blk"), axis=0, tiled=True),
        ),
    )
    attended = numerator / denominator[:, :, None]
    attended_low = attended.astype(jnp.bfloat16).reshape(token_count, WIDTH)
    mixed, rank_mixer = projected(
        attended_low, weight_mixer, bias_mixer, down_mixer, upward_mixer, selection
    )
    residual = stream + mixed
    second_normed = second_norm(residual).astype(jnp.bfloat16)
    expanded, rank_expand = projected(
        second_normed, weight_expand, bias_expand, down_expand, upward_expand, selection
    )
    activated = jax.nn.gelu(expanded, approximate=True).astype(jnp.bfloat16)
    reduced, rank_reduce = projected(
        activated, weight_reduce, bias_reduce, down_reduce, upward_reduce, selection
    )
    layer_out = (residual + reduced).astype(jnp.bfloat16)
    reduce_down_grad, reduce_up_grad, through_reduce = adapter_grads(
        activated, rank_reduce, cotangent, down_reduce, upward_reduce, selection
    )
    activated_grad = (by_transpose(cotangent, weight_reduce) + through_reduce).astype(jnp.bfloat16)
    gelu_back = jax.vjp(lambda values_in: jax.nn.gelu(values_in, approximate=True), expanded)[1]
    expanded_grad = gelu_back(activated_grad.astype(jnp.float32))[0].astype(jnp.bfloat16)
    expand_down_grad, expand_up_grad, through_expand = adapter_grads(
        second_normed, rank_expand, expanded_grad, down_expand, upward_expand, selection
    )
    normed_grad = by_transpose(expanded_grad, weight_expand) + through_expand
    second_back = jax.vjp(second_norm, residual)[1]
    residual_grad = cotangent.astype(jnp.float32) + second_back(normed_grad)[0]
    mixed_grad = residual_grad.astype(jnp.bfloat16)
    mixer_down_grad, mixer_up_grad, through_mixer = adapter_grads(
        attended_low, rank_mixer, mixed_grad, down_mixer, upward_mixer, selection
    )
    attended_grad = (by_transpose(mixed_grad, weight_mixer) + through_mixer).astype(jnp.bfloat16)
    output_grad = attended_grad.reshape(token_count, HEADS, HEAD_DIM).astype(jnp.float32)
    numer_grad = (output_grad / denominator[:, :, None]).astype(jnp.bfloat16)
    denom_grad = (-jnp.sum(output_grad * attended, axis=-1) / denominator).astype(jnp.bfloat16)
    payload = (flat_keys, flat_values)
    query_grad = query_grad_fold(
        queries,
        query_places,
        locate,
        numer_grad,
        denom_grad.astype(jnp.float32),
        zeros_rows,
        (
            lax.all_gather(payload[0], ("head", "blk"), axis=0, tiled=True),
            lax.all_gather(payload[1], ("head", "blk"), axis=0, tiled=True),
        ),
    )
    payload = (
        queries.reshape(token_count, head_count * HEAD_DIM),
        numer_grad.reshape(token_count, head_count * HEAD_DIM),
        denom_grad,
    )
    keys_grad, values_grad = key_grad_fold(
        keys_here,
        values_here,
        query_places,
        locate,
        (zeros_rows, zeros_rows),
        (
            lax.all_gather(payload[0], ("head", "blk"), axis=0, tiled=True),
            lax.all_gather(payload[1], ("head", "blk"), axis=0, tiled=True),
            lax.all_gather(payload[2], ("head", "blk"), axis=0, tiled=True),
        ),
    )
    factor = 1.0 / math.sqrt(HEAD_DIM)
    joint_grad = jnp.stack([query_grad * factor, keys_grad * factor, values_grad], axis=1).astype(
        jnp.bfloat16
    )
    joint_tokens = joint_grad.reshape(token_count, 3 * WIDTH)
    triple_down_grad, triple_up_grad, through_triple = adapter_grads(
        first_normed, rank_triple, joint_tokens, down_triple, upward_triple, selection
    )
    normed_one_grad = by_transpose(joint_tokens, weight_triple) + through_triple
    first_back = jax.vjp(first_norm, stream)[1]
    hidden_grad = (residual_grad + first_back(normed_one_grad)[0]).astype(jnp.bfloat16)
    summed = lax.psum(
        (
            triple_down_grad,
            triple_up_grad,
            mixer_down_grad,
            mixer_up_grad,
            expand_down_grad,
            expand_up_grad,
            reduce_down_grad,
            reduce_up_grad,
        ),
        ("head", "blk"),
    )
    return (
        layer_out,
        hidden_grad,
        unflat_down(summed[0]),
        unflat_up(summed[1]),
        unflat_down(summed[2]),
        unflat_up(summed[3]),
        unflat_down(summed[4]),
        unflat_up(summed[5]),
        unflat_down(summed[6]),
        unflat_up(summed[7]),
    )


MESH = pl.DeviceIdType.MESH
CHIPS = 16
LIMIT = 62 * 1024 * 1024 - 512 * 1024
BF = jnp.bfloat16
F4 = jnp.float32


ALONG = ((0, 1, 2, 3), (1, 0, 2, 3), (2, 1, 3, 0), (3, 2, 1, 0))


class Links:
    def __init__(self):
        self.h = lax.axis_index("head")
        self.b = lax.axis_index("blk")
        self.o = 1 - self.h
        self.sent = []
        self.x = lax.rem(self.b, 2)
        self.y = lax.rem(self.b // 2, 2)
        self.z = self.b // 4
        self.xb = self.b + 1 - 2 * self.x
        self.yb = self.b + 2 - 4 * self.y
        self.db = self.xb + 2 - 4 * self.y
        self.columns = [lax.rem(chip, 4) for chip in (self.b, self.xb, self.yb, self.db)]

    def nth(self, n):
        return sum(jnp.where(self.z == z, table[n], 0) for z, table in enumerate(ALONG))

    def at_line(self, z):
        return lax.rem(self.b, 4) + 4 * z

    def along(self, piece, sems, index):
        for k, wanted in ((1, self.z < 3), (3, self.z > 0), (2, None)):
            where = (piece, piece, sems, index + (self.z,), (self.h, self.ahead(4 * k)))
            if wanted is None:
                self.send(*where)
            else:
                self.send_if(wanted, *where)

    def pass_on(self, piece, z, sems, index):
        wanted = (self.z == 2) & (z == 0) | (self.z == 1) & (z == 3)
        chip = self.columns[0] + 4 * (3 - z)
        self.send_if(wanted, piece, piece, sems, index + (z,), (self.h, chip))

    def ahead(self, k):
        return lax.rem(self.b + k, CHIPS)

    def behind(self, k):
        return lax.rem(self.b + CHIPS - k, CHIPS)

    def greet(self):
        barrier = pltpu.get_barrier_semaphore()
        for k in range(1, CHIPS):
            pl.semaphore_signal(
                barrier, 1, device_id=(self.h, self.ahead(k)), device_id_type=MESH
            )
        pl.semaphore_signal(barrier, 1, device_id=(self.o, self.b), device_id_type=MESH)

    def met(self):
        pl.semaphore_wait(pltpu.get_barrier_semaphore(), CHIPS)

    def copy(self, source, target, sems, at, device):
        return pltpu.make_async_remote_copy(
            src_ref=source,
            dst_ref=target,
            send_sem=sems[0].at[at],
            recv_sem=sems[1].at[at],
            device_id=device,
            device_id_type=MESH,
        )

    def send(self, source, target, sems, at, device):
        copy = self.copy(source, target, sems, at, device)
        copy.start()
        self.sent.append((None, copy))

    def send_if(self, wanted, *where):
        copy = self.copy(*where)
        pl.when(wanted)(copy.start)
        self.sent.append((wanted, copy))

    def arrived(self, target, sems, at):
        self.copy(target, target, sems, at, (self.o, self.b)).wait_recv()

    def settle(self):
        for wanted, copy in self.sent:
            if wanted is None:
                copy.wait_send()
            else:
                pl.when(wanted)(copy.wait_send)
        self.sent = []


class Exchange:
    def __init__(self, links, source, target, rows, sems, slot=None):
        self.links, self.source, self.target = links, source, target
        self.rows, self.sems = rows, sems
        self.slot = slot or (lambda chip: rows_at(target, chip * rows, rows))

    def send(self, t):
        l = self.links

        @pl.when(l.b != t)
        def _():
            l.copy(
                rows_at(self.source, t * self.rows, self.rows),
                self.slot(l.b), self.sems, lax.rem(t + CHIPS - l.b, CHIPS), (l.h, t),
            ).start()

    def own(self):
        l = self.links
        copy = pltpu.make_async_copy(
            rows_at(self.source, l.b * self.rows, self.rows), self.slot(l.b), self.sems[0].at[0]
        )
        copy.start()
        copy.wait()

    def wait(self, k):
        self.links.arrived(self.slot(self.links.behind(k)), self.sems, k)

    def settle(self):
        for k in range(1, CHIPS):
            l = self.links
            part = rows_at(self.source, l.ahead(k) * self.rows, self.rows)
            l.copy(part, part, self.sems, k, (l.h, l.ahead(k))).wait_send()


def half_mask(rows):
    return lax.broadcasted_iota(jnp.int32, (rows, 128), 1) < 64


def swap(tile):
    return pltpu.roll(tile, 64, 1)


def rows_at(ref, start, count):
    return ref.at[pl.ds(pl.multiple_of(start, 16), count), :]


class Gather:
    def __init__(self, links, number, slot, sems):
        self.links, self.p, self.slot = links, number, slot
        self.sems = sems

    def send(self, axis, n, chip, device):
        piece = self.slot(self.links.h, chip)
        self.links.send(piece, piece, self.sems[axis], (self.p, n), device)

    def chip(self, side, n):
        return side + 4 * self.links.nth(n)

    def own(self, n):
        l = self.links
        chip = self.chip(l.columns[0], n)
        if n:
            l.pass_on(self.slot(l.h, chip), l.nth(n), self.sems["z"], (self.p,))
        else:
            l.along(self.slot(l.h, chip), self.sems["z"], (self.p,))
        self.send("x", n, chip, (l.h, l.xb))
        self.send("y", n, chip, (l.h, l.yb))
        self.send("c", n, chip, (l.o, l.b))

    def from_line(self, n):
        l = self.links
        chip = self.chip(l.columns[0], n)
        l.arrived(self.slot(l.h, chip), self.sems["z"], (self.p, l.nth(n)))
        self.own(n)

    def arrived(self, axis, n, chip):
        self.links.arrived(self.slot(self.links.h, chip), self.sems[axis], (self.p, n))

    def from_side(self, axis, n):
        l = self.links
        chip = self.chip(l.columns[1 if axis == "x" else 2], n)
        self.arrived(axis, n, chip)
        if (n % 2 == 0) == (axis == "x"):
            self.send("d", n, chip, (l.h, l.yb if axis == "x" else l.xb))
        self.send("c", (4 if axis == "x" else 8) + n, chip, (l.o, l.b))

    def from_corner(self, n):
        l = self.links
        chip = self.chip(l.columns[3], n)
        self.arrived("d", n, chip)
        self.send("c", 12 + n, chip, (l.o, l.b))

    def stages(self):
        part = functools.partial
        return [
            [part(self.own, 0)],
            [part(self.from_line, 1), part(self.from_side, "x", 0), part(self.from_side, "y", 0), part(self.from_line, 2)],
            [part(self.from_side, axis, 1) for axis in "xy"]
            + [part(self.from_line, 3)]
            + [part(self.from_side, axis, n) for n in (2, 3) for axis in "xy"],
            [part(self.from_corner, n) for n in range(4)],
        ]

    def whole(self):
        l = self.links
        for number in range(16):
            chip = self.chip(l.columns[number // 4], number % 4)
            l.arrived(self.slot(l.o, chip), self.sems["c"], (self.p, number))


class RowSlice:
    def __init__(self, links, ref, sems):
        self.links, self.ref = links, ref
        self.line_sems, self.core_sems = sems

    def slot(self, h, z):
        return rows_at(self.ref, (h * 4 + z) * 128, 128)

    def core(self, k, z):
        l = self.links
        l.send(self.slot(l.h, z), self.slot(l.h, z), self.core_sems, k, (l.o, l.b))

    def own(self, n):
        l = self.links
        z = l.nth(n)
        if n:
            l.pass_on(self.slot(l.h, z), z, self.line_sems, ())
        else:
            l.along(self.slot(l.h, z), self.line_sems, ())
        self.core(n, z)

    def from_line(self, n):
        l = self.links
        z = l.nth(n)
        l.arrived(self.slot(l.h, z), self.line_sems, (z,))
        self.own(n)

    def stages(self):
        part = functools.partial
        return [[part(self.own, 0)], [part(self.from_line, 1)], [part(self.from_line, 2)], [part(self.from_line, 3)]]

    def whole(self):
        l = self.links
        for n in range(4):
            l.arrived(self.slot(l.o, l.nth(n)), self.core_sems, n)


class ColumnSlice:
    def __init__(self, links, ref, stage, sems):
        self.links, self.ref, self.stage = links, ref, stage
        self.plane_sems, self.line_sems, self.core_sems = sems

    def chip(self, j, n):
        return self.links.columns[j] + 4 * self.links.nth(n)

    def slot(self, h, chip):
        return rows_at(self.ref, shard_of(h, chip) * 32, 32)

    def own(self, j, n):
        l = self.links
        piece = self.slot(l.h, self.chip(j, n))
        if n:
            l.pass_on(piece, l.nth(n), self.line_sems, (j,))
        else:
            l.along(piece, self.line_sems, (j,))
        l.send(piece, piece, self.core_sems, (j, n), (l.o, l.b))

    def start(self):
        l = self.links
        for j, chip in enumerate((l.b, l.xb, l.yb, l.db)):
            if j:
                l.send(rows_at(self.stage, j * 32, 32), self.slot(l.h, l.b), self.plane_sems, j, (l.h, chip))

    def from_plane(self, j):
        self.links.arrived(self.slot(self.links.h, self.chip(j, 0)), self.plane_sems, j)
        self.own(j, 0)

    def from_line(self, j, n):
        l = self.links
        l.arrived(self.slot(l.h, self.chip(j, n)), self.line_sems, (j, l.nth(n)))
        self.own(j, n)

    def stages(self):
        part = functools.partial
        return [
            [self.start],
            [part(self.own, 0, 0)] + [part(self.from_plane, j) for j in range(1, 4)],
            [part(self.from_line, j, n) for n in range(1, 4) for j in range(4)],
        ]

    def whole(self):
        l = self.links
        for j in range(4):
            for n in range(4):
                l.arrived(self.slot(l.o, self.chip(j, n)), self.core_sems, (j, n))


def ordered(stages, lag):
    events = []
    deepest = max(len(stage) for stage in stages)
    for tick in range(len(stages) * lag + deepest):
        for n, stage in enumerate(stages):
            if 0 <= tick - n * lag < len(stage):
                events += stage[tick - n * lag]
    return events


class Reduce:
    def __init__(self, links, g, out, base, width, bufs, sems, rows=slice(0, 128)):
        self.l, self.g, self.out, self.base, self.sems = links, g, out, base, sems
        self.by_core, self.by_side, self.by_turn, self.by_line = bufs
        self.half, self.p, self.rows = width // 2, width // 4, rows
        l = links
        self.mine = base + l.h * self.half
        p = self.p
        self.keep1 = (self.mine + l.x * (p // 2), self.mine + p + l.y * (p // 2))
        self.give1 = (self.mine + (1 - l.x) * (p // 2), self.mine + p + (1 - l.y) * (p // 2))
        self.keep2 = (self.keep1[0] + l.y * (p // 4), self.keep1[1] + l.x * (p // 4))
        self.give2 = (self.keep1[0] + (1 - l.y) * (p // 4), self.keep1[1] + (1 - l.x) * (p // 4))

    def at(self, start, width):
        return self.g.at[self.rows, pl.ds(pl.multiple_of(start, 128), width)]

    def out_at(self, start, width):
        return self.out.at[self.rows, pl.ds(pl.multiple_of(start, 128), width)]

    def chunk(self, z):
        first, second = self.keep2
        return first * (1 - z // 2) + second * (z // 2) + lax.rem(z, 2) * (self.p // 8)

    def add(self, start, width, others, final=False):
        tile = 384 if width % 384 == 0 else 128
        for n in range(width // tile):
            here = pl.ds(pl.multiple_of(start + n * tile, 128), tile)
            total = self.g[self.rows, here].astype(F4)
            for other in others:
                total = total + other[:, n * tile : (n + 1) * tile].astype(F4)
            (self.out if final else self.g)[self.rows, here] = total.astype(BF)

    def steps(self):
        l, p = self.l, self.p
        sides, turns = (l.xb, l.yb), (l.yb, l.xb)

        def cores():
            away = self.base + l.o * self.half
            l.send(self.at(away, self.half), self.by_core, self.sems, 0, (l.o, l.b))

        def side():
            l.arrived(self.by_core, self.sems, 0)
            for n in range(2):
                self.add(self.give1[n], p // 2, [self.by_core.at[:, pl.ds(pl.multiple_of(self.give1[n] - self.mine, 128), p // 2)]])
                l.send(self.at(self.give1[n], p // 2), self.by_side.at[n], self.sems, 1 + n, (l.h, sides[n]))
            for n in range(2):
                self.add(self.keep1[n], p // 2, [self.by_core.at[:, pl.ds(pl.multiple_of(self.keep1[n] - self.mine, 128), p // 2)]])

        def turn():
            for n in range(2):
                l.arrived(self.by_side.at[n], self.sems, 1 + n)
                self.add(self.keep1[n], p // 2, [self.by_side.at[n]])
                l.send(self.at(self.give2[n], p // 4), self.by_turn.at[n], self.sems, 3 + n, (l.h, turns[n]))

        def line():
            for n in range(2):
                l.arrived(self.by_turn.at[n], self.sems, 3 + n)
                self.add(self.keep2[n], p // 4, [self.by_turn.at[n]])
            for k in range(1, 4):
                away = self.chunk(lax.rem(l.z + k, 4))
                l.send(self.at(away, p // 8), self.by_line.at[k - 1], self.sems, 4 + k, (l.h, l.ahead(4 * k)))

        def line_back():
            for k in range(1, 4):
                l.arrived(self.by_line.at[k - 1], self.sems, 4 + k)
            self.add(self.chunk(l.z), p // 8, [self.by_line.at[k] for k in range(3)], True)
            here = self.out_at(self.chunk(l.z), p // 8)
            for k in range(1, 4):
                l.send(here, here, self.sems, 7 + k, (l.h, l.ahead(4 * k)))

        def turn_back():
            for k in range(1, 4):
                l.arrived(self.out_at(self.chunk(lax.rem(l.z + 4 - k, 4)), p // 8), self.sems, 7 + k)
            for n in range(2):
                here = self.out_at(self.keep2[n], p // 4)
                l.send(here, here, self.sems, 11 + n, (l.h, turns[n]))

        def side_back():
            for n in range(2):
                l.arrived(self.out_at(self.give2[n], p // 4), self.sems, 11 + n)
                here = self.out_at(self.keep1[n], p // 2)
                l.send(here, here, self.sems, 13 + n, (l.h, sides[n]))

        def cores_back():
            for n in range(2):
                l.arrived(self.out_at(self.give1[n], p // 2), self.sems, 13 + n)
            here = self.out_at(self.mine, self.half)
            l.send(here, here, self.sems, 15, (l.o, l.b))

        def done():
            l.arrived(self.out_at(self.base + l.o * self.half, self.half), self.sems, 15)

        return [cores, side, turn, line, line_back, turn_back, side_back, cores_back, done]


class SliceReduce:
    def __init__(self, links, g, out, base, bufs, sems):
        self.l, self.g, self.out, self.base, self.sems = links, g, out, base, sems
        self.by_core, self.by_line = bufs

    def at(self, ref, start, width):
        return ref.at[:, pl.ds(pl.multiple_of(start, 128), width)]

    def steps(self):
        l = self.l
        chips = (l.b, l.xb, l.yb, l.db)
        places = [
            self.base + 2048 * (lax.rem(chip, 4)) for chip in chips
        ]

        def region(j, h, z=None):
            if z is None:
                return self.at(self.out, places[j] + h * 1024, 1024)
            return self.at(self.out, places[j] + h * 1024 + z * 256, 256)

        def cores():
            l.send(self.at(self.g, l.o * 1024, 1024), self.by_core, self.sems, 0, (l.o, l.b))

        def line():
            l.arrived(self.by_core, self.sems, 0)
            for n in range(4):
                here = pl.ds(pl.multiple_of(l.h * 1024 + n * 256, 128), 256)
                total = self.g[:, here].astype(F4) + self.by_core[:, n * 256 : (n + 1) * 256].astype(F4)
                self.g[:, here] = total.astype(BF)
            for k in range(1, 4):
                z = lax.rem(l.z + k, 4)
                l.send(self.at(self.g, l.h * 1024 + z * 256, 256), self.by_line.at[k - 1], self.sems, k, (l.h, l.ahead(4 * k)))

        def line_back():
            total = self.g[:, pl.ds(pl.multiple_of(l.h * 1024 + l.z * 256, 128), 256)].astype(F4)
            for k in range(1, 4):
                l.arrived(self.by_line.at[k - 1], self.sems, k)
                total = total + self.by_line[k - 1].astype(F4)
            self.out[:, pl.ds(pl.multiple_of(places[0] + l.h * 1024 + l.z * 256, 128), 256)] = total.astype(BF)
            for k in range(1, 4):
                l.send(region(0, l.h, l.z), region(0, l.h, l.z), self.sems, 3 + k, (l.h, l.ahead(4 * k)))

        def plane():
            for k in range(1, 4):
                l.arrived(region(0, l.h, lax.rem(l.z + 4 - k, 4)), self.sems, 3 + k)
            for j in range(1, 4):
                l.send(region(0, l.h), region(0, l.h), self.sems, 6 + j, (l.h, chips[j]))
            l.send(region(0, l.h), region(0, l.h), self.sems, 10, (l.o, l.b))

        def cores_back():
            for j in range(1, 4):
                l.arrived(region(j, l.h), self.sems, 6 + j)
                l.send(region(j, l.h), region(j, l.h), self.sems, 10 + j, (l.o, l.b))

        def done():
            for j in range(4):
                l.arrived(region(j, l.o), self.sems, 10 + j)

        return [cores, line, line_back, plane, cores_back, done]


def shard_of(h, chip):
    return h * CHIPS + chip


def centre(stream):
    average = jnp.mean(stream, axis=-1, keepdims=True)
    centred = stream - average
    variance = jnp.mean(centred * centred, axis=-1, keepdims=True)
    scale = lax.rsqrt(variance + EPSILON)
    return centred * scale, scale


def norm_back(stream, gain, grad):
    hat, scale = centre(stream)
    q = grad * gain
    return scale * (
        q - jnp.mean(q, axis=-1, keepdims=True) - hat * jnp.mean(q * hat, axis=-1, keepdims=True)
    )


def gelu_parts(u):
    cubic = 0.044715 * u * u
    slope = math.sqrt(2.0 / math.pi)
    t = jnp.tanh(slope * u * (1.0 + cubic))
    grown = 0.5 * (1.0 + t)
    return u * grown, grown + 0.5 * u * (1.0 - t * t) * slope * (1.0 + 3.0 * cubic)


PIECES = 5
MIXER_D, MIXER_U, EXPAND_D, REDUCE_U, TRIPLE_D, TRIPLE_U, SLICES, COLUMNS = (
    0, 1024, 2048, 3072, 4096, 5120, 8192, 16384,
)

INPUTS = (
    "hidden", "cot", "sel", "small_sh", "triple_sh", "mixer_sh", "reduce_sh", "expand_sh",
    "down_t", "up_t", "down_m", "up_m", "down_e", "up_e", "down_r", "up_r",
)
OUTPUTS = {"layer_out": ((128, 1024), BF), "hidden_grad": ((128, 1024), BF), "g": ((128, COLUMNS), BF)}
SCRATCH = {
    "wt": ((1024, 3072), BF), "wm": ((1024, 1024), BF), "wr": ((1024, 1024), BF), "we": ((1024, 1024), BF),
    "e_in": ((32, 4096), BF), "e_stage": ((128, 1024), BF), "up_es": ((128, 1024), BF), "down_rs": ((128, 1024), BF), "bias_es": ((1, 1024), F4),
    "small": ((512, 128), BF), "vecs": ((16, 1024), F4), "bias_t": ((1, 3072), F4), "bias_e": ((1, 4096), F4),
    "fn": ((128, 1024), BF), "rank_t": ((128, 128), BF), "kv": ((4096, 128), BF), "q": ((2048, 128), BF),
    "attden": ((2048, 128), F4), "attended": ((128, 1024), BF), "ones_v": ((4096, 128), BF),
    "send_kv": ((2048, 128), BF), "send_q": ((1024, 128), BF), "recv_q": ((1024, 128), BF),
    "send_a": ((1024, 128), BF), "recv_a": ((1024, 128), BF),
    "residual": ((128, 1024), F4), "sn_all": ((512, 1152), BF), "cot_all": ((512, 1152), BF),
    "act": ((512, 1024), BF), "agrad": ((512, 1024), BF), "ng_part": ((512, 1152), BF), "ng_recv": ((512, 1152), BF),
    "red_part": ((512, 1152), BF), "red_recv": ((512, 1152), BF),
    "send_g": ((1024, 128), BF), "recv_g": ((1024, 128), BF),
    "qd": ((2048, 128), BF), "dz": ((2048, 128), BF), "vz": ((4096, 128), BF),
    "k_t": ((64, 4096), BF), "ddrow": ((1, 2048), F4), "dq_t": ((128, 2048), F4), "part": ((4096, 128), F4),
    "recv_part": ((2048, 128), F4), "send_dkv": ((2048, 128), BF), "send_dq": ((1024, 128), BF),
    "recv_dkv": ((2048, 128), BF), "recv_dq": ((1024, 128), BF), "jg": ((128, 3072), BF),
"gp": ((128, SLICES), BF), "gs": ((128, 2048), BF), "slice_c": ((128, 1024), BF), "slice_l": ((3, 128, 256), BF),
    "early_c": ((128, 2048), BF), "early_1": ((2, 128, 512), BF), "early_2": ((2, 128, 256), BF), "early_3": ((3, 128, 128), BF),
    "late_c": ((2, 64, 2048), BF), "late_1": ((2, 2, 64, 512), BF), "late_2": ((2, 2, 64, 256), BF), "late_3": ((2, 3, 64, 128), BF),
}
SEMS = {
    "z": (PIECES, 4), "x": (PIECES, 4), "y": (PIECES, 4), "d": (PIECES, 4), "c": (PIECES, 16),
    "kv": (16,), "q": (16,), "f": (16,), "a": (16,), "g": (16,), "e": (16,), "dkv": (16,), "dq": (16,),
    "early": (16,), "late": (16,), "late_two": (16,), "slice": (16,),
    "rz": (4,), "rc": (4,), "ep": (4,), "ez": (4, 4), "ec": (4, 4), "ct": (2, 4), "sn": (2, 4), "ng": (2, 4), "rd": (2, 4),
}


def layer_kernel(*refs):
    names = list(INPUTS) + list(OUTPUTS) + list(SCRATCH)
    r = types.SimpleNamespace(**dict(zip(names, refs)))
    rest = refs[len(names) :]
    local_sem = rest[0]
    sems = {name: (rest[1 + 2 * n], rest[2 + 2 * n]) for n, name in enumerate(SEMS)}
    l = Links()
    low, low64 = half_mask(128), half_mask(64)
    mine = shard_of(l.h, l.b)
    local_copies = [
        pltpu.make_async_copy(r.small_sh, rows_at(r.small, mine * 16, 16), local_sem.at[0]),
        pltpu.make_async_copy(r.triple_sh, rows_at(r.wt, mine * 32, 32), local_sem.at[1]),
        pltpu.make_async_copy(r.mixer_sh, rows_at(r.wm, mine * 32, 32), local_sem.at[2]),
        pltpu.make_async_copy(r.reduce_sh, rows_at(r.wr, (l.h * 4 + l.z) * 128, 128), local_sem.at[3]),
        pltpu.make_async_copy(r.expand_sh, r.e_in, local_sem.at[4]),
    ]
    for copy in local_copies:
        copy.start()
    l.greet()

    def columns(ref, at):
        return lambda h, chip: ref.at[
            pl.ds(pl.multiple_of(shard_of(h, chip) * 32, 32), 32), at : at + 1024
        ]

    slots = [lambda h, chip: rows_at(r.small, shard_of(h, chip) * 16, 16)]
    slots += [columns(r.wt, m * 1024) for m in range(3)]
    slots += [columns(r.wm, 0)]
    pieces = [Gather(l, n, slot, sems) for n, slot in enumerate(slots)]
    pieces.append(RowSlice(l, r.wr, (sems["rz"], sems["rc"])))
    pieces.append(ColumnSlice(l, r.we, r.e_stage, (sems["ep"], sems["ez"], sems["ec"])))
    places = [lax.rem(chip, 4) for chip in (l.b, l.xb, l.yb, l.db)]

    def block(j, i):
        return pl.ds(pl.multiple_of((i // 4 * 16 + places[j] + i % 4 * 4) * 128, 128), 128)

    for i in range(8):
        here = slice(i * 128, (i + 1) * 128)
        r.up_es[:, here] = r.up_e[:, block(0, i)]
        r.down_rs[:, here] = r.down_r[:, block(0, i)]
    for copy in local_copies:
        copy.wait()
    for i in range(8):
        here = slice(i * 128, (i + 1) * 128)
        r.we[pl.ds(pl.multiple_of(mine * 32, 32), 32), here] = r.e_in[:, block(0, i)]
        for j in range(1, 4):
            r.e_stage[j * 32 : (j + 1) * 32, here] = r.e_in[:, block(j, i)]
    l.met()
    stages = [piece.stages() for piece in pieces]
    events = [event for n in (0, 1, 2, 3, 6) for event in stages[n].pop(0)]
    stages[2][1] += stages[5].pop(0)
    events += ordered(stages[:4], 1)
    ends = {n: len(events) for n in range(4)}
    events += stages[4].pop(0)
    begun = len(events)
    events += stages[6].pop(0)
    crossed = len(events) + 8
    events += [event for stage in stages[4] for event in stage]
    ends[4] = len(events)
    events += [event for stage in stages[5] for event in stage]
    ends[5] = len(events)
    events += [event for stage in stages[6] for event in stage]
    ends[6] = len(events)
    state = [0]

    def pump(count):
        until(state[0] + count)

    def until(end):
        end = min(end, len(events))
        while state[0] < end:
            events[state[0]]()
            state[0] += 1

    def need(first, last):
        until(ends[last])
        for n in range(first, last + 1):
            pieces[n].whole()

    until(ends[3] - 4)
    pieces[0].whole()
    for g in range(8):
        tile = jnp.zeros((16, 128), F4)
        for n in range(4):
            at = (4 * g + n) * 16
            tile = tile + r.small[at : at + 16, :].astype(F4)
        r.vecs[:, g * 128 : (g + 1) * 128] = tile
        for n in range(3):
            at = (g * 3 + n) * 128
            r.bias_t[0:1, at : at + 128] = tile[6 + n : 7 + n, :]
        for n in range(4):
            at = (g * 4 + n) * 128
            r.bias_e[0:1, at : at + 128] = tile[9 + n : 10 + n, :]
    gain_one, bias_one, bias_m, gain_two, bias_two, bias_r = [
        (lambda n=n: r.vecs[n : n + 1, :]) for n in range(6)
    ]
    hat, _ = centre(r.hidden[...].astype(F4))
    r.fn[...] = (hat * gain_one() + bias_one()).astype(BF)

    def rank(source, down):
        return (r.sel[...] * by_transpose(source, down)).astype(BF)

    r.rank_t[...] = rank(r.fn[...], r.down_t[...])
    need(1, 3)
    until(begun)

    own = l.b * 256 + l.h * 128

    def kv_at(chip, h):
        return rows_at(r.kv, chip * 256 + h * 128, 128)

    kv_out = Exchange(l, r.send_kv, r.kv, 128, sems["kv"], lambda chip: kv_at(chip, l.h))
    q_out = Exchange(l, r.send_q, r.recv_q, 64, sems["q"])
    for step in range(4):
        plane = lax.rem(l.z + 1 + step, 4)

        def joint(part):
            at = pl.ds(pl.multiple_of(part * 1024 + plane * 256, 256), 256)
            tile = (
                product(r.fn[...], r.wt[:, at]) + r.bias_t[0:1, at] + product(r.rank_t[...], r.up_t[:, at])
            )
            return tile[:, :128], tile[:, 128:]

        for n, (qt, kt, vt) in enumerate(zip(joint(0), joint(1), joint(2))):
            c = plane * 4 + n * 2
            send_kv, send_q = rows_at(r.send_kv, c * 128, 256), rows_at(r.send_q, c * 64, 128)
            send_kv[0:128, :] = jnp.where(low, kt, swap(vt)).astype(BF)
            send_kv[128:256, :] = jnp.where(low, swap(kt), vt).astype(BF)
            qt = qt.astype(BF).astype(F4) * 0.125
            turned = swap(qt)
            send_q[0:64, :] = jnp.where(low64, qt[:64], turned[64:]).astype(BF)
            send_q[64:128, :] = jnp.where(low64, turned[:64], qt[64:]).astype(BF)
        for n in range(4):
            kv_out.send(plane * 4 + n)
            q_out.send(plane * 4 + n)
    kv_out.own()
    q_out.own()
    until(crossed)
    rank_grad_r = rank(r.cot[...], r.up_r[...])
    for i in range(8):
        r.bias_es[0:1, i * 128 : (i + 1) * 128] = r.bias_e[0:1, block(0, i)]

    def to_plane(source, target, name, half, own):
        for j, chip in ((3, l.db), (1, l.xb), (2, l.yb)):
            part = rows_at(source, half * 256 + (0 if own else j * 64), 64)
            l.send(part, rows_at(target, half * 256 + j * 64, 64), sems[name], (half, j), (l.h, chip))

    def from_plane(target, name, half):
        for j in range(1, 4):
            l.arrived(rows_at(target, half * 256 + j * 64, 64), sems[name], (half, j))

    def keep_own(target, at, tile):
        target[0:64, at] = tile[:64]
        target[256:320, at] = tile[64:]

    all_columns, ranks = slice(0, 1024), slice(1024, 1152)
    keep_own(r.cot_all, all_columns, r.cot[...])
    keep_own(r.cot_all, ranks, rank_grad_r)
    l.send(kv_at(l.b, l.h), kv_at(l.b, l.h), sems["f"], 0, (l.o, l.b))
    for k in range(1, CHIPS):
        kv_out.wait(k)
        c = l.behind(k)
        l.send(kv_at(c, l.h), kv_at(c, l.h), sems["f"], k, (l.o, l.b))
        until(min(state[0] + 1, ends[4]))
    to_plane(r.cot_all, r.cot_all, "ct", 0, True)
    to_plane(r.cot_all, r.cot_all, "ct", 1, True)
    until(ends[5])
    for k in range(1, CHIPS):
        q_out.wait(k)
    for k in range(CHIPS):
        l.arrived(kv_at(l.behind(k), l.o), sems["f"], k)

    for n in range(CHIPS):
        tile = r.recv_q[n * 64 : n * 64 + 64, :].astype(F4)
        r.q[n * 128 : n * 128 + 64, :] = jnp.where(low64, tile, 0.0).astype(BF)
        r.q[n * 128 + 64 : n * 128 + 128, :] = jnp.where(low64, swap(tile), 0.0).astype(BF)
        tile = r.kv[n * 256 : n * 256 + 256, :].astype(F4)
        r.ones_v[n * 256 : n * 256 + 256, :] = jnp.where(half_mask(256), 1.0, tile).astype(BF)
    a_out = Exchange(l, r.send_a, r.recv_a, 64, sems["a"])
    for i in range(8):
        queries = r.q[i * 256 : (i + 1) * 256, :]

        def fold(jj, total, masked=False):
            at = pl.ds(pl.multiple_of(jj * 512, 512), 512)
            powers = jnp.exp(by_transpose(queries, r.kv[at, :]))
            if masked:
                row = lax.broadcasted_iota(jnp.int32, (256, 512), 0)
                column = lax.broadcasted_iota(jnp.int32, (256, 512), 1)
                powers = jnp.where((row >= 128) | (column < 256), powers, 0.0)
            return total + product(powers.astype(BF), r.ones_v[at, :])

        total = fold(i, jnp.zeros((256, 128), F4), True)
        if i:
            total = lax.fori_loop(0, i, fold, total)
        share = total / swap(total)
        r.attden[i * 256 : (i + 1) * 256, :] = jnp.where(half_mask(256), total, share)
        for n in range(2):
            t = 2 * i + n
            part = share[n * 128 : n * 128 + 128]
            packed = jnp.where(low64, swap(part[64:]), part[:64]).astype(BF)
            r.send_a[t * 64 : t * 64 + 64, :] = packed
            a_out.send(t)
    a_out.own()
    until(ends[6])
    need(4, 4)
    for k in range(1, CHIPS):
        a_out.wait(k)
    for p in range(8):
        one = r.recv_a[p * 128 : p * 128 + 64, :].astype(F4)
        two = r.recv_a[p * 128 + 64 : p * 128 + 128, :].astype(F4)
        at = p * 128
        r.attended[0:64, at : at + 128] = jnp.where(low64, swap(one), two).astype(BF)
        r.attended[64:128, at : at + 128] = jnp.where(low64, one, swap(two)).astype(BF)

    rank_m = rank(r.attended[...], r.down_m[...])
    r.residual[...] = (
        r.hidden[...].astype(F4)
        + product(r.attended[...], r.wm[...])
        + bias_m()
        + product(rank_m, r.up_m[...])
    )
    hat, _ = centre(r.residual[...])
    second_normed = (hat * gain_two() + bias_two()).astype(BF)
    rank_e = rank(second_normed, r.down_e[...])
    keep_own(r.sn_all, all_columns, second_normed)
    keep_own(r.sn_all, ranks, rank_e)
    to_plane(r.sn_all, r.sn_all, "sn", 0, True)
    to_plane(r.sn_all, r.sn_all, "sn", 1, True)

    def tile_at(n, width):
        return pl.ds(pl.multiple_of(n * width, width), width)

    need(5, 6)
    from_plane(r.cot_all, "ct", 0)
    from_plane(r.cot_all, "ct", 1)

    def grad_tile(n, carry):
        at = tile_at(n, 256)
        r.agrad[:, at] = (
            by_transpose(r.cot_all[:, :1024], r.wr[at, :]) + product(r.cot_all[:, 1024:], r.down_rs[:, at])
        ).astype(BF)
        return carry

    lax.fori_loop(0, 4, grad_tile, 0)
    for half in range(2):
        from_plane(r.sn_all, "sn", half)
        these = slice(half * 256, half * 256 + 256)

        def inner_tile(n, carry):
            at = tile_at(n, 256)
            expanded = (
                product(r.sn_all[these, :1024], r.we[:, at])
                + r.bias_es[0:1, at]
                + product(r.sn_all[these, 1024:], r.up_es[:, at])
            )
            value, slope = gelu_parts(expanded)
            r.act[these, at] = value.astype(BF)
            r.agrad[these, at] = (r.agrad[these, at].astype(F4) * slope).astype(BF)
            return carry

        lax.fori_loop(0, 4, inner_tile, 0)

        def normed_tile(n, carry):
            at = tile_at(n, 256)
            r.ng_part[these, at] = by_transpose(r.agrad[these, :], r.we[at, :]).astype(BF)
            return carry

        lax.fori_loop(0, 4, normed_tile, 0)
        r.ng_part[these, 1024:] = by_transpose(r.agrad[these, :], r.up_es[...]).astype(BF)
        to_plane(r.ng_part, r.ng_recv, "ng", half, False)
    def flipped(tile):
        return tile.astype(F4).T.astype(BF)

    def reduce_tile(n, carry):
        at = tile_at(n, 256)
        r.red_part[:, at] = product(r.act[...], r.wr[:, at]).astype(BF)
        return carry

    lax.fori_loop(0, 4, reduce_tile, 0)
    r.red_part[:, 1024:] = by_transpose(r.act[...], r.down_rs[...]).astype(BF)
    rank_e_t, rank_grad_r_t = flipped(r.sn_all[:, 1024:]), flipped(r.cot_all[:, 1024:])
    for n in range(4):
        at = slice(n * 256, (n + 1) * 256)
        for kind, tile in enumerate((product(rank_e_t, r.agrad[:, at]), product(rank_grad_r_t, r.act[:, at]))):
            for m in range(2):
                to = (n * 2 + m) * 256 + kind * 128
                r.gs[:, to : to + 128] = tile[:, m * 128 : (m + 1) * 128].astype(BF)
    sliced = SliceReduce(l, r.gs, r.g, SLICES, (r.slice_c, r.slice_l), sems["slice"]).steps()
    sliced.pop(0)()
    from_plane(r.ng_recv, "ng", 0)
    from_plane(r.ng_recv, "ng", 1)

    def plane_sum(part, received, at):
        halves = []
        for start in (0, 256):
            total = part[start : start + 64, at].astype(F4)
            for j in range(1, 4):
                total = total + received[start + j * 64 : start + j * 64 + 64, at].astype(F4)
            halves.append(total)
        return jnp.concatenate(halves, axis=0)

    rank_grad_e = (r.sel[...] * plane_sum(r.ng_part, r.ng_recv, ranks)).astype(BF)
    normed_grad = plane_sum(r.ng_part, r.ng_recv, all_columns) + product(rank_grad_e, r.down_e[...])
    back_two = norm_back(r.residual[...], gain_two(), normed_grad)
    residual_grad = r.cot[...].astype(F4) + back_two
    mixed_grad = residual_grad.astype(BF)
    rank_grad_m = rank(mixed_grad, r.up_m[...])
    g_out = Exchange(l, r.send_g, r.recv_g, 64, sems["g"])
    for step in range(4):
        plane = lax.rem(l.z + 1 + step, 4)
        at = pl.ds(pl.multiple_of(plane * 256, 256), 256)
        both = by_transpose(mixed_grad, r.wm[at, :]) + product(rank_grad_m, r.down_m[:, at])
        for n in range(2):
            tile = both[:, n * 128 : n * 128 + 128]
            turned = swap(tile)
            send_g = rows_at(r.send_g, (plane * 4 + n * 2) * 64, 128)
            send_g[0:64, :] = jnp.where(low64, tile[64:], turned[:64]).astype(BF)
            send_g[64:128, :] = jnp.where(low64, turned[64:], tile[:64]).astype(BF)
        for n in range(4):
            g_out.send(plane * 4 + n)
    g_out.own()

    to_plane(r.red_part, r.red_recv, "rd", 0, False)
    to_plane(r.red_part, r.red_recv, "rd", 1, False)

    def adapter(at, left, right, width):
        for n in range(width // 512):
            r.gp[:, at + n * 512 : at + (n + 1) * 512] = product(left, right[:, n * 512 : (n + 1) * 512]).astype(BF)

    adapter(MIXER_D, flipped(rank_grad_m), r.attended, 1024)
    adapter(MIXER_U, flipped(rank_m), mixed_grad, 1024)
    adapter(EXPAND_D, flipped(rank_grad_e), second_normed, 1024)
    early = Reduce(l, r.gp, r.g, 0, TRIPLE_D, (r.early_c, r.early_1, r.early_2, r.early_3), sems["early"]).steps()

    def finish_output():
        from_plane(r.red_recv, "rd", 0)
        from_plane(r.red_recv, "rd", 1)
        rank_r = (r.sel[...] * plane_sum(r.red_part, r.red_recv, ranks)).astype(BF)
        reduced = plane_sum(r.red_part, r.red_recv, all_columns)
        r.layer_out[...] = (r.residual[...] + reduced + bias_r() + product(rank_r, r.up_r[...])).astype(BF)
        adapter(REDUCE_U, flipped(rank_r), r.cot, 1024)
        r.residual[...] = residual_grad
        early.pop(0)()

    for n in range(CHIPS):
        tile = r.kv[n * 256 : n * 256 + 256, :].astype(F4)
        wide = half_mask(256)
        r.ones_v[n * 256 : n * 256 + 256, :] = jnp.where(wide, tile, 0.0).astype(BF)
        r.vz[n * 256 : n * 256 + 256, :] = jnp.where(wide, 0.0, tile).astype(BF)
        r.k_t[:, n * 256 : n * 256 + 256] = tile.T[:64, :].astype(BF)
    r.dq_t[...] = jnp.zeros((128, 2048), F4)
    for k in range(1, CHIPS):
        g_out.wait(k)
    for n in range(CHIPS):
        at = n * 128
        g = r.recv_g[n * 64 : n * 64 + 64, :].astype(F4)
        both = r.attden[at : at + 128, :]
        grad = jnp.concatenate([g, swap(g)], axis=0)
        numer = jnp.where(low, 0.0, grad / swap(both))
        numer_low = numer.astype(BF)
        r.dz[at : at + 128, :] = numer_low
        r.qd[at : at + 128, :] = jnp.where(
            low, r.q[at : at + 128, :].astype(F4), numer_low.astype(F4)
        ).astype(BF)
        term = jnp.where(low, 0.0, numer * both)
        row = -jnp.sum(term.T, axis=0, keepdims=True)
        r.ddrow[0:1, at : at + 128] = row.astype(BF).astype(F4)
    dkv_out = Exchange(l, r.send_dkv, r.recv_dkv, 128, sems["dkv"])
    dq_out = Exchange(l, r.send_dq, r.recv_dq, 64, sems["dq"])

    def exchange(jj):
        for n in range(2):
            t = 2 * jj + n
            l.send(rows_at(r.part, t * 256 + l.o * 128, 128), rows_at(r.recv_part, t * 128, 128), sems["e"], t, (l.o, l.b))

    def finish(jj):
        for n in range(2):
            t = 2 * jj + n
            l.arrived(rows_at(r.recv_part, t * 128, 128), sems["e"], t)
            here = r.part[pl.ds(pl.multiple_of(t * 256 + l.h * 128, 128), 128), :]
            r.send_dkv[t * 128 : t * 128 + 128, :] = (here + r.recv_part[t * 128 : t * 128 + 128, :]).astype(BF)
            y = r.dq_t[:, t * 128 : t * 128 + 128].T * 0.125
            r.send_dq[t * 64 : t * 64 + 64, :] = jnp.where(low64, y[:64], swap(y[64:])).astype(BF)
            dkv_out.send(t)
            dq_out.send(t)

    for jj in range(8):
        keys = slice(jj * 512, jj * 512 + 512)

        def fold_back(i, total, masked=False):
            at = tile_at(i, 256)
            both = r.qd[at, :]
            powers = jnp.exp(by_transpose(r.ones_v[keys, :], both))
            if masked:
                row = lax.broadcasted_iota(jnp.int32, (512, 256), 0)
                column = lax.broadcasted_iota(jnp.int32, (512, 256), 1)
                powers = jnp.where((row < 256) | (column >= 128), powers, 0.0)
            prob = by_transpose(r.vz[keys, :], both) + r.ddrow[0:1, at]
            score = (powers * prob).astype(BF)
            r.dq_t[0:64, at] += product(r.k_t[:, keys], score)
            return total + product(score, r.q[at, :]) + product(powers.astype(BF), r.dz[at, :])

        total = fold_back(jj, jnp.zeros((512, 128), F4), True)
        if jj < 7:
            total = lax.fori_loop(jj + 1, 8, fold_back, total)
        r.part[keys, :] = total
        exchange(jj)
        if jj:
            finish(jj - 1)
        if jj == 1:
            finish_output()
        for steps in {0: [sliced], 2: [sliced, early], 4: [early], 5: [sliced], 7: [early]}.get(jj, []):
            steps.pop(0)()
    finish(7)
    dkv_out.own()
    dq_out.own()
    for k in range(1, CHIPS):
        dkv_out.wait(k)
        dq_out.wait(k)
    for p in range(8):
        at = p * 128
        one = r.recv_dq[p * 128 : p * 128 + 64, :].astype(F4)
        two = r.recv_dq[p * 128 + 64 : p * 128 + 128, :].astype(F4)
        r.jg[0:64, at : at + 128] = jnp.where(low64, one, swap(two)).astype(BF)
        r.jg[64:128, at : at + 128] = jnp.where(low64, swap(one), two).astype(BF)
        one = r.recv_dkv[p * 256 : p * 256 + 128, :].astype(F4)
        two = r.recv_dkv[p * 256 + 128 : p * 256 + 256, :].astype(F4)
        r.jg[:, 1024 + at : 1152 + at] = jnp.where(low, one, swap(two)).astype(BF)
        r.jg[:, 2048 + at : 2176 + at] = jnp.where(low, swap(one), two).astype(BF)

    rank_grad_t = rank(r.jg[...], r.up_t[...])
    adapter(TRIPLE_D, flipped(rank_grad_t), r.fn, 1024)
    adapter(TRIPLE_U, flipped(r.rank_t[...]), r.jg, 3072)
    halves = [
        Reduce(
            l, r.gp, r.g, TRIPLE_D, SLICES - TRIPLE_D,
            [buf.at[n] for buf in (r.late_c, r.late_1, r.late_2, r.late_3)],
            sems[("late", "late_two")[n]], slice(n * 64, n * 64 + 64),
        ).steps()
        for n in range(2)
    ]
    late = [step for pair in zip(*halves) for step in pair]
    for _ in range(4):
        late.pop(0)()

    def triple_tile(n, carry):
        at = tile_at(n, 512)
        return carry + by_transpose(r.jg[:, at], r.wt[:, at])

    normed_grad = lax.fori_loop(0, 6, triple_tile, product(rank_grad_t, r.down_t[...]))
    back_one = norm_back(r.hidden[...].astype(F4), gain_one(), normed_grad)
    r.hidden_grad[...] = (r.residual[...] + back_one).astype(BF)
    while late or early or sliced:
        for rest in (late, late, early, sliced):
            if rest:
                rest.pop(0)()
    for out in (kv_out, q_out, a_out, g_out, dkv_out, dq_out):
        out.settle()
    l.settle()


def layer(*arrays):
    vmem = pl.BlockSpec(memory_space=pltpu.VMEM)
    hbm = pl.BlockSpec(memory_space=pl.ANY)
    dma = pltpu.SemaphoreType.DMA
    return pl.pallas_call(
        layer_kernel,
        name="layer",
        in_specs=[hbm if name.endswith("_sh") else vmem for name in INPUTS],
        out_shape=[jax.ShapeDtypeStruct(*OUTPUTS[name]) for name in OUTPUTS],
        out_specs=[vmem] * len(OUTPUTS),
        scratch_shapes=[pltpu.VMEM(*SCRATCH[name]) for name in SCRATCH]
        + [dma((5,))]
        + [dma(SEMS[name]) for name in SEMS for _ in range(2)],
        compiler_params=pltpu.CompilerParams(
            collective_id=0, has_side_effects=True, vmem_limit_bytes=LIMIT
        ),
    )(*arrays)


WRITTEN = (1024, 3072, 1024, 1024, 1024, 4096, 4096, 1024)


def write_kernel(layer_in, hidden_in, g, layer_out, hidden_out, td, tu, md, mu, ed, eu, rd, ru, low, high, in_sem, out_sem):
    passed = [
        pltpu.make_async_copy(layer_in, layer_out, out_sem.at[0]),
        pltpu.make_async_copy(hidden_in, hidden_out, out_sem.at[1]),
    ]
    reads = [
        pltpu.make_async_copy(
            g.at[:, n * 2048 : (n + 1) * 2048], low.at[:, n * 2048 : (n + 1) * 2048], in_sem.at[n]
        )
        for n in range(8)
    ]
    for copy in reads + passed:
        copy.start()
    writes = []

    def write(start, width, target, at):
        copy = pltpu.make_async_copy(
            high.at[:, start : start + width], target.at[:, at : at + width], out_sem.at[2 + len(writes)]
        )
        copy.start()
        writes.append(copy)

    whole = (
        (MIXER_D, 1024, md, 0), (MIXER_U, 1024, mu, 0), (EXPAND_D, 1024, ed, 0), (REDUCE_U, 1024, ru, 0),
        (TRIPLE_D, 1024, td, 0), (TRIPLE_U, 1024, tu, 0), (TRIPLE_U + 1024, 2048, tu, 1024),
    )
    done = 0
    for start, width, target, at in whole:
        while done * 2048 < start + width:
            reads[done].wait()
            done += 1
        high[:, start : start + width] = low[:, start : start + width].astype(F4)
        write(start, width, target, at)
    for n in range(done, 8):
        reads[n].wait()
    for h in range(2):
        for kind, target in enumerate((eu, rd)):
            to = SLICES + (h * 2 + kind) * 2048
            for z in range(4):
                for p in range(4):
                    source = SLICES + p * 2048 + h * 1024 + z * 256 + kind * 128
                    here = to + (z * 4 + p) * 128
                    high[:, here : here + 128] = low[:, source : source + 128].astype(F4)
            write(to, 2048, target, h * 2048)
    for copy in passed + writes:
        copy.wait()


def written(layer_out, hidden_grad, g):
    hbm = pl.BlockSpec(memory_space=pl.ANY)
    dma = pltpu.SemaphoreType.DMA
    return pl.pallas_call(
        write_kernel,
        name="written",
        in_specs=[hbm] * 3,
        out_shape=[jax.ShapeDtypeStruct((128, 1024), BF)] * 2 + [jax.ShapeDtypeStruct((128, width), F4) for width in WRITTEN],
        out_specs=[hbm] * 10,
        scratch_shapes=[pltpu.VMEM((128, COLUMNS), BF), pltpu.VMEM((128, COLUMNS), F4), dma((8,)), dma((16,))],
        compiler_params=pltpu.CompilerParams(vmem_limit_bytes=20 * 1024 * 1024),
    )(layer_out, hidden_grad, g)


def small_block(blocks, triple_bias, expand_bias):
    place = lax.rem(shard_of(lax.axis_index("head"), lax.axis_index("blk")), 4)
    lane = jnp.arange(128, dtype=jnp.int32)[None, :]
    six = jnp.where(lane // 32 == place, jnp.tile(jnp.stack(blocks), (1, 4)), 0)
    wide = jnp.arange(384, dtype=jnp.int32)
    three = jnp.where(wide // 96 == place, jnp.tile(triple_bias, 4), 0).reshape(3, 128)
    row = jnp.arange(4, dtype=jnp.int32)[:, None]
    four = jnp.where(row == place, expand_bias[None, :], 0)
    return jnp.concatenate([six, three, four, jnp.zeros((3, 128), BF)], axis=0).astype(BF)


def local_fast(
    hidden, adapter_index, first_gain, first_bias, triple_weight, triple_bias, mixer_weight, mixer_bias,
    second_gain, second_bias, expand_weight, expand_bias, reduce_weight, reduce_bias, triple_down, triple_up,
    mixer_down, mixer_up, expand_down, expand_up, reduce_down, reduce_up, cotangent,
):
    def turned(factor):
        return jnp.transpose(factor, (0, 2, 1)).reshape(ADAPTERS * RANK, factor.shape[1])

    small_sh = small_block(
        [first_gain, first_bias, mixer_bias, second_gain, second_bias, reduce_bias], triple_bias, expand_bias
    )
    layer_out, hidden_grad, g = layer(
        hidden, cotangent, selector(adapter_index), small_sh, triple_weight, mixer_weight, reduce_weight, expand_weight,
        turned(triple_down), flat_up(triple_up), turned(mixer_down), flat_up(mixer_up),
        turned(expand_down), flat_up(expand_up), turned(reduce_down), flat_up(reduce_up),
    )
    layer_out, hidden_grad, *grads = written(layer_out, hidden_grad, g)

    def down_out(part):
        return jnp.transpose(part.reshape(ADAPTERS, RANK, part.shape[1]), (0, 2, 1))

    def up_out(part):
        return part.reshape(ADAPTERS, RANK, part.shape[1])

    shaped = [down_out, up_out, down_out, up_out, down_out, up_out, down_out, up_out]
    return (layer_out, hidden_grad) + tuple(shape(part) for shape, part in zip(shaped, grads))


def solution(mesh):
    placed = (
        P(("blk", "head"), None),
        P(("blk", "head")),
        P(("head", "blk")),
        P(("head", "blk")),
        P(("head", "blk"), None),
        P(("head", "blk")),
        P(("head", "blk"), None),
        P(("head", "blk")),
        P(("head", "blk")),
        P(("head", "blk")),
        P(("head", "blk"), None),
        P(("head", "blk")),
        P(("head", "blk"), None),
        P(("head", "blk")),
        P(),
        P(),
        P(),
        P(),
        P(),
        P(),
        P(),
        P(),
        P(("blk", "head"), None),
    )
    fits = tuple(mesh.shape[name] for name in ("head", "blk")) == (2, CHIPS)
    return jax.shard_map(
        local_fast if fits else local,
        mesh=mesh,
        in_specs=placed,
        out_specs=(
            P(("blk", "head"), None),
            P(("blk", "head"), None),
            P(),
            P(),
            P(),
            P(),
            P(),
            P(),
            P(),
            P(),
        ),
        check_vma=False,
    )
```

```python
import functools
import math
import types

import jax
import jax.numpy as jnp
from jax import lax
from jax.experimental import pallas as pl
from jax.experimental.pallas import tpu as pltpu
from jax.sharding import PartitionSpec as P

WIDTH = 1024
HEADS = 16
HEAD_DIM = 64
RANK = 16
ADAPTERS = 8
BLOCK = 256


EPSILON = 1e-05


def product(left, right):
    return jnp.dot(left, right, preferred_element_type=jnp.float32)


def by_transpose(left, right):
    return lax.dot_general(
        left, right, (((1,), (1,)), ((), ())), preferred_element_type=jnp.float32
    )


def transpose_by(left, right):
    return lax.dot_general(
        left, right, (((0,), (0,)), ((), ())), preferred_element_type=jnp.float32
    )


def layer_norm(stream, scales, offset):
    average = jnp.mean(stream, axis=-1, keepdims=True)
    centred = stream - average
    variance = jnp.mean(centred * centred, axis=-1, keepdims=True)
    return centred * lax.rsqrt(variance + EPSILON) * scales + offset


def selector(adapter_index):
    column = jnp.arange(ADAPTERS * RANK, dtype=jnp.int32) // RANK
    return (adapter_index[:, None] == column[None, :]).astype(jnp.float32)


def flat_down(factor):
    return jnp.transpose(factor, (1, 0, 2)).reshape(factor.shape[1], ADAPTERS * RANK)


def flat_up(factor):
    return factor.reshape(ADAPTERS * RANK, factor.shape[2])


def unflat_down(gradient):
    return jnp.transpose(gradient.reshape(gradient.shape[0], ADAPTERS, RANK), (1, 0, 2))


def unflat_up(gradient):
    return gradient.reshape(ADAPTERS, RANK, gradient.shape[1])


def projected(source, weight, offset, down_flat, up_flat, selection):
    low_rank = (selection * product(source, down_flat)).astype(jnp.bfloat16)
    return (
        product(source, weight) + offset.astype(jnp.float32) + product(low_rank, up_flat),
        low_rank,
    )


def adapter_grads(source, low_rank, out_grad, down_flat, up_flat, selection):
    rank_grad = (selection * by_transpose(out_grad, up_flat)).astype(jnp.bfloat16)
    down_grad = transpose_by(source, rank_grad)
    up_grad = transpose_by(low_rank, out_grad)
    return (down_grad, up_grad, by_transpose(rank_grad, down_flat))


def score_block(queries, keys_block):
    return jnp.einsum("qhd,khd->qhk", queries, keys_block, preferred_element_type=jnp.float32) * (
        1.0 / math.sqrt(HEAD_DIM)
    )


def cut_rows(arrays, trailing):
    length = arrays[0].shape[0]
    block_rows = math.gcd(length, 512)
    repeats = length // block_rows
    shaped = tuple(
        (
            array.reshape((repeats, block_rows) + shape_tail)
            for array, shape_tail in zip(arrays, trailing)
        )
    )
    firsts = jnp.arange(repeats, dtype=jnp.int32) * block_rows
    return (shaped, firsts, block_rows)


def forward_fold(queries, query_places, locate, totals, portion):
    head_count = queries.shape[1]
    query_block = query_places // BLOCK
    last_block = jnp.max(query_block)
    shaped, firsts, block_rows = cut_rows(portion, ((head_count, HEAD_DIM), (head_count, HEAD_DIM)))

    def forward_visiting(carried, packet):
        keys_block, values_block, first_row = packet
        key_places = locate(first_row, block_rows)

        def forward_compute(running):
            numerator, denominator = running
            allowed = (key_places // BLOCK)[None, None, :] <= query_block[:, None, None]
            powers = jnp.where(allowed, jnp.exp(score_block(queries, keys_block)), 0.0)
            numerator = numerator + jnp.einsum(
                "qhk,khd->qhd",
                powers.astype(jnp.bfloat16),
                values_block,
                preferred_element_type=jnp.float32,
            )
            return (numerator, denominator + jnp.sum(powers, axis=-1))

        skipped = jnp.min(key_places) // BLOCK > last_block
        return (lax.cond(skipped, lambda running: running, forward_compute, carried), None)

    return lax.scan(forward_visiting, totals, shaped + (firsts,))[0]


def query_grad_fold(queries, query_places, locate, numer_grad, denom_grad, totals, portion):
    head_count = queries.shape[1]
    query_block = query_places // BLOCK
    last_block = jnp.max(query_block)
    shaped, firsts, block_rows = cut_rows(portion, ((head_count, HEAD_DIM), (head_count, HEAD_DIM)))

    def query_visiting(carried, packet):
        keys_block, values_block, first_row = packet
        key_places = locate(first_row, block_rows)

        def query_compute(running):
            allowed = (key_places // BLOCK)[None, None, :] <= query_block[:, None, None]
            powers = jnp.where(allowed, jnp.exp(score_block(queries, keys_block)), 0.0)
            prob_grad = jnp.einsum(
                "qhd,khd->qhk", numer_grad, values_block, preferred_element_type=jnp.float32
            )
            score_grad = (powers * (prob_grad + denom_grad[:, :, None])).astype(jnp.bfloat16)
            return running + jnp.einsum(
                "qhk,khd->qhd", score_grad, keys_block, preferred_element_type=jnp.float32
            )

        skipped = jnp.min(key_places) // BLOCK > last_block
        return (lax.cond(skipped, lambda running: running, query_compute, carried), None)

    return lax.scan(query_visiting, totals, shaped + (firsts,))[0]


def key_grad_fold(keys_here, values_here, key_places, locate, totals, portion):
    head_count = keys_here.shape[1]
    key_block = key_places // BLOCK
    first_block = jnp.min(key_block)
    shaped, firsts, block_rows = cut_rows(
        portion, ((head_count, HEAD_DIM), (head_count, HEAD_DIM), (head_count,))
    )

    def key_visiting(carried, packet):
        query_rows, numer_rows, denom_rows, first_row = packet
        query_places = locate(first_row, block_rows)

        def key_compute(running):
            keys_grad, values_grad = running
            allowed = key_block[None, None, :] <= (query_places // BLOCK)[:, None, None]
            powers = jnp.where(allowed, jnp.exp(score_block(query_rows, keys_here)), 0.0)
            prob_grad = jnp.einsum(
                "qhd,khd->qhk", numer_rows, values_here, preferred_element_type=jnp.float32
            )
            score_grad = (powers * (prob_grad + denom_rows.astype(jnp.float32)[:, :, None])).astype(
                jnp.bfloat16
            )
            keys_grad = keys_grad + jnp.einsum(
                "qhk,qhd->khd", score_grad, query_rows, preferred_element_type=jnp.float32
            )
            values_grad = values_grad + jnp.einsum(
                "qhk,qhd->khd",
                powers.astype(jnp.bfloat16),
                numer_rows,
                preferred_element_type=jnp.float32,
            )
            return (keys_grad, values_grad)

        skipped = jnp.max(query_places) // BLOCK < first_block
        return (lax.cond(skipped, lambda running: running, key_compute, carried), None)

    return lax.scan(key_visiting, totals, shaped + (firsts,))[0]


def local(
    hidden,
    adapter_index,
    first_gain,
    first_bias,
    triple_weight,
    triple_bias,
    mixer_weight,
    mixer_bias,
    second_gain,
    second_bias,
    expand_weight,
    expand_bias,
    reduce_weight,
    reduce_bias,
    triple_down,
    triple_up,
    mixer_down,
    mixer_up,
    expand_down,
    expand_up,
    reduce_down,
    reduce_up,
    cotangent,
):
    gathered = (
        lax.all_gather(first_gain, ("head", "blk"), axis=0, tiled=True),
        lax.all_gather(first_bias, ("head", "blk"), axis=0, tiled=True),
        lax.all_gather(triple_weight, ("head", "blk"), axis=0, tiled=True),
        lax.all_gather(triple_bias, ("head", "blk"), axis=0, tiled=True),
        lax.all_gather(mixer_weight, ("head", "blk"), axis=0, tiled=True),
        lax.all_gather(mixer_bias, ("head", "blk"), axis=0, tiled=True),
        lax.all_gather(second_gain, ("head", "blk"), axis=0, tiled=True),
        lax.all_gather(second_bias, ("head", "blk"), axis=0, tiled=True),
        lax.all_gather(expand_weight, ("head", "blk"), axis=0, tiled=True),
        lax.all_gather(expand_bias, ("head", "blk"), axis=0, tiled=True),
        lax.all_gather(reduce_weight, ("head", "blk"), axis=0, tiled=True),
        lax.all_gather(reduce_bias, ("head", "blk"), axis=0, tiled=True),
    )
    (
        gain_one,
        bias_one,
        weight_triple,
        bias_triple,
        weight_mixer,
        bias_mixer,
        gain_two,
        bias_two,
        weight_expand,
        bias_expand,
        weight_reduce,
        bias_reduce,
    ) = gathered
    token_count = hidden.shape[0]
    head_ways = lax.axis_size("head")
    cycle_ways = lax.axis_size("blk")
    selection = selector(adapter_index)
    down_triple = flat_down(triple_down)
    upward_triple = flat_up(triple_up)
    down_mixer = flat_down(mixer_down)
    upward_mixer = flat_up(mixer_up)
    down_expand = flat_down(expand_down)
    upward_expand = flat_up(expand_up)
    down_reduce = flat_down(reduce_down)
    upward_reduce = flat_up(reduce_up)
    stream = hidden.astype(jnp.float32)

    def first_norm(values_in):
        return layer_norm(values_in, gain_one.astype(jnp.float32), bias_one.astype(jnp.float32))

    def second_norm(values_in):
        return layer_norm(values_in, gain_two.astype(jnp.float32), bias_two.astype(jnp.float32))

    first_normed = first_norm(stream).astype(jnp.bfloat16)
    joint, rank_triple = projected(
        first_normed, weight_triple, bias_triple, down_triple, upward_triple, selection
    )
    joint = joint.astype(jnp.bfloat16)
    parts = joint.reshape(token_count, 3, HEADS, HEAD_DIM)
    own_shard = lax.axis_index("blk") * head_ways + lax.axis_index("head")
    query_places = own_shard * token_count + jnp.arange(token_count, dtype=jnp.int32)

    def locate(first_row, length):
        rows_here = first_row + jnp.arange(length, dtype=jnp.int32)
        shard_index = rows_here // token_count
        return (
            shard_index % cycle_ways * head_ways + shard_index // cycle_ways
        ) * token_count + rows_here % token_count

    queries = parts[:, 0]
    keys_here = parts[:, 1]
    values_here = parts[:, 2]
    head_count = queries.shape[1]
    flat_keys = keys_here.reshape(token_count, head_count * HEAD_DIM)
    flat_values = values_here.reshape(token_count, head_count * HEAD_DIM)
    zeros_rows = jnp.zeros((token_count, head_count, HEAD_DIM), jnp.float32)
    payload = (flat_keys, flat_values)
    numerator, denominator = forward_fold(
        queries,
        query_places,
        locate,
        (zeros_rows, jnp.zeros((token_count, head_count), jnp.float32)),
        (
            lax.all_gather(payload[0], ("head", "blk"), axis=0, tiled=True),
            lax.all_gather(payload[1], ("head", "blk"), axis=0, tiled=True),
        ),
    )
    attended = numerator / denominator[:, :, None]
    attended_low = attended.astype(jnp.bfloat16).reshape(token_count, WIDTH)
    mixed, rank_mixer = projected(
        attended_low, weight_mixer, bias_mixer, down_mixer, upward_mixer, selection
    )
    residual = stream + mixed
    second_normed = second_norm(residual).astype(jnp.bfloat16)
    expanded, rank_expand = projected(
        second_normed, weight_expand, bias_expand, down_expand, upward_expand, selection
    )
    activated = jax.nn.gelu(expanded, approximate=True).astype(jnp.bfloat16)
    reduced, rank_reduce = projected(
        activated, weight_reduce, bias_reduce, down_reduce, upward_reduce, selection
    )
    layer_out = (residual + reduced).astype(jnp.bfloat16)
    reduce_down_grad, reduce_up_grad, through_reduce = adapter_grads(
        activated, rank_reduce, cotangent, down_reduce, upward_reduce, selection
    )
    activated_grad = (by_transpose(cotangent, weight_reduce) + through_reduce).astype(jnp.bfloat16)
    gelu_back = jax.vjp(lambda values_in: jax.nn.gelu(values_in, approximate=True), expanded)[1]
    expanded_grad = gelu_back(activated_grad.astype(jnp.float32))[0].astype(jnp.bfloat16)
    expand_down_grad, expand_up_grad, through_expand = adapter_grads(
        second_normed, rank_expand, expanded_grad, down_expand, upward_expand, selection
    )
    normed_grad = by_transpose(expanded_grad, weight_expand) + through_expand
    second_back = jax.vjp(second_norm, residual)[1]
    residual_grad = cotangent.astype(jnp.float32) + second_back(normed_grad)[0]
    mixed_grad = residual_grad.astype(jnp.bfloat16)
    mixer_down_grad, mixer_up_grad, through_mixer = adapter_grads(
        attended_low, rank_mixer, mixed_grad, down_mixer, upward_mixer, selection
    )
    attended_grad = (by_transpose(mixed_grad, weight_mixer) + through_mixer).astype(jnp.bfloat16)
    output_grad = attended_grad.reshape(token_count, HEADS, HEAD_DIM).astype(jnp.float32)
    numer_grad = (output_grad / denominator[:, :, None]).astype(jnp.bfloat16)
    denom_grad = (-jnp.sum(output_grad * attended, axis=-1) / denominator).astype(jnp.bfloat16)
    payload = (flat_keys, flat_values)
    query_grad = query_grad_fold(
        queries,
        query_places,
        locate,
        numer_grad,
        denom_grad.astype(jnp.float32),
        zeros_rows,
        (
            lax.all_gather(payload[0], ("head", "blk"), axis=0, tiled=True),
            lax.all_gather(payload[1], ("head", "blk"), axis=0, tiled=True),
        ),
    )
    payload = (
        queries.reshape(token_count, head_count * HEAD_DIM),
        numer_grad.reshape(token_count, head_count * HEAD_DIM),
        denom_grad,
    )
    keys_grad, values_grad = key_grad_fold(
        keys_here,
        values_here,
        query_places,
        locate,
        (zeros_rows, zeros_rows),
        (
            lax.all_gather(payload[0], ("head", "blk"), axis=0, tiled=True),
            lax.all_gather(payload[1], ("head", "blk"), axis=0, tiled=True),
            lax.all_gather(payload[2], ("head", "blk"), axis=0, tiled=True),
        ),
    )
    factor = 1.0 / math.sqrt(HEAD_DIM)
    joint_grad = jnp.stack([query_grad * factor, keys_grad * factor, values_grad], axis=1).astype(
        jnp.bfloat16
    )
    joint_tokens = joint_grad.reshape(token_count, 3 * WIDTH)
    triple_down_grad, triple_up_grad, through_triple = adapter_grads(
        first_normed, rank_triple, joint_tokens, down_triple, upward_triple, selection
    )
    normed_one_grad = by_transpose(joint_tokens, weight_triple) + through_triple
    first_back = jax.vjp(first_norm, stream)[1]
    hidden_grad = (residual_grad + first_back(normed_one_grad)[0]).astype(jnp.bfloat16)
    summed = lax.psum(
        (
            triple_down_grad,
            triple_up_grad,
            mixer_down_grad,
            mixer_up_grad,
            expand_down_grad,
            expand_up_grad,
            reduce_down_grad,
            reduce_up_grad,
        ),
        ("head", "blk"),
    )
    return (
        layer_out,
        hidden_grad,
        unflat_down(summed[0]),
        unflat_up(summed[1]),
        unflat_down(summed[2]),
        unflat_up(summed[3]),
        unflat_down(summed[4]),
        unflat_up(summed[5]),
        unflat_down(summed[6]),
        unflat_up(summed[7]),
    )


MESH = pl.DeviceIdType.MESH
CHIPS = 16
LIMIT = 62 * 1024 * 1024 - 512 * 1024
BF = jnp.bfloat16
F4 = jnp.float32


ALONG = ((0, 1, 2, 3), (1, 0, 2, 3), (2, 1, 3, 0), (3, 2, 1, 0))


class Links:
    def __init__(self):
        self.h = lax.axis_index("head")
        self.b = lax.axis_index("blk")
        self.o = 1 - self.h
        self.sent = []
        self.x = lax.rem(self.b, 2)
        self.y = lax.rem(self.b // 2, 2)
        self.z = self.b // 4
        self.xb = self.b + 1 - 2 * self.x
        self.yb = self.b + 2 - 4 * self.y
        self.db = self.xb + 2 - 4 * self.y
        self.columns = [lax.rem(chip, 4) for chip in (self.b, self.xb, self.yb, self.db)]

    def nth(self, n):
        return sum(jnp.where(self.z == z, table[n], 0) for z, table in enumerate(ALONG))

    def at_line(self, z):
        return lax.rem(self.b, 4) + 4 * z

    def along(self, piece, sems, index):
        for k, wanted in ((1, self.z < 3), (3, self.z > 0), (2, None)):
            where = (piece, piece, sems, index + (self.z,), (self.h, self.ahead(4 * k)))
            if wanted is None:
                self.send(*where)
            else:
                self.send_if(wanted, *where)

    def pass_on(self, piece, z, sems, index):
        wanted = (self.z == 2) & (z == 0) | (self.z == 1) & (z == 3)
        chip = self.columns[0] + 4 * (3 - z)
        self.send_if(wanted, piece, piece, sems, index + (z,), (self.h, chip))

    def ahead(self, k):
        return lax.rem(self.b + k, CHIPS)

    def behind(self, k):
        return lax.rem(self.b + CHIPS - k, CHIPS)

    def greet(self):
        barrier = pltpu.get_barrier_semaphore()
        for k in range(1, CHIPS):
            pl.semaphore_signal(
                barrier, 1, device_id=(self.h, self.ahead(k)), device_id_type=MESH
            )
        pl.semaphore_signal(barrier, 1, device_id=(self.o, self.b), device_id_type=MESH)

    def met(self):
        pl.semaphore_wait(pltpu.get_barrier_semaphore(), CHIPS)

    def copy(self, source, target, sems, at, device):
        return pltpu.make_async_remote_copy(
            src_ref=source,
            dst_ref=target,
            send_sem=sems[0].at[at],
            recv_sem=sems[1].at[at],
            device_id=device,
            device_id_type=MESH,
        )

    def send(self, source, target, sems, at, device):
        copy = self.copy(source, target, sems, at, device)
        copy.start()
        self.sent.append((None, copy))

    def send_if(self, wanted, *where):
        copy = self.copy(*where)
        pl.when(wanted)(copy.start)
        self.sent.append((wanted, copy))

    def arrived(self, target, sems, at):
        self.copy(target, target, sems, at, (self.o, self.b)).wait_recv()

    def settle(self):
        for wanted, copy in self.sent:
            if wanted is None:
                copy.wait_send()
            else:
                pl.when(wanted)(copy.wait_send)
        self.sent = []


class Exchange:
    def __init__(self, links, source, target, rows, sems, slot=None):
        self.links, self.source, self.target = links, source, target
        self.rows, self.sems = rows, sems
        self.slot = slot or (lambda chip: rows_at(target, chip * rows, rows))

    def send(self, t):
        l = self.links

        @pl.when(l.b != t)
        def _():
            l.copy(
                rows_at(self.source, t * self.rows, self.rows),
                self.slot(l.b), self.sems, lax.rem(t + CHIPS - l.b, CHIPS), (l.h, t),
            ).start()

    def own(self):
        l = self.links
        copy = pltpu.make_async_copy(
            rows_at(self.source, l.b * self.rows, self.rows), self.slot(l.b), self.sems[0].at[0]
        )
        copy.start()
        copy.wait()

    def wait(self, k):
        self.links.arrived(self.slot(self.links.behind(k)), self.sems, k)

    def settle(self):
        for k in range(1, CHIPS):
            l = self.links
            part = rows_at(self.source, l.ahead(k) * self.rows, self.rows)
            l.copy(part, part, self.sems, k, (l.h, l.ahead(k))).wait_send()


def half_mask(rows):
    return lax.broadcasted_iota(jnp.int32, (rows, 128), 1) < 64


def swap(tile):
    return pltpu.roll(tile, 64, 1)


def rows_at(ref, start, count):
    return ref.at[pl.ds(pl.multiple_of(start, 16), count), :]


class Gather:
    def __init__(self, links, number, slot, sems):
        self.links, self.p, self.slot = links, number, slot
        self.sems = sems

    def send(self, axis, n, chip, device):
        piece = self.slot(self.links.h, chip)
        self.links.send(piece, piece, self.sems[axis], (self.p, n), device)

    def chip(self, side, n):
        return side + 4 * self.links.nth(n)

    def own(self, n):
        l = self.links
        chip = self.chip(l.columns[0], n)
        if n:
            l.pass_on(self.slot(l.h, chip), l.nth(n), self.sems["z"], (self.p,))
        else:
            l.along(self.slot(l.h, chip), self.sems["z"], (self.p,))
        self.send("x", n, chip, (l.h, l.xb))
        self.send("y", n, chip, (l.h, l.yb))
        self.send("c", n, chip, (l.o, l.b))

    def from_line(self, n):
        l = self.links
        chip = self.chip(l.columns[0], n)
        l.arrived(self.slot(l.h, chip), self.sems["z"], (self.p, l.nth(n)))
        self.own(n)

    def arrived(self, axis, n, chip):
        self.links.arrived(self.slot(self.links.h, chip), self.sems[axis], (self.p, n))

    def from_side(self, axis, n):
        l = self.links
        chip = self.chip(l.columns[1 if axis == "x" else 2], n)
        self.arrived(axis, n, chip)
        if (n % 2 == 0) == (axis == "x"):
            self.send("d", n, chip, (l.h, l.yb if axis == "x" else l.xb))
        self.send("c", (4 if axis == "x" else 8) + n, chip, (l.o, l.b))

    def from_corner(self, n):
        l = self.links
        chip = self.chip(l.columns[3], n)
        self.arrived("d", n, chip)
        self.send("c", 12 + n, chip, (l.o, l.b))

    def stages(self):
        part = functools.partial
        return [
            [part(self.own, 0)],
            [part(self.from_line, 1), part(self.from_side, "x", 0), part(self.from_side, "y", 0), part(self.from_line, 2)],
            [part(self.from_side, axis, 1) for axis in "xy"]
            + [part(self.from_line, 3)]
            + [part(self.from_side, axis, n) for n in (2, 3) for axis in "xy"],
            [part(self.from_corner, n) for n in range(4)],
        ]

    def whole(self):
        l = self.links
        for number in range(16):
            chip = self.chip(l.columns[number // 4], number % 4)
            l.arrived(self.slot(l.o, chip), self.sems["c"], (self.p, number))


class RowSlice:
    def __init__(self, links, ref, sems):
        self.links, self.ref = links, ref
        self.line_sems, self.core_sems = sems

    def slot(self, h, z):
        return rows_at(self.ref, (h * 4 + z) * 128, 128)

    def core(self, k, z):
        l = self.links
        l.send(self.slot(l.h, z), self.slot(l.h, z), self.core_sems, k, (l.o, l.b))

    def own(self, n):
        l = self.links
        z = l.nth(n)
        if n:
            l.pass_on(self.slot(l.h, z), z, self.line_sems, ())
        else:
            l.along(self.slot(l.h, z), self.line_sems, ())
        self.core(n, z)

    def from_line(self, n):
        l = self.links
        z = l.nth(n)
        l.arrived(self.slot(l.h, z), self.line_sems, (z,))
        self.own(n)

    def stages(self):
        part = functools.partial
        return [[part(self.own, 0)], [part(self.from_line, 1)], [part(self.from_line, 2)], [part(self.from_line, 3)]]

    def whole(self):
        l = self.links
        for n in range(4):
            l.arrived(self.slot(l.o, l.nth(n)), self.core_sems, n)


class ColumnSlice:
    def __init__(self, links, ref, stage, sems):
        self.links, self.ref, self.stage = links, ref, stage
        self.plane_sems, self.line_sems, self.core_sems = sems

    def chip(self, j, n):
        return self.links.columns[j] + 4 * self.links.nth(n)

    def slot(self, h, chip):
        return rows_at(self.ref, shard_of(h, chip) * 32, 32)

    def own(self, j, n):
        l = self.links
        piece = self.slot(l.h, self.chip(j, n))
        if n:
            l.pass_on(piece, l.nth(n), self.line_sems, (j,))
        else:
            l.along(piece, self.line_sems, (j,))
        l.send(piece, piece, self.core_sems, (j, n), (l.o, l.b))

    def start(self):
        l = self.links
        for j, chip in enumerate((l.b, l.xb, l.yb, l.db)):
            if j:
                l.send(rows_at(self.stage, j * 32, 32), self.slot(l.h, l.b), self.plane_sems, j, (l.h, chip))

    def from_plane(self, j):
        self.links.arrived(self.slot(self.links.h, self.chip(j, 0)), self.plane_sems, j)
        self.own(j, 0)

    def from_line(self, j, n):
        l = self.links
        l.arrived(self.slot(l.h, self.chip(j, n)), self.line_sems, (j, l.nth(n)))
        self.own(j, n)

    def stages(self):
        part = functools.partial
        return [
            [self.start],
            [part(self.own, 0, 0)] + [part(self.from_plane, j) for j in range(1, 4)],
            [part(self.from_line, j, n) for n in range(1, 4) for j in range(4)],
        ]

    def whole(self):
        l = self.links
        for j in range(4):
            for n in range(4):
                l.arrived(self.slot(l.o, self.chip(j, n)), self.core_sems, (j, n))


def ordered(stages, lag):
    events = []
    deepest = max(len(stage) for stage in stages)
    for tick in range(len(stages) * lag + deepest):
        for n, stage in enumerate(stages):
            if 0 <= tick - n * lag < len(stage):
                events += stage[tick - n * lag]
    return events


class Reduce:
    def __init__(self, links, g, out, base, width, bufs, sems, rows=slice(0, 128)):
        self.l, self.g, self.out, self.base, self.sems = links, g, out, base, sems
        self.by_core, self.by_side, self.by_turn, self.by_line = bufs
        self.half, self.p, self.rows = width // 2, width // 4, rows
        l = links
        self.mine = base + l.h * self.half
        p = self.p
        self.keep1 = (self.mine + l.x * (p // 2), self.mine + p + l.y * (p // 2))
        self.give1 = (self.mine + (1 - l.x) * (p // 2), self.mine + p + (1 - l.y) * (p // 2))
        self.keep2 = (self.keep1[0] + l.y * (p // 4), self.keep1[1] + l.x * (p // 4))
        self.give2 = (self.keep1[0] + (1 - l.y) * (p // 4), self.keep1[1] + (1 - l.x) * (p // 4))

    def at(self, start, width):
        return self.g.at[self.rows, pl.ds(pl.multiple_of(start, 128), width)]

    def out_at(self, start, width):
        return self.out.at[self.rows, pl.ds(pl.multiple_of(start, 128), width)]

    def chunk(self, z):
        first, second = self.keep2
        return first * (1 - z // 2) + second * (z // 2) + lax.rem(z, 2) * (self.p // 8)

    def add(self, start, width, others, final=False):
        tile = 384 if width % 384 == 0 else 128
        for n in range(width // tile):
            here = pl.ds(pl.multiple_of(start + n * tile, 128), tile)
            total = self.g[self.rows, here].astype(F4)
            for other in others:
                total = total + other[:, n * tile : (n + 1) * tile].astype(F4)
            (self.out if final else self.g)[self.rows, here] = total.astype(BF)

    def steps(self):
        l, p = self.l, self.p
        sides, turns = (l.xb, l.yb), (l.yb, l.xb)

        def cores():
            away = self.base + l.o * self.half
            l.send(self.at(away, self.half), self.by_core, self.sems, 0, (l.o, l.b))

        def side():
            l.arrived(self.by_core, self.sems, 0)
            for n in range(2):
                self.add(self.give1[n], p // 2, [self.by_core.at[:, pl.ds(pl.multiple_of(self.give1[n] - self.mine, 128), p // 2)]])
                l.send(self.at(self.give1[n], p // 2), self.by_side.at[n], self.sems, 1 + n, (l.h, sides[n]))
            for n in range(2):
                self.add(self.keep1[n], p // 2, [self.by_core.at[:, pl.ds(pl.multiple_of(self.keep1[n] - self.mine, 128), p // 2)]])

        def turn():
            for n in range(2):
                l.arrived(self.by_side.at[n], self.sems, 1 + n)
                self.add(self.keep1[n], p // 2, [self.by_side.at[n]])
                l.send(self.at(self.give2[n], p // 4), self.by_turn.at[n], self.sems, 3 + n, (l.h, turns[n]))

        def line():
            for n in range(2):
                l.arrived(self.by_turn.at[n], self.sems, 3 + n)
                self.add(self.keep2[n], p // 4, [self.by_turn.at[n]])
            for k in range(1, 4):
                away = self.chunk(lax.rem(l.z + k, 4))
                l.send(self.at(away, p // 8), self.by_line.at[k - 1], self.sems, 4 + k, (l.h, l.ahead(4 * k)))

        def line_back():
            for k in range(1, 4):
                l.arrived(self.by_line.at[k - 1], self.sems, 4 + k)
            self.add(self.chunk(l.z), p // 8, [self.by_line.at[k] for k in range(3)], True)
            here = self.out_at(self.chunk(l.z), p // 8)
            for k in range(1, 4):
                l.send(here, here, self.sems, 7 + k, (l.h, l.ahead(4 * k)))

        def turn_back():
            for k in range(1, 4):
                l.arrived(self.out_at(self.chunk(lax.rem(l.z + 4 - k, 4)), p // 8), self.sems, 7 + k)
            for n in range(2):
                here = self.out_at(self.keep2[n], p // 4)
                l.send(here, here, self.sems, 11 + n, (l.h, turns[n]))

        def side_back():
            for n in range(2):
                l.arrived(self.out_at(self.give2[n], p // 4), self.sems, 11 + n)
                here = self.out_at(self.keep1[n], p // 2)
                l.send(here, here, self.sems, 13 + n, (l.h, sides[n]))

        def cores_back():
            for n in range(2):
                l.arrived(self.out_at(self.give1[n], p // 2), self.sems, 13 + n)
            here = self.out_at(self.mine, self.half)
            l.send(here, here, self.sems, 15, (l.o, l.b))

        def done():
            l.arrived(self.out_at(self.base + l.o * self.half, self.half), self.sems, 15)

        return [cores, side, turn, line, line_back, turn_back, side_back, cores_back, done]


class SliceReduce:
    def __init__(self, links, g, out, base, bufs, sems):
        self.l, self.g, self.out, self.base, self.sems = links, g, out, base, sems
        self.by_core, self.by_line = bufs

    def at(self, ref, start, width):
        return ref.at[:, pl.ds(pl.multiple_of(start, 128), width)]

    def steps(self):
        l = self.l
        chips = (l.b, l.xb, l.yb, l.db)
        places = [
            self.base + 2048 * (lax.rem(chip, 4)) for chip in chips
        ]

        def region(j, h, z=None):
            if z is None:
                return self.at(self.out, places[j] + h * 1024, 1024)
            return self.at(self.out, places[j] + h * 1024 + z * 256, 256)

        def cores():
            l.send(self.at(self.g, l.o * 1024, 1024), self.by_core, self.sems, 0, (l.o, l.b))

        def line():
            l.arrived(self.by_core, self.sems, 0)
            for n in range(4):
                here = pl.ds(pl.multiple_of(l.h * 1024 + n * 256, 128), 256)
                total = self.g[:, here].astype(F4) + self.by_core[:, n * 256 : (n + 1) * 256].astype(F4)
                self.g[:, here] = total.astype(BF)
            for k in range(1, 4):
                z = lax.rem(l.z + k, 4)
                l.send(self.at(self.g, l.h * 1024 + z * 256, 256), self.by_line.at[k - 1], self.sems, k, (l.h, l.ahead(4 * k)))

        def line_back():
            total = self.g[:, pl.ds(pl.multiple_of(l.h * 1024 + l.z * 256, 128), 256)].astype(F4)
            for k in range(1, 4):
                l.arrived(self.by_line.at[k - 1], self.sems, k)
                total = total + self.by_line[k - 1].astype(F4)
            self.out[:, pl.ds(pl.multiple_of(places[0] + l.h * 1024 + l.z * 256, 128), 256)] = total.astype(BF)
            for k in range(1, 4):
                l.send(region(0, l.h, l.z), region(0, l.h, l.z), self.sems, 3 + k, (l.h, l.ahead(4 * k)))

        def plane():
            for k in range(1, 4):
                l.arrived(region(0, l.h, lax.rem(l.z + 4 - k, 4)), self.sems, 3 + k)
            for j in range(1, 4):
                l.send(region(0, l.h), region(0, l.h), self.sems, 6 + j, (l.h, chips[j]))
            l.send(region(0, l.h), region(0, l.h), self.sems, 10, (l.o, l.b))

        def cores_back():
            for j in range(1, 4):
                l.arrived(region(j, l.h), self.sems, 6 + j)
                l.send(region(j, l.h), region(j, l.h), self.sems, 10 + j, (l.o, l.b))

        def done():
            for j in range(4):
                l.arrived(region(j, l.o), self.sems, 10 + j)

        return [cores, line, line_back, plane, cores_back, done]


def shard_of(h, chip):
    return h * CHIPS + chip


def centre(stream):
    average = jnp.mean(stream, axis=-1, keepdims=True)
    centred = stream - average
    variance = jnp.mean(centred * centred, axis=-1, keepdims=True)
    scale = lax.rsqrt(variance + EPSILON)
    return centred * scale, scale


def norm_back(stream, gain, grad):
    hat, scale = centre(stream)
    q = grad * gain
    return scale * (
        q - jnp.mean(q, axis=-1, keepdims=True) - hat * jnp.mean(q * hat, axis=-1, keepdims=True)
    )


def gelu_parts(u):
    cubic = 0.044715 * u * u
    slope = math.sqrt(2.0 / math.pi)
    t = jnp.tanh(slope * u * (1.0 + cubic))
    grown = 0.5 * (1.0 + t)
    return u * grown, grown + 0.5 * u * (1.0 - t * t) * slope * (1.0 + 3.0 * cubic)


PIECES = 5
MIXER_D, MIXER_U, EXPAND_D, REDUCE_U, TRIPLE_D, TRIPLE_U, SLICES, COLUMNS = (
    0, 1024, 2048, 3072, 4096, 5120, 8192, 16384,
)

INPUTS = (
    "hidden", "cot", "sel", "small_sh", "triple_sh", "mixer_sh", "reduce_sh", "expand_sh",
    "down_t", "up_t", "down_m", "up_m", "down_e", "up_e", "down_r", "up_r",
)
OUTPUTS = {"layer_out": ((128, 1024), BF), "hidden_grad": ((128, 1024), BF), "g": ((128, COLUMNS), BF)}
SCRATCH = {
    "wt": ((1024, 3072), BF), "wm": ((1024, 1024), BF), "wr": ((1024, 1024), BF), "we": ((1024, 1024), BF),
    "e_in": ((32, 4096), BF), "e_stage": ((128, 1024), BF), "up_es": ((128, 1024), BF), "down_rs": ((128, 1024), BF), "bias_es": ((1, 1024), F4),
    "small": ((512, 128), BF), "vecs": ((16, 1024), F4), "bias_t": ((1, 3072), F4), "bias_e": ((1, 4096), F4),
    "fn": ((128, 1024), BF), "rank_t": ((128, 128), BF), "kv": ((4096, 128), BF), "q": ((2048, 128), BF),
    "attden": ((2048, 128), F4), "attended": ((128, 1024), BF), "ones_v": ((4096, 128), BF),
    "send_kv": ((2048, 128), BF), "send_q": ((1024, 128), BF), "recv_q": ((1024, 128), BF),
    "send_a": ((1024, 128), BF), "recv_a": ((1024, 128), BF),
    "residual": ((128, 1024), F4), "sn_all": ((512, 1152), BF), "cot_all": ((512, 1152), BF),
    "act": ((512, 1024), BF), "agrad": ((512, 1024), BF), "ng_part": ((512, 1152), BF), "ng_recv": ((512, 1152), BF),
    "red_part": ((512, 1152), BF), "red_recv": ((512, 1152), BF),
    "send_g": ((1024, 128), BF), "recv_g": ((1024, 128), BF),
    "qd": ((2048, 128), BF), "dz": ((2048, 128), BF), "vz": ((4096, 128), BF),
    "k_t": ((64, 4096), BF), "ddrow": ((1, 2048), F4), "dq_t": ((128, 2048), F4), "part": ((4096, 128), F4),
    "recv_part": ((2048, 128), F4), "send_dkv": ((2048, 128), BF), "send_dq": ((1024, 128), BF),
    "recv_dkv": ((2048, 128), BF), "recv_dq": ((1024, 128), BF), "jg": ((128, 3072), BF),
"gp": ((128, SLICES), BF), "gs": ((128, 2048), BF), "slice_c": ((128, 1024), BF), "slice_l": ((3, 128, 256), BF),
    "early_c": ((128, 2048), BF), "early_1": ((2, 128, 512), BF), "early_2": ((2, 128, 256), BF), "early_3": ((3, 128, 128), BF),
    "late_c": ((2, 64, 2048), BF), "late_1": ((2, 2, 64, 512), BF), "late_2": ((2, 2, 64, 256), BF), "late_3": ((2, 3, 64, 128), BF),
}
SEMS = {
    "z": (PIECES, 4), "x": (PIECES, 4), "y": (PIECES, 4), "d": (PIECES, 4), "c": (PIECES, 16),
    "kv": (16,), "q": (16,), "f": (16,), "a": (16,), "g": (16,), "e": (16,), "dkv": (16,), "dq": (16,),
    "early": (16,), "late": (16,), "late_two": (16,), "slice": (16,),
    "rz": (4,), "rc": (4,), "ep": (4,), "ez": (4, 4), "ec": (4, 4), "ct": (2, 4), "sn": (2, 4), "ng": (2, 4), "rd": (2, 4),
}


def layer_kernel(*refs):
    names = list(INPUTS) + list(OUTPUTS) + list(SCRATCH)
    r = types.SimpleNamespace(**dict(zip(names, refs)))
    rest = refs[len(names) :]
    local_sem = rest[0]
    sems = {name: (rest[1 + 2 * n], rest[2 + 2 * n]) for n, name in enumerate(SEMS)}
    l = Links()
    low, low64 = half_mask(128), half_mask(64)
    mine = shard_of(l.h, l.b)
    local_copies = [
        pltpu.make_async_copy(r.small_sh, rows_at(r.small, mine * 16, 16), local_sem.at[0]),
        pltpu.make_async_copy(r.triple_sh, rows_at(r.wt, mine * 32, 32), local_sem.at[1]),
        pltpu.make_async_copy(r.mixer_sh, rows_at(r.wm, mine * 32, 32), local_sem.at[2]),
        pltpu.make_async_copy(r.reduce_sh, rows_at(r.wr, (l.h * 4 + l.z) * 128, 128), local_sem.at[3]),
        pltpu.make_async_copy(r.expand_sh, r.e_in, local_sem.at[4]),
    ]
    for copy in local_copies:
        copy.start()
    l.greet()

    def columns(ref, at):
        return lambda h, chip: ref.at[
            pl.ds(pl.multiple_of(shard_of(h, chip) * 32, 32), 32), at : at + 1024
        ]

    slots = [lambda h, chip: rows_at(r.small, shard_of(h, chip) * 16, 16)]
    slots += [columns(r.wt, m * 1024) for m in range(3)]
    slots += [columns(r.wm, 0)]
    pieces = [Gather(l, n, slot, sems) for n, slot in enumerate(slots)]
    pieces.append(RowSlice(l, r.wr, (sems["rz"], sems["rc"])))
    pieces.append(ColumnSlice(l, r.we, r.e_stage, (sems["ep"], sems["ez"], sems["ec"])))
    places = [lax.rem(chip, 4) for chip in (l.b, l.xb, l.yb, l.db)]

    def block(j, i):
        return pl.ds(pl.multiple_of((i // 4 * 16 + places[j] + i % 4 * 4) * 128, 128), 128)

    for i in range(8):
        here = slice(i * 128, (i + 1) * 128)
        r.up_es[:, here] = r.up_e[:, block(0, i)]
        r.down_rs[:, here] = r.down_r[:, block(0, i)]
    for copy in local_copies:
        copy.wait()
    for i in range(8):
        here = slice(i * 128, (i + 1) * 128)
        r.we[pl.ds(pl.multiple_of(mine * 32, 32), 32), here] = r.e_in[:, block(0, i)]
        for j in range(1, 4):
            r.e_stage[j * 32 : (j + 1) * 32, here] = r.e_in[:, block(j, i)]
    l.met()
    stages = [piece.stages() for piece in pieces]
    events = [event for n in (0, 1, 2, 3, 6) for event in stages[n].pop(0)]
    stages[2][1] += stages[5].pop(0)
    events += ordered(stages[:4], 1)
    ends = {n: len(events) for n in range(4)}
    events += stages[4].pop(0)
    begun = len(events)
    events += stages[6].pop(0)
    crossed = len(events) + 8
    events += [event for stage in stages[4] for event in stage]
    ends[4] = len(events)
    events += [event for stage in stages[5] for event in stage]
    ends[5] = len(events)
    events += [event for stage in stages[6] for event in stage]
    ends[6] = len(events)
    state = [0]

    def pump(count):
        until(state[0] + count)

    def until(end):
        end = min(end, len(events))
        while state[0] < end:
            events[state[0]]()
            state[0] += 1

    def need(first, last):
        until(ends[last])
        for n in range(first, last + 1):
            pieces[n].whole()

    until(ends[3] - 4)
    pieces[0].whole()
    for g in range(8):
        tile = jnp.zeros((16, 128), F4)
        for n in range(4):
            at = (4 * g + n) * 16
            tile = tile + r.small[at : at + 16, :].astype(F4)
        r.vecs[:, g * 128 : (g + 1) * 128] = tile
        for n in range(3):
            at = (g * 3 + n) * 128
            r.bias_t[0:1, at : at + 128] = tile[6 + n : 7 + n, :]
        for n in range(4):
            at = (g * 4 + n) * 128
            r.bias_e[0:1, at : at + 128] = tile[9 + n : 10 + n, :]
    gain_one, bias_one, bias_m, gain_two, bias_two, bias_r = [
        (lambda n=n: r.vecs[n : n + 1, :]) for n in range(6)
    ]
    hat, _ = centre(r.hidden[...].astype(F4))
    r.fn[...] = (hat * gain_one() + bias_one()).astype(BF)

    def rank(source, down):
        return (r.sel[...] * by_transpose(source, down)).astype(BF)

    r.rank_t[...] = rank(r.fn[...], r.down_t[...])
    need(1, 3)
    until(begun)

    own = l.b * 256 + l.h * 128

    def kv_at(chip, h):
        return rows_at(r.kv, chip * 256 + h * 128, 128)

    kv_out = Exchange(l, r.send_kv, r.kv, 128, sems["kv"], lambda chip: kv_at(chip, l.h))
    q_out = Exchange(l, r.send_q, r.recv_q, 64, sems["q"])
    for step in range(4):
        plane = lax.rem(l.z + 1 + step, 4)

        def joint(part):
            at = pl.ds(pl.multiple_of(part * 1024 + plane * 256, 256), 256)
            tile = (
                product(r.fn[...], r.wt[:, at]) + r.bias_t[0:1, at] + product(r.rank_t[...], r.up_t[:, at])
            )
            return tile[:, :128], tile[:, 128:]

        for n, (qt, kt, vt) in enumerate(zip(joint(0), joint(1), joint(2))):
            c = plane * 4 + n * 2
            send_kv, send_q = rows_at(r.send_kv, c * 128, 256), rows_at(r.send_q, c * 64, 128)
            send_kv[0:128, :] = jnp.where(low, kt, swap(vt)).astype(BF)
            send_kv[128:256, :] = jnp.where(low, swap(kt), vt).astype(BF)
            qt = qt.astype(BF).astype(F4) * 0.125
            turned = swap(qt)
            send_q[0:64, :] = jnp.where(low64, qt[:64], turned[64:]).astype(BF)
            send_q[64:128, :] = jnp.where(low64, turned[:64], qt[64:]).astype(BF)
        for n in range(4):
            kv_out.send(plane * 4 + n)
            q_out.send(plane * 4 + n)
    kv_out.own()
    q_out.own()
    until(crossed)
    rank_grad_r = rank(r.cot[...], r.up_r[...])
    for i in range(8):
        r.bias_es[0:1, i * 128 : (i + 1) * 128] = r.bias_e[0:1, block(0, i)]

    def to_plane(source, target, name, half, own):
        for j, chip in ((3, l.db), (1, l.xb), (2, l.yb)):
            part = rows_at(source, half * 256 + (0 if own else j * 64), 64)
            l.send(part, rows_at(target, half * 256 + j * 64, 64), sems[name], (half, j), (l.h, chip))

    def from_plane(target, name, half):
        for j in range(1, 4):
            l.arrived(rows_at(target, half * 256 + j * 64, 64), sems[name], (half, j))

    def keep_own(target, at, tile):
        target[0:64, at] = tile[:64]
        target[256:320, at] = tile[64:]

    all_columns, ranks = slice(0, 1024), slice(1024, 1152)
    keep_own(r.cot_all, all_columns, r.cot[...])
    keep_own(r.cot_all, ranks, rank_grad_r)
    l.send(kv_at(l.b, l.h), kv_at(l.b, l.h), sems["f"], 0, (l.o, l.b))
    for k in range(1, CHIPS):
        kv_out.wait(k)
        c = l.behind(k)
        l.send(kv_at(c, l.h), kv_at(c, l.h), sems["f"], k, (l.o, l.b))
        until(min(state[0] + 1, ends[4]))
    to_plane(r.cot_all, r.cot_all, "ct", 0, True)
    to_plane(r.cot_all, r.cot_all, "ct", 1, True)
    until(ends[5])
    for k in range(1, CHIPS):
        q_out.wait(k)
    for k in range(CHIPS):
        l.arrived(kv_at(l.behind(k), l.o), sems["f"], k)

    for n in range(CHIPS):
        tile = r.recv_q[n * 64 : n * 64 + 64, :].astype(F4)
        r.q[n * 128 : n * 128 + 64, :] = jnp.where(low64, tile, 0.0).astype(BF)
        r.q[n * 128 + 64 : n * 128 + 128, :] = jnp.where(low64, swap(tile), 0.0).astype(BF)
        tile = r.kv[n * 256 : n * 256 + 256, :].astype(F4)
        r.ones_v[n * 256 : n * 256 + 256, :] = jnp.where(half_mask(256), 1.0, tile).astype(BF)
    a_out = Exchange(l, r.send_a, r.recv_a, 64, sems["a"])
    for i in range(8):
        queries = r.q[i * 256 : (i + 1) * 256, :]

        def fold(jj, total, masked=False):
            at = pl.ds(pl.multiple_of(jj * 512, 512), 512)
            powers = jnp.exp(by_transpose(queries, r.kv[at, :]))
            if masked:
                row = lax.broadcasted_iota(jnp.int32, (256, 512), 0)
                column = lax.broadcasted_iota(jnp.int32, (256, 512), 1)
                powers = jnp.where((row >= 128) | (column < 256), powers, 0.0)
            return total + product(powers.astype(BF), r.ones_v[at, :])

        total = fold(i, jnp.zeros((256, 128), F4), True)
        if i:
            total = lax.fori_loop(0, i, fold, total)
        share = total / swap(total)
        r.attden[i * 256 : (i + 1) * 256, :] = jnp.where(half_mask(256), total, share)
        for n in range(2):
            t = 2 * i + n
            part = share[n * 128 : n * 128 + 128]
            packed = jnp.where(low64, swap(part[64:]), part[:64]).astype(BF)
            r.send_a[t * 64 : t * 64 + 64, :] = packed
            a_out.send(t)
    a_out.own()
    until(ends[6])
    need(4, 4)
    for k in range(1, CHIPS):
        a_out.wait(k)
    for p in range(8):
        one = r.recv_a[p * 128 : p * 128 + 64, :].astype(F4)
        two = r.recv_a[p * 128 + 64 : p * 128 + 128, :].astype(F4)
        at = p * 128
        r.attended[0:64, at : at + 128] = jnp.where(low64, swap(one), two).astype(BF)
        r.attended[64:128, at : at + 128] = jnp.where(low64, one, swap(two)).astype(BF)

    rank_m = rank(r.attended[...], r.down_m[...])
    r.residual[...] = (
        r.hidden[...].astype(F4)
        + product(r.attended[...], r.wm[...])
        + bias_m()
        + product(rank_m, r.up_m[...])
    )
    hat, _ = centre(r.residual[...])
    second_normed = (hat * gain_two() + bias_two()).astype(BF)
    rank_e = rank(second_normed, r.down_e[...])
    keep_own(r.sn_all, all_columns, second_normed)
    keep_own(r.sn_all, ranks, rank_e)
    to_plane(r.sn_all, r.sn_all, "sn", 0, True)
    to_plane(r.sn_all, r.sn_all, "sn", 1, True)

    def tile_at(n, width):
        return pl.ds(pl.multiple_of(n * width, width), width)

    need(5, 6)
    from_plane(r.cot_all, "ct", 0)
    from_plane(r.cot_all, "ct", 1)

    def grad_tile(n, carry):
        at = tile_at(n, 256)
        r.agrad[:, at] = (
            by_transpose(r.cot_all[:, :1024], r.wr[at, :]) + product(r.cot_all[:, 1024:], r.down_rs[:, at])
        ).astype(BF)
        return carry

    lax.fori_loop(0, 4, grad_tile, 0)
    for half in range(2):
        from_plane(r.sn_all, "sn", half)
        these = slice(half * 256, half * 256 + 256)

        def inner_tile(n, carry):
            at = tile_at(n, 256)
            expanded = (
                product(r.sn_all[these, :1024], r.we[:, at])
                + r.bias_es[0:1, at]
                + product(r.sn_all[these, 1024:], r.up_es[:, at])
            )
            value, slope = gelu_parts(expanded)
            r.act[these, at] = value.astype(BF)
            r.agrad[these, at] = (r.agrad[these, at].astype(F4) * slope).astype(BF)
            return carry

        lax.fori_loop(0, 4, inner_tile, 0)

        def normed_tile(n, carry):
            at = tile_at(n, 256)
            r.ng_part[these, at] = by_transpose(r.agrad[these, :], r.we[at, :]).astype(BF)
            return carry

        lax.fori_loop(0, 4, normed_tile, 0)
        r.ng_part[these, 1024:] = by_transpose(r.agrad[these, :], r.up_es[...]).astype(BF)
        to_plane(r.ng_part, r.ng_recv, "ng", half, False)
    def flipped(tile):
        return tile.astype(F4).T.astype(BF)

    def reduce_tile(n, carry):
        at = tile_at(n, 256)
        r.red_part[:, at] = product(r.act[...], r.wr[:, at]).astype(BF)
        return carry

    lax.fori_loop(0, 4, reduce_tile, 0)
    r.red_part[:, 1024:] = by_transpose(r.act[...], r.down_rs[...]).astype(BF)
    rank_e_t, rank_grad_r_t = flipped(r.sn_all[:, 1024:]), flipped(r.cot_all[:, 1024:])
    for n in range(4):
        at = slice(n * 256, (n + 1) * 256)
        for kind, tile in enumerate((product(rank_e_t, r.agrad[:, at]), product(rank_grad_r_t, r.act[:, at]))):
            for m in range(2):
                to = (n * 2 + m) * 256 + kind * 128
                r.gs[:, to : to + 128] = tile[:, m * 128 : (m + 1) * 128].astype(BF)
    sliced = SliceReduce(l, r.gs, r.g, SLICES, (r.slice_c, r.slice_l), sems["slice"]).steps()
    sliced.pop(0)()
    from_plane(r.ng_recv, "ng", 0)
    from_plane(r.ng_recv, "ng", 1)

    def plane_sum(part, received, at):
        halves = []
        for start in (0, 256):
            total = part[start : start + 64, at].astype(F4)
            for j in range(1, 4):
                total = total + received[start + j * 64 : start + j * 64 + 64, at].astype(F4)
            halves.append(total)
        return jnp.concatenate(halves, axis=0)

    rank_grad_e = (r.sel[...] * plane_sum(r.ng_part, r.ng_recv, ranks)).astype(BF)
    normed_grad = plane_sum(r.ng_part, r.ng_recv, all_columns) + product(rank_grad_e, r.down_e[...])
    back_two = norm_back(r.residual[...], gain_two(), normed_grad)
    residual_grad = r.cot[...].astype(F4) + back_two
    mixed_grad = residual_grad.astype(BF)
    rank_grad_m = rank(mixed_grad, r.up_m[...])
    g_out = Exchange(l, r.send_g, r.recv_g, 64, sems["g"])
    for step in range(4):
        plane = lax.rem(l.z + 1 + step, 4)
        at = pl.ds(pl.multiple_of(plane * 256, 256), 256)
        both = by_transpose(mixed_grad, r.wm[at, :]) + product(rank_grad_m, r.down_m[:, at])
        for n in range(2):
            tile = both[:, n * 128 : n * 128 + 128]
            turned = swap(tile)
            send_g = rows_at(r.send_g, (plane * 4 + n * 2) * 64, 128)
            send_g[0:64, :] = jnp.where(low64, tile[64:], turned[:64]).astype(BF)
            send_g[64:128, :] = jnp.where(low64, turned[64:], tile[:64]).astype(BF)
        for n in range(4):
            g_out.send(plane * 4 + n)
    g_out.own()

    to_plane(r.red_part, r.red_recv, "rd", 0, False)
    to_plane(r.red_part, r.red_recv, "rd", 1, False)

    def adapter(at, left, right, width):
        for n in range(width // 512):
            r.gp[:, at + n * 512 : at + (n + 1) * 512] = product(left, right[:, n * 512 : (n + 1) * 512]).astype(BF)

    adapter(MIXER_D, flipped(rank_grad_m), r.attended, 1024)
    adapter(MIXER_U, flipped(rank_m), mixed_grad, 1024)
    adapter(EXPAND_D, flipped(rank_grad_e), second_normed, 1024)
    early = Reduce(l, r.gp, r.g, 0, TRIPLE_D, (r.early_c, r.early_1, r.early_2, r.early_3), sems["early"]).steps()

    def finish_output():
        from_plane(r.red_recv, "rd", 0)
        from_plane(r.red_recv, "rd", 1)
        rank_r = (r.sel[...] * plane_sum(r.red_part, r.red_recv, ranks)).astype(BF)
        reduced = plane_sum(r.red_part, r.red_recv, all_columns)
        r.layer_out[...] = (r.residual[...] + reduced + bias_r() + product(rank_r, r.up_r[...])).astype(BF)
        adapter(REDUCE_U, flipped(rank_r), r.cot, 1024)
        r.residual[...] = residual_grad
        early.pop(0)()

    for n in range(CHIPS):
        tile = r.kv[n * 256 : n * 256 + 256, :].astype(F4)
        wide = half_mask(256)
        r.ones_v[n * 256 : n * 256 + 256, :] = jnp.where(wide, tile, 0.0).astype(BF)
        r.vz[n * 256 : n * 256 + 256, :] = jnp.where(wide, 0.0, tile).astype(BF)
        r.k_t[:, n * 256 : n * 256 + 256] = tile.T[:64, :].astype(BF)
    r.dq_t[...] = jnp.zeros((128, 2048), F4)
    for k in range(1, CHIPS):
        g_out.wait(k)
    for n in range(CHIPS):
        at = n * 128
        g = r.recv_g[n * 64 : n * 64 + 64, :].astype(F4)
        both = r.attden[at : at + 128, :]
        grad = jnp.concatenate([g, swap(g)], axis=0)
        numer = jnp.where(low, 0.0, grad / swap(both))
        numer_low = numer.astype(BF)
        r.dz[at : at + 128, :] = numer_low
        r.qd[at : at + 128, :] = jnp.where(
            low, r.q[at : at + 128, :].astype(F4), numer_low.astype(F4)
        ).astype(BF)
        term = jnp.where(low, 0.0, numer * both)
        row = -jnp.sum(term.T, axis=0, keepdims=True)
        r.ddrow[0:1, at : at + 128] = row.astype(BF).astype(F4)
    dkv_out = Exchange(l, r.send_dkv, r.recv_dkv, 128, sems["dkv"])
    dq_out = Exchange(l, r.send_dq, r.recv_dq, 64, sems["dq"])

    def exchange(jj):
        for n in range(2):
            t = 2 * jj + n
            l.send(rows_at(r.part, t * 256 + l.o * 128, 128), rows_at(r.recv_part, t * 128, 128), sems["e"], t, (l.o, l.b))

    def finish(jj):
        for n in range(2):
            t = 2 * jj + n
            l.arrived(rows_at(r.recv_part, t * 128, 128), sems["e"], t)
            here = r.part[pl.ds(pl.multiple_of(t * 256 + l.h * 128, 128), 128), :]
            r.send_dkv[t * 128 : t * 128 + 128, :] = (here + r.recv_part[t * 128 : t * 128 + 128, :]).astype(BF)
            dkv_out.send(t)

    def finish_queries(i):
        for t in (2 * i, 2 * i + 1):
            y = r.dq_t[:, t * 128 : t * 128 + 128].T * 0.125
            r.send_dq[t * 64 : t * 64 + 64, :] = jnp.where(low64, y[:64], swap(y[64:])).astype(BF)
            dq_out.send(t)

    order = (4, 0, 5, 1, 6, 2, 7, 3)
    queries_sent = 0
    for place, jj in enumerate(order):
        keys = slice(jj * 512, jj * 512 + 512)

        def fold_back(i, total, masked=False):
            at = tile_at(i, 256)
            both = r.qd[at, :]
            powers = jnp.exp(by_transpose(r.ones_v[keys, :], both))
            if masked:
                row = lax.broadcasted_iota(jnp.int32, (512, 256), 0)
                column = lax.broadcasted_iota(jnp.int32, (512, 256), 1)
                powers = jnp.where((row < 256) | (column >= 128), powers, 0.0)
            prob = by_transpose(r.vz[keys, :], both) + r.ddrow[0:1, at]
            score = (powers * prob).astype(BF)
            r.dq_t[0:64, at] += product(r.k_t[:, keys], score)
            return total + product(score, r.q[at, :]) + product(powers.astype(BF), r.dz[at, :])

        total = fold_back(jj, jnp.zeros((512, 128), F4), True)
        if jj < 7:
            total = lax.fori_loop(jj + 1, 8, fold_back, total)
        r.part[keys, :] = total
        exchange(jj)
        if place:
            finish(order[place - 1])
        while queries_sent < 8 and all(n in order[: place + 1] for n in range(queries_sent + 1)):
            finish_queries(queries_sent)
            queries_sent += 1
        if place == 1:
            finish_output()
        for steps in {0: [sliced], 2: [sliced, early], 4: [early], 5: [sliced], 7: [early]}.get(place, []):
            steps.pop(0)()
    finish(order[-1])
    dkv_out.own()
    dq_out.own()
    for k in range(1, CHIPS):
        dkv_out.wait(k)
        dq_out.wait(k)
    for p in range(8):
        at = p * 128
        one = r.recv_dq[p * 128 : p * 128 + 64, :].astype(F4)
        two = r.recv_dq[p * 128 + 64 : p * 128 + 128, :].astype(F4)
        r.jg[0:64, at : at + 128] = jnp.where(low64, one, swap(two)).astype(BF)
        r.jg[64:128, at : at + 128] = jnp.where(low64, swap(one), two).astype(BF)
        one = r.recv_dkv[p * 256 : p * 256 + 128, :].astype(F4)
        two = r.recv_dkv[p * 256 + 128 : p * 256 + 256, :].astype(F4)
        r.jg[:, 1024 + at : 1152 + at] = jnp.where(low, one, swap(two)).astype(BF)
        r.jg[:, 2048 + at : 2176 + at] = jnp.where(low, swap(one), two).astype(BF)

    rank_grad_t = rank(r.jg[...], r.up_t[...])
    adapter(TRIPLE_D, flipped(rank_grad_t), r.fn, 1024)
    adapter(TRIPLE_U, flipped(r.rank_t[...]), r.jg, 3072)
    halves = [
        Reduce(
            l, r.gp, r.g, TRIPLE_D, SLICES - TRIPLE_D,
            [buf.at[n] for buf in (r.late_c, r.late_1, r.late_2, r.late_3)],
            sems[("late", "late_two")[n]], slice(n * 64, n * 64 + 64),
        ).steps()
        for n in range(2)
    ]
    late = [step for pair in zip(*halves) for step in pair]
    for _ in range(4):
        late.pop(0)()

    def triple_tile(n, carry):
        at = tile_at(n, 512)
        return carry + by_transpose(r.jg[:, at], r.wt[:, at])

    normed_grad = lax.fori_loop(0, 6, triple_tile, product(rank_grad_t, r.down_t[...]))
    back_one = norm_back(r.hidden[...].astype(F4), gain_one(), normed_grad)
    r.hidden_grad[...] = (r.residual[...] + back_one).astype(BF)
    while late or early or sliced:
        for rest in (late, late, early, sliced):
            if rest:
                rest.pop(0)()
    for out in (kv_out, q_out, a_out, g_out, dkv_out, dq_out):
        out.settle()
    l.settle()


def layer(*arrays):
    vmem = pl.BlockSpec(memory_space=pltpu.VMEM)
    hbm = pl.BlockSpec(memory_space=pl.ANY)
    dma = pltpu.SemaphoreType.DMA
    return pl.pallas_call(
        layer_kernel,
        name="layer",
        in_specs=[hbm if name.endswith("_sh") else vmem for name in INPUTS],
        out_shape=[jax.ShapeDtypeStruct(*OUTPUTS[name]) for name in OUTPUTS],
        out_specs=[vmem] * len(OUTPUTS),
        scratch_shapes=[pltpu.VMEM(*SCRATCH[name]) for name in SCRATCH]
        + [dma((5,))]
        + [dma(SEMS[name]) for name in SEMS for _ in range(2)],
        compiler_params=pltpu.CompilerParams(
            collective_id=0, has_side_effects=True, vmem_limit_bytes=LIMIT
        ),
    )(*arrays)


WRITTEN = (1024, 3072, 1024, 1024, 1024, 4096, 4096, 1024)


def write_kernel(layer_in, hidden_in, g, layer_out, hidden_out, td, tu, md, mu, ed, eu, rd, ru, low, high, in_sem, out_sem):
    passed = [
        pltpu.make_async_copy(layer_in, layer_out, out_sem.at[0]),
        pltpu.make_async_copy(hidden_in, hidden_out, out_sem.at[1]),
    ]
    reads = [
        pltpu.make_async_copy(
            g.at[:, n * 2048 : (n + 1) * 2048], low.at[:, n * 2048 : (n + 1) * 2048], in_sem.at[n]
        )
        for n in range(8)
    ]
    for copy in reads + passed:
        copy.start()
    writes = []

    def write(start, width, target, at):
        copy = pltpu.make_async_copy(
            high.at[:, start : start + width], target.at[:, at : at + width], out_sem.at[2 + len(writes)]
        )
        copy.start()
        writes.append(copy)

    whole = (
        (MIXER_D, 1024, md, 0), (MIXER_U, 1024, mu, 0), (EXPAND_D, 1024, ed, 0), (REDUCE_U, 1024, ru, 0),
        (TRIPLE_D, 1024, td, 0), (TRIPLE_U, 1024, tu, 0), (TRIPLE_U + 1024, 2048, tu, 1024),
    )
    done = 0
    for start, width, target, at in whole:
        while done * 2048 < start + width:
            reads[done].wait()
            done += 1
        high[:, start : start + width] = low[:, start : start + width].astype(F4)
        write(start, width, target, at)
    for n in range(done, 8):
        reads[n].wait()
    for h in range(2):
        for kind, target in enumerate((eu, rd)):
            to = SLICES + (h * 2 + kind) * 2048
            for z in range(4):
                for p in range(4):
                    source = SLICES + p * 2048 + h * 1024 + z * 256 + kind * 128
                    here = to + (z * 4 + p) * 128
                    high[:, here : here + 128] = low[:, source : source + 128].astype(F4)
            write(to, 2048, target, h * 2048)
    for copy in passed + writes:
        copy.wait()


def written(layer_out, hidden_grad, g):
    hbm = pl.BlockSpec(memory_space=pl.ANY)
    dma = pltpu.SemaphoreType.DMA
    return pl.pallas_call(
        write_kernel,
        name="written",
        in_specs=[hbm] * 3,
        out_shape=[jax.ShapeDtypeStruct((128, 1024), BF)] * 2 + [jax.ShapeDtypeStruct((128, width), F4) for width in WRITTEN],
        out_specs=[hbm] * 10,
        scratch_shapes=[pltpu.VMEM((128, COLUMNS), BF), pltpu.VMEM((128, COLUMNS), F4), dma((8,)), dma((16,))],
        compiler_params=pltpu.CompilerParams(vmem_limit_bytes=20 * 1024 * 1024),
    )(layer_out, hidden_grad, g)


def small_block(blocks, triple_bias, expand_bias):
    place = lax.rem(shard_of(lax.axis_index("head"), lax.axis_index("blk")), 4)
    lane = jnp.arange(128, dtype=jnp.int32)[None, :]
    six = jnp.where(lane // 32 == place, jnp.tile(jnp.stack(blocks), (1, 4)), 0)
    wide = jnp.arange(384, dtype=jnp.int32)
    three = jnp.where(wide // 96 == place, jnp.tile(triple_bias, 4), 0).reshape(3, 128)
    row = jnp.arange(4, dtype=jnp.int32)[:, None]
    four = jnp.where(row == place, expand_bias[None, :], 0)
    return jnp.concatenate([six, three, four, jnp.zeros((3, 128), BF)], axis=0).astype(BF)


def local_fast(
    hidden, adapter_index, first_gain, first_bias, triple_weight, triple_bias, mixer_weight, mixer_bias,
    second_gain, second_bias, expand_weight, expand_bias, reduce_weight, reduce_bias, triple_down, triple_up,
    mixer_down, mixer_up, expand_down, expand_up, reduce_down, reduce_up, cotangent,
):
    def turned(factor):
        return jnp.transpose(factor, (0, 2, 1)).reshape(ADAPTERS * RANK, factor.shape[1])

    small_sh = small_block(
        [first_gain, first_bias, mixer_bias, second_gain, second_bias, reduce_bias], triple_bias, expand_bias
    )
    layer_out, hidden_grad, g = layer(
        hidden, cotangent, selector(adapter_index), small_sh, triple_weight, mixer_weight, reduce_weight, expand_weight,
        turned(triple_down), flat_up(triple_up), turned(mixer_down), flat_up(mixer_up),
        turned(expand_down), flat_up(expand_up), turned(reduce_down), flat_up(reduce_up),
    )
    layer_out, hidden_grad, *grads = written(layer_out, hidden_grad, g)

    def down_out(part):
        return jnp.transpose(part.reshape(ADAPTERS, RANK, part.shape[1]), (0, 2, 1))

    def up_out(part):
        return part.reshape(ADAPTERS, RANK, part.shape[1])

    shaped = [down_out, up_out, down_out, up_out, down_out, up_out, down_out, up_out]
    return (layer_out, hidden_grad) + tuple(shape(part) for shape, part in zip(shaped, grads))


def solution(mesh):
    placed = (
        P(("blk", "head"), None),
        P(("blk", "head")),
        P(("head", "blk")),
        P(("head", "blk")),
        P(("head", "blk"), None),
        P(("head", "blk")),
        P(("head", "blk"), None),
        P(("head", "blk")),
        P(("head", "blk")),
        P(("head", "blk")),
        P(("head", "blk"), None),
        P(("head", "blk")),
        P(("head", "blk"), None),
        P(("head", "blk")),
        P(),
        P(),
        P(),
        P(),
        P(),
        P(),
        P(),
        P(),
        P(("blk", "head"), None),
    )
    fits = tuple(mesh.shape[name] for name in ("head", "blk")) == (2, CHIPS)
    return jax.shard_map(
        local_fast if fits else local,
        mesh=mesh,
        in_specs=placed,
        out_specs=(
            P(("blk", "head"), None),
            P(("blk", "head"), None),
            P(),
            P(),
            P(),
            P(),
            P(),
            P(),
            P(),
            P(),
        ),
        check_vma=False,
    )
```

```python
import functools
import math
import types

import jax
import jax.numpy as jnp
from jax import lax
from jax.experimental import pallas as pl
from jax.experimental.pallas import tpu as pltpu
from jax.sharding import PartitionSpec as P

WIDTH = 1024
HEADS = 16
HEAD_DIM = 64
RANK = 16
ADAPTERS = 8
BLOCK = 256


EPSILON = 1e-05


def product(left, right):
    return jnp.dot(left, right, preferred_element_type=jnp.float32)


def by_transpose(left, right):
    return lax.dot_general(
        left, right, (((1,), (1,)), ((), ())), preferred_element_type=jnp.float32
    )


def transpose_by(left, right):
    return lax.dot_general(
        left, right, (((0,), (0,)), ((), ())), preferred_element_type=jnp.float32
    )


def layer_norm(stream, scales, offset):
    average = jnp.mean(stream, axis=-1, keepdims=True)
    centred = stream - average
    variance = jnp.mean(centred * centred, axis=-1, keepdims=True)
    return centred * lax.rsqrt(variance + EPSILON) * scales + offset


def selector(adapter_index):
    column = jnp.arange(ADAPTERS * RANK, dtype=jnp.int32) // RANK
    return (adapter_index[:, None] == column[None, :]).astype(jnp.float32)


def flat_down(factor):
    return jnp.transpose(factor, (1, 0, 2)).reshape(factor.shape[1], ADAPTERS * RANK)


def flat_up(factor):
    return factor.reshape(ADAPTERS * RANK, factor.shape[2])


def unflat_down(gradient):
    return jnp.transpose(gradient.reshape(gradient.shape[0], ADAPTERS, RANK), (1, 0, 2))


def unflat_up(gradient):
    return gradient.reshape(ADAPTERS, RANK, gradient.shape[1])


def projected(source, weight, offset, down_flat, up_flat, selection):
    low_rank = (selection * product(source, down_flat)).astype(jnp.bfloat16)
    return (
        product(source, weight) + offset.astype(jnp.float32) + product(low_rank, up_flat),
        low_rank,
    )


def adapter_grads(source, low_rank, out_grad, down_flat, up_flat, selection):
    rank_grad = (selection * by_transpose(out_grad, up_flat)).astype(jnp.bfloat16)
    down_grad = transpose_by(source, rank_grad)
    up_grad = transpose_by(low_rank, out_grad)
    return (down_grad, up_grad, by_transpose(rank_grad, down_flat))


def score_block(queries, keys_block):
    return jnp.einsum("qhd,khd->qhk", queries, keys_block, preferred_element_type=jnp.float32) * (
        1.0 / math.sqrt(HEAD_DIM)
    )


def cut_rows(arrays, trailing):
    length = arrays[0].shape[0]
    block_rows = math.gcd(length, 512)
    repeats = length // block_rows
    shaped = tuple(
        (
            array.reshape((repeats, block_rows) + shape_tail)
            for array, shape_tail in zip(arrays, trailing)
        )
    )
    firsts = jnp.arange(repeats, dtype=jnp.int32) * block_rows
    return (shaped, firsts, block_rows)


def forward_fold(queries, query_places, locate, totals, portion):
    head_count = queries.shape[1]
    query_block = query_places // BLOCK
    last_block = jnp.max(query_block)
    shaped, firsts, block_rows = cut_rows(portion, ((head_count, HEAD_DIM), (head_count, HEAD_DIM)))

    def forward_visiting(carried, packet):
        keys_block, values_block, first_row = packet
        key_places = locate(first_row, block_rows)

        def forward_compute(running):
            numerator, denominator = running
            allowed = (key_places // BLOCK)[None, None, :] <= query_block[:, None, None]
            powers = jnp.where(allowed, jnp.exp(score_block(queries, keys_block)), 0.0)
            numerator = numerator + jnp.einsum(
                "qhk,khd->qhd",
                powers.astype(jnp.bfloat16),
                values_block,
                preferred_element_type=jnp.float32,
            )
            return (numerator, denominator + jnp.sum(powers, axis=-1))

        skipped = jnp.min(key_places) // BLOCK > last_block
        return (lax.cond(skipped, lambda running: running, forward_compute, carried), None)

    return lax.scan(forward_visiting, totals, shaped + (firsts,))[0]


def query_grad_fold(queries, query_places, locate, numer_grad, denom_grad, totals, portion):
    head_count = queries.shape[1]
    query_block = query_places // BLOCK
    last_block = jnp.max(query_block)
    shaped, firsts, block_rows = cut_rows(portion, ((head_count, HEAD_DIM), (head_count, HEAD_DIM)))

    def query_visiting(carried, packet):
        keys_block, values_block, first_row = packet
        key_places = locate(first_row, block_rows)

        def query_compute(running):
            allowed = (key_places // BLOCK)[None, None, :] <= query_block[:, None, None]
            powers = jnp.where(allowed, jnp.exp(score_block(queries, keys_block)), 0.0)
            prob_grad = jnp.einsum(
                "qhd,khd->qhk", numer_grad, values_block, preferred_element_type=jnp.float32
            )
            score_grad = (powers * (prob_grad + denom_grad[:, :, None])).astype(jnp.bfloat16)
            return running + jnp.einsum(
                "qhk,khd->qhd", score_grad, keys_block, preferred_element_type=jnp.float32
            )

        skipped = jnp.min(key_places) // BLOCK > last_block
        return (lax.cond(skipped, lambda running: running, query_compute, carried), None)

    return lax.scan(query_visiting, totals, shaped + (firsts,))[0]


def key_grad_fold(keys_here, values_here, key_places, locate, totals, portion):
    head_count = keys_here.shape[1]
    key_block = key_places // BLOCK
    first_block = jnp.min(key_block)
    shaped, firsts, block_rows = cut_rows(
        portion, ((head_count, HEAD_DIM), (head_count, HEAD_DIM), (head_count,))
    )

    def key_visiting(carried, packet):
        query_rows, numer_rows, denom_rows, first_row = packet
        query_places = locate(first_row, block_rows)

        def key_compute(running):
            keys_grad, values_grad = running
            allowed = key_block[None, None, :] <= (query_places // BLOCK)[:, None, None]
            powers = jnp.where(allowed, jnp.exp(score_block(query_rows, keys_here)), 0.0)
            prob_grad = jnp.einsum(
                "qhd,khd->qhk", numer_rows, values_here, preferred_element_type=jnp.float32
            )
            score_grad = (powers * (prob_grad + denom_rows.astype(jnp.float32)[:, :, None])).astype(
                jnp.bfloat16
            )
            keys_grad = keys_grad + jnp.einsum(
                "qhk,qhd->khd", score_grad, query_rows, preferred_element_type=jnp.float32
            )
            values_grad = values_grad + jnp.einsum(
                "qhk,qhd->khd",
                powers.astype(jnp.bfloat16),
                numer_rows,
                preferred_element_type=jnp.float32,
            )
            return (keys_grad, values_grad)

        skipped = jnp.max(query_places) // BLOCK < first_block
        return (lax.cond(skipped, lambda running: running, key_compute, carried), None)

    return lax.scan(key_visiting, totals, shaped + (firsts,))[0]


def local(
    hidden,
    adapter_index,
    first_gain,
    first_bias,
    triple_weight,
    triple_bias,
    mixer_weight,
    mixer_bias,
    second_gain,
    second_bias,
    expand_weight,
    expand_bias,
    reduce_weight,
    reduce_bias,
    triple_down,
    triple_up,
    mixer_down,
    mixer_up,
    expand_down,
    expand_up,
    reduce_down,
    reduce_up,
    cotangent,
):
    gathered = (
        lax.all_gather(first_gain, ("head", "blk"), axis=0, tiled=True),
        lax.all_gather(first_bias, ("head", "blk"), axis=0, tiled=True),
        lax.all_gather(triple_weight, ("head", "blk"), axis=0, tiled=True),
        lax.all_gather(triple_bias, ("head", "blk"), axis=0, tiled=True),
        lax.all_gather(mixer_weight, ("head", "blk"), axis=0, tiled=True),
        lax.all_gather(mixer_bias, ("head", "blk"), axis=0, tiled=True),
        lax.all_gather(second_gain, ("head", "blk"), axis=0, tiled=True),
        lax.all_gather(second_bias, ("head", "blk"), axis=0, tiled=True),
        lax.all_gather(expand_weight, ("head", "blk"), axis=0, tiled=True),
        lax.all_gather(expand_bias, ("head", "blk"), axis=0, tiled=True),
        lax.all_gather(reduce_weight, ("head", "blk"), axis=0, tiled=True),
        lax.all_gather(reduce_bias, ("head", "blk"), axis=0, tiled=True),
    )
    (
        gain_one,
        bias_one,
        weight_triple,
        bias_triple,
        weight_mixer,
        bias_mixer,
        gain_two,
        bias_two,
        weight_expand,
        bias_expand,
        weight_reduce,
        bias_reduce,
    ) = gathered
    token_count = hidden.shape[0]
    head_ways = lax.axis_size("head")
    cycle_ways = lax.axis_size("blk")
    selection = selector(adapter_index)
    down_triple = flat_down(triple_down)
    upward_triple = flat_up(triple_up)
    down_mixer = flat_down(mixer_down)
    upward_mixer = flat_up(mixer_up)
    down_expand = flat_down(expand_down)
    upward_expand = flat_up(expand_up)
    down_reduce = flat_down(reduce_down)
    upward_reduce = flat_up(reduce_up)
    stream = hidden.astype(jnp.float32)

    def first_norm(values_in):
        return layer_norm(values_in, gain_one.astype(jnp.float32), bias_one.astype(jnp.float32))

    def second_norm(values_in):
        return layer_norm(values_in, gain_two.astype(jnp.float32), bias_two.astype(jnp.float32))

    first_normed = first_norm(stream).astype(jnp.bfloat16)
    joint, rank_triple = projected(
        first_normed, weight_triple, bias_triple, down_triple, upward_triple, selection
    )
    joint = joint.astype(jnp.bfloat16)
    parts = joint.reshape(token_count, 3, HEADS, HEAD_DIM)
    own_shard = lax.axis_index("blk") * head_ways + lax.axis_index("head")
    query_places = own_shard * token_count + jnp.arange(token_count, dtype=jnp.int32)

    def locate(first_row, length):
        rows_here = first_row + jnp.arange(length, dtype=jnp.int32)
        shard_index = rows_here // token_count
        return (
            shard_index % cycle_ways * head_ways + shard_index // cycle_ways
        ) * token_count + rows_here % token_count

    queries = parts[:, 0]
    keys_here = parts[:, 1]
    values_here = parts[:, 2]
    head_count = queries.shape[1]
    flat_keys = keys_here.reshape(token_count, head_count * HEAD_DIM)
    flat_values = values_here.reshape(token_count, head_count * HEAD_DIM)
    zeros_rows = jnp.zeros((token_count, head_count, HEAD_DIM), jnp.float32)
    payload = (flat_keys, flat_values)
    numerator, denominator = forward_fold(
        queries,
        query_places,
        locate,
        (zeros_rows, jnp.zeros((token_count, head_count), jnp.float32)),
        (
            lax.all_gather(payload[0], ("head", "blk"), axis=0, tiled=True),
            lax.all_gather(payload[1], ("head", "blk"), axis=0, tiled=True),
        ),
    )
    attended = numerator / denominator[:, :, None]
    attended_low = attended.astype(jnp.bfloat16).reshape(token_count, WIDTH)
    mixed, rank_mixer = projected(
        attended_low, weight_mixer, bias_mixer, down_mixer, upward_mixer, selection
    )
    residual = stream + mixed
    second_normed = second_norm(residual).astype(jnp.bfloat16)
    expanded, rank_expand = projected(
        second_normed, weight_expand, bias_expand, down_expand, upward_expand, selection
    )
    activated = jax.nn.gelu(expanded, approximate=True).astype(jnp.bfloat16)
    reduced, rank_reduce = projected(
        activated, weight_reduce, bias_reduce, down_reduce, upward_reduce, selection
    )
    layer_out = (residual + reduced).astype(jnp.bfloat16)
    reduce_down_grad, reduce_up_grad, through_reduce = adapter_grads(
        activated, rank_reduce, cotangent, down_reduce, upward_reduce, selection
    )
    activated_grad = (by_transpose(cotangent, weight_reduce) + through_reduce).astype(jnp.bfloat16)
    gelu_back = jax.vjp(lambda values_in: jax.nn.gelu(values_in, approximate=True), expanded)[1]
    expanded_grad = gelu_back(activated_grad.astype(jnp.float32))[0].astype(jnp.bfloat16)
    expand_down_grad, expand_up_grad, through_expand = adapter_grads(
        second_normed, rank_expand, expanded_grad, down_expand, upward_expand, selection
    )
    normed_grad = by_transpose(expanded_grad, weight_expand) + through_expand
    second_back = jax.vjp(second_norm, residual)[1]
    residual_grad = cotangent.astype(jnp.float32) + second_back(normed_grad)[0]
    mixed_grad = residual_grad.astype(jnp.bfloat16)
    mixer_down_grad, mixer_up_grad, through_mixer = adapter_grads(
        attended_low, rank_mixer, mixed_grad, down_mixer, upward_mixer, selection
    )
    attended_grad = (by_transpose(mixed_grad, weight_mixer) + through_mixer).astype(jnp.bfloat16)
    output_grad = attended_grad.reshape(token_count, HEADS, HEAD_DIM).astype(jnp.float32)
    numer_grad = (output_grad / denominator[:, :, None]).astype(jnp.bfloat16)
    denom_grad = (-jnp.sum(output_grad * attended, axis=-1) / denominator).astype(jnp.bfloat16)
    payload = (flat_keys, flat_values)
    query_grad = query_grad_fold(
        queries,
        query_places,
        locate,
        numer_grad,
        denom_grad.astype(jnp.float32),
        zeros_rows,
        (
            lax.all_gather(payload[0], ("head", "blk"), axis=0, tiled=True),
            lax.all_gather(payload[1], ("head", "blk"), axis=0, tiled=True),
        ),
    )
    payload = (
        queries.reshape(token_count, head_count * HEAD_DIM),
        numer_grad.reshape(token_count, head_count * HEAD_DIM),
        denom_grad,
    )
    keys_grad, values_grad = key_grad_fold(
        keys_here,
        values_here,
        query_places,
        locate,
        (zeros_rows, zeros_rows),
        (
            lax.all_gather(payload[0], ("head", "blk"), axis=0, tiled=True),
            lax.all_gather(payload[1], ("head", "blk"), axis=0, tiled=True),
            lax.all_gather(payload[2], ("head", "blk"), axis=0, tiled=True),
        ),
    )
    factor = 1.0 / math.sqrt(HEAD_DIM)
    joint_grad = jnp.stack([query_grad * factor, keys_grad * factor, values_grad], axis=1).astype(
        jnp.bfloat16
    )
    joint_tokens = joint_grad.reshape(token_count, 3 * WIDTH)
    triple_down_grad, triple_up_grad, through_triple = adapter_grads(
        first_normed, rank_triple, joint_tokens, down_triple, upward_triple, selection
    )
    normed_one_grad = by_transpose(joint_tokens, weight_triple) + through_triple
    first_back = jax.vjp(first_norm, stream)[1]
    hidden_grad = (residual_grad + first_back(normed_one_grad)[0]).astype(jnp.bfloat16)
    summed = lax.psum(
        (
            triple_down_grad,
            triple_up_grad,
            mixer_down_grad,
            mixer_up_grad,
            expand_down_grad,
            expand_up_grad,
            reduce_down_grad,
            reduce_up_grad,
        ),
        ("head", "blk"),
    )
    return (
        layer_out,
        hidden_grad,
        unflat_down(summed[0]),
        unflat_up(summed[1]),
        unflat_down(summed[2]),
        unflat_up(summed[3]),
        unflat_down(summed[4]),
        unflat_up(summed[5]),
        unflat_down(summed[6]),
        unflat_up(summed[7]),
    )


MESH = pl.DeviceIdType.MESH
CHIPS = 16
LIMIT = 62 * 1024 * 1024 - 512 * 1024
BF = jnp.bfloat16
F4 = jnp.float32


ALONG = ((0, 1, 2, 3), (1, 0, 2, 3), (2, 1, 3, 0), (3, 2, 1, 0))


class Links:
    def __init__(self):
        self.h = lax.axis_index("head")
        self.b = lax.axis_index("blk")
        self.o = 1 - self.h
        self.sent = []
        self.x = lax.rem(self.b, 2)
        self.y = lax.rem(self.b // 2, 2)
        self.z = self.b // 4
        self.xb = self.b + 1 - 2 * self.x
        self.yb = self.b + 2 - 4 * self.y
        self.db = self.xb + 2 - 4 * self.y
        self.columns = [lax.rem(chip, 4) for chip in (self.b, self.xb, self.yb, self.db)]

    def nth(self, n):
        return sum(jnp.where(self.z == z, table[n], 0) for z, table in enumerate(ALONG))

    def at_line(self, z):
        return lax.rem(self.b, 4) + 4 * z

    def along(self, piece, sems, index):
        for k, wanted in ((1, self.z < 3), (3, self.z > 0), (2, None)):
            where = (piece, piece, sems, index + (self.z,), (self.h, self.ahead(4 * k)))
            if wanted is None:
                self.send(*where)
            else:
                self.send_if(wanted, *where)

    def pass_on(self, piece, z, sems, index):
        wanted = (self.z == 2) & (z == 0) | (self.z == 1) & (z == 3)
        chip = self.columns[0] + 4 * (3 - z)
        self.send_if(wanted, piece, piece, sems, index + (z,), (self.h, chip))

    def ahead(self, k):
        return lax.rem(self.b + k, CHIPS)

    def behind(self, k):
        return lax.rem(self.b + CHIPS - k, CHIPS)

    def greet(self):
        barrier = pltpu.get_barrier_semaphore()
        for k in range(1, CHIPS):
            pl.semaphore_signal(
                barrier, 1, device_id=(self.h, self.ahead(k)), device_id_type=MESH
            )
        pl.semaphore_signal(barrier, 1, device_id=(self.o, self.b), device_id_type=MESH)

    def met(self):
        pl.semaphore_wait(pltpu.get_barrier_semaphore(), CHIPS)

    def copy(self, source, target, sems, at, device):
        return pltpu.make_async_remote_copy(
            src_ref=source,
            dst_ref=target,
            send_sem=sems[0].at[at],
            recv_sem=sems[1].at[at],
            device_id=device,
            device_id_type=MESH,
        )

    def send(self, source, target, sems, at, device):
        copy = self.copy(source, target, sems, at, device)
        copy.start()
        self.sent.append((None, copy))

    def send_if(self, wanted, *where):
        copy = self.copy(*where)
        pl.when(wanted)(copy.start)
        self.sent.append((wanted, copy))

    def arrived(self, target, sems, at):
        self.copy(target, target, sems, at, (self.o, self.b)).wait_recv()

    def settle(self):
        for wanted, copy in self.sent:
            if wanted is None:
                copy.wait_send()
            else:
                pl.when(wanted)(copy.wait_send)
        self.sent = []


class Exchange:
    def __init__(self, links, source, target, rows, sems, slot=None):
        self.links, self.source, self.target = links, source, target
        self.rows, self.sems = rows, sems
        self.slot = slot or (lambda chip: rows_at(target, chip * rows, rows))

    def send(self, t):
        l = self.links

        @pl.when(l.b != t)
        def _():
            l.copy(
                rows_at(self.source, t * self.rows, self.rows),
                self.slot(l.b), self.sems, lax.rem(t + CHIPS - l.b, CHIPS), (l.h, t),
            ).start()

    def own(self):
        l = self.links
        copy = pltpu.make_async_copy(
            rows_at(self.source, l.b * self.rows, self.rows), self.slot(l.b), self.sems[0].at[0]
        )
        copy.start()
        copy.wait()

    def wait(self, k):
        self.links.arrived(self.slot(self.links.behind(k)), self.sems, k)

    def settle(self):
        for k in range(1, CHIPS):
            l = self.links
            part = rows_at(self.source, l.ahead(k) * self.rows, self.rows)
            l.copy(part, part, self.sems, k, (l.h, l.ahead(k))).wait_send()


def half_mask(rows):
    return lax.broadcasted_iota(jnp.int32, (rows, 128), 1) < 64


def swap(tile):
    return pltpu.roll(tile, 64, 1)


def rows_at(ref, start, count):
    return ref.at[pl.ds(pl.multiple_of(start, 16), count), :]


class Gather:
    def __init__(self, links, number, slot, sems):
        self.links, self.p, self.slot = links, number, slot
        self.sems = sems

    def send(self, axis, n, chip, device):
        piece = self.slot(self.links.h, chip)
        self.links.send(piece, piece, self.sems[axis], (self.p, n), device)

    def chip(self, side, n):
        return side + 4 * self.links.nth(n)

    def own(self, n):
        l = self.links
        chip = self.chip(l.columns[0], n)
        if n:
            l.pass_on(self.slot(l.h, chip), l.nth(n), self.sems["z"], (self.p,))
        else:
            l.along(self.slot(l.h, chip), self.sems["z"], (self.p,))
        self.send("x", n, chip, (l.h, l.xb))
        self.send("y", n, chip, (l.h, l.yb))
        self.send("c", n, chip, (l.o, l.b))

    def from_line(self, n):
        l = self.links
        chip = self.chip(l.columns[0], n)
        l.arrived(self.slot(l.h, chip), self.sems["z"], (self.p, l.nth(n)))
        self.own(n)

    def arrived(self, axis, n, chip):
        self.links.arrived(self.slot(self.links.h, chip), self.sems[axis], (self.p, n))

    def from_side(self, axis, n):
        l = self.links
        chip = self.chip(l.columns[1 if axis == "x" else 2], n)
        self.arrived(axis, n, chip)
        if (n % 2 == 0) == (axis == "x"):
            self.send("d", n, chip, (l.h, l.yb if axis == "x" else l.xb))
        self.send("c", (4 if axis == "x" else 8) + n, chip, (l.o, l.b))

    def from_corner(self, n):
        l = self.links
        chip = self.chip(l.columns[3], n)
        self.arrived("d", n, chip)
        self.send("c", 12 + n, chip, (l.o, l.b))

    def stages(self):
        part = functools.partial
        return [
            [part(self.own, 0)],
            [part(self.from_line, 1), part(self.from_side, "x", 0), part(self.from_side, "y", 0), part(self.from_line, 2)],
            [part(self.from_side, axis, 1) for axis in "xy"]
            + [part(self.from_line, 3)]
            + [part(self.from_side, axis, n) for n in (2, 3) for axis in "xy"],
            [part(self.from_corner, n) for n in range(4)],
        ]

    def whole(self):
        l = self.links
        for number in range(16):
            chip = self.chip(l.columns[number // 4], number % 4)
            l.arrived(self.slot(l.o, chip), self.sems["c"], (self.p, number))


class RowSlice:
    def __init__(self, links, ref, sems):
        self.links, self.ref = links, ref
        self.line_sems, self.core_sems = sems

    def slot(self, h, z):
        return rows_at(self.ref, (h * 4 + z) * 128, 128)

    def core(self, k, z):
        l = self.links
        l.send(self.slot(l.h, z), self.slot(l.h, z), self.core_sems, k, (l.o, l.b))

    def own(self, n):
        l = self.links
        z = l.nth(n)
        if n:
            l.pass_on(self.slot(l.h, z), z, self.line_sems, ())
        else:
            l.along(self.slot(l.h, z), self.line_sems, ())
        self.core(n, z)

    def from_line(self, n):
        l = self.links
        z = l.nth(n)
        l.arrived(self.slot(l.h, z), self.line_sems, (z,))
        self.own(n)

    def stages(self):
        part = functools.partial
        return [[part(self.own, 0)], [part(self.from_line, 1)], [part(self.from_line, 2)], [part(self.from_line, 3)]]

    def whole(self):
        l = self.links
        for n in range(4):
            l.arrived(self.slot(l.o, l.nth(n)), self.core_sems, n)


class ColumnSlice:
    def __init__(self, links, ref, stage, sems):
        self.links, self.ref, self.stage = links, ref, stage
        self.plane_sems, self.line_sems, self.core_sems = sems

    def chip(self, j, n):
        return self.links.columns[j] + 4 * self.links.nth(n)

    def slot(self, h, chip):
        return rows_at(self.ref, shard_of(h, chip) * 32, 32)

    def own(self, j, n):
        l = self.links
        piece = self.slot(l.h, self.chip(j, n))
        if n:
            l.pass_on(piece, l.nth(n), self.line_sems, (j,))
        else:
            l.along(piece, self.line_sems, (j,))
        l.send(piece, piece, self.core_sems, (j, n), (l.o, l.b))

    def start(self):
        l = self.links
        for j, chip in enumerate((l.b, l.xb, l.yb, l.db)):
            if j:
                l.send(rows_at(self.stage, j * 32, 32), self.slot(l.h, l.b), self.plane_sems, j, (l.h, chip))

    def from_plane(self, j):
        self.links.arrived(self.slot(self.links.h, self.chip(j, 0)), self.plane_sems, j)
        self.own(j, 0)

    def from_line(self, j, n):
        l = self.links
        l.arrived(self.slot(l.h, self.chip(j, n)), self.line_sems, (j, l.nth(n)))
        self.own(j, n)

    def stages(self):
        part = functools.partial
        return [
            [self.start],
            [part(self.own, 0, 0)] + [part(self.from_plane, j) for j in range(1, 4)],
            [part(self.from_line, j, n) for n in range(1, 4) for j in range(4)],
        ]

    def whole(self):
        l = self.links
        for j in range(4):
            for n in range(4):
                l.arrived(self.slot(l.o, self.chip(j, n)), self.core_sems, (j, n))


def ordered(stages, lag):
    events = []
    deepest = max(len(stage) for stage in stages)
    for tick in range(len(stages) * lag + deepest):
        for n, stage in enumerate(stages):
            if 0 <= tick - n * lag < len(stage):
                events += stage[tick - n * lag]
    return events


class Reduce:
    def __init__(self, links, g, out, base, width, bufs, sems, rows=slice(0, 128)):
        self.l, self.g, self.out, self.base, self.sems = links, g, out, base, sems
        self.by_core, self.by_side, self.by_turn, self.by_line = bufs
        self.half, self.p, self.rows = width // 2, width // 4, rows
        l = links
        self.mine = base + l.h * self.half
        p = self.p
        self.keep1 = (self.mine + l.x * (p // 2), self.mine + p + l.y * (p // 2))
        self.give1 = (self.mine + (1 - l.x) * (p // 2), self.mine + p + (1 - l.y) * (p // 2))
        self.keep2 = (self.keep1[0] + l.y * (p // 4), self.keep1[1] + l.x * (p // 4))
        self.give2 = (self.keep1[0] + (1 - l.y) * (p // 4), self.keep1[1] + (1 - l.x) * (p // 4))

    def at(self, start, width):
        return self.g.at[self.rows, pl.ds(pl.multiple_of(start, 128), width)]

    def out_at(self, start, width):
        return self.out.at[self.rows, pl.ds(pl.multiple_of(start, 128), width)]

    def chunk(self, z):
        first, second = self.keep2
        return first * (1 - z // 2) + second * (z // 2) + lax.rem(z, 2) * (self.p // 8)

    def add(self, start, width, others, final=False):
        tile = 384 if width % 384 == 0 else 128
        for n in range(width // tile):
            here = pl.ds(pl.multiple_of(start + n * tile, 128), tile)
            total = self.g[self.rows, here].astype(F4)
            for other in others:
                total = total + other[:, n * tile : (n + 1) * tile].astype(F4)
            (self.out if final else self.g)[self.rows, here] = total.astype(BF)

    def steps(self):
        l, p = self.l, self.p
        sides, turns = (l.xb, l.yb), (l.yb, l.xb)

        def cores():
            away = self.base + l.o * self.half
            l.send(self.at(away, self.half), self.by_core, self.sems, 0, (l.o, l.b))

        def side():
            l.arrived(self.by_core, self.sems, 0)
            for n in range(2):
                self.add(self.give1[n], p // 2, [self.by_core.at[:, pl.ds(pl.multiple_of(self.give1[n] - self.mine, 128), p // 2)]])
                l.send(self.at(self.give1[n], p // 2), self.by_side.at[n], self.sems, 1 + n, (l.h, sides[n]))
            for n in range(2):
                self.add(self.keep1[n], p // 2, [self.by_core.at[:, pl.ds(pl.multiple_of(self.keep1[n] - self.mine, 128), p // 2)]])

        def turn():
            for n in range(2):
                l.arrived(self.by_side.at[n], self.sems, 1 + n)
                self.add(self.keep1[n], p // 2, [self.by_side.at[n]])
                l.send(self.at(self.give2[n], p // 4), self.by_turn.at[n], self.sems, 3 + n, (l.h, turns[n]))

        def line():
            for n in range(2):
                l.arrived(self.by_turn.at[n], self.sems, 3 + n)
                self.add(self.keep2[n], p // 4, [self.by_turn.at[n]])
            for k in range(1, 4):
                away = self.chunk(lax.rem(l.z + k, 4))
                l.send(self.at(away, p // 8), self.by_line.at[k - 1], self.sems, 4 + k, (l.h, l.ahead(4 * k)))

        def line_back():
            for k in range(1, 4):
                l.arrived(self.by_line.at[k - 1], self.sems, 4 + k)
            self.add(self.chunk(l.z), p // 8, [self.by_line.at[k] for k in range(3)], True)
            here = self.out_at(self.chunk(l.z), p // 8)
            for k in range(1, 4):
                l.send(here, here, self.sems, 7 + k, (l.h, l.ahead(4 * k)))

        def turn_back():
            for k in range(1, 4):
                l.arrived(self.out_at(self.chunk(lax.rem(l.z + 4 - k, 4)), p // 8), self.sems, 7 + k)
            for n in range(2):
                here = self.out_at(self.keep2[n], p // 4)
                l.send(here, here, self.sems, 11 + n, (l.h, turns[n]))

        def side_back():
            for n in range(2):
                l.arrived(self.out_at(self.give2[n], p // 4), self.sems, 11 + n)
                here = self.out_at(self.keep1[n], p // 2)
                l.send(here, here, self.sems, 13 + n, (l.h, sides[n]))

        def cores_back():
            for n in range(2):
                l.arrived(self.out_at(self.give1[n], p // 2), self.sems, 13 + n)
            here = self.out_at(self.mine, self.half)
            l.send(here, here, self.sems, 15, (l.o, l.b))

        def done():
            l.arrived(self.out_at(self.base + l.o * self.half, self.half), self.sems, 15)

        return [cores, side, turn, line, line_back, turn_back, side_back, cores_back, done]


class SliceReduce:
    def __init__(self, links, g, out, base, bufs, sems):
        self.l, self.g, self.out, self.base, self.sems = links, g, out, base, sems
        self.by_core, self.by_line = bufs

    def at(self, ref, start, width):
        return ref.at[:, pl.ds(pl.multiple_of(start, 128), width)]

    def steps(self):
        l = self.l
        chips = (l.b, l.xb, l.yb, l.db)
        places = [
            self.base + 2048 * (lax.rem(chip, 4)) for chip in chips
        ]

        def region(j, h, z=None):
            if z is None:
                return self.at(self.out, places[j] + h * 1024, 1024)
            return self.at(self.out, places[j] + h * 1024 + z * 256, 256)

        def cores():
            l.send(self.at(self.g, l.o * 1024, 1024), self.by_core, self.sems, 0, (l.o, l.b))

        def line():
            l.arrived(self.by_core, self.sems, 0)
            for n in range(4):
                here = pl.ds(pl.multiple_of(l.h * 1024 + n * 256, 128), 256)
                total = self.g[:, here].astype(F4) + self.by_core[:, n * 256 : (n + 1) * 256].astype(F4)
                self.g[:, here] = total.astype(BF)
            for k in range(1, 4):
                z = lax.rem(l.z + k, 4)
                l.send(self.at(self.g, l.h * 1024 + z * 256, 256), self.by_line.at[k - 1], self.sems, k, (l.h, l.ahead(4 * k)))

        def line_back():
            total = self.g[:, pl.ds(pl.multiple_of(l.h * 1024 + l.z * 256, 128), 256)].astype(F4)
            for k in range(1, 4):
                l.arrived(self.by_line.at[k - 1], self.sems, k)
                total = total + self.by_line[k - 1].astype(F4)
            self.out[:, pl.ds(pl.multiple_of(places[0] + l.h * 1024 + l.z * 256, 128), 256)] = total.astype(BF)
            for k in range(1, 4):
                l.send(region(0, l.h, l.z), region(0, l.h, l.z), self.sems, 3 + k, (l.h, l.ahead(4 * k)))

        def plane():
            for k in range(1, 4):
                l.arrived(region(0, l.h, lax.rem(l.z + 4 - k, 4)), self.sems, 3 + k)
            for j in range(1, 4):
                l.send(region(0, l.h), region(0, l.h), self.sems, 6 + j, (l.h, chips[j]))
            l.send(region(0, l.h), region(0, l.h), self.sems, 10, (l.o, l.b))

        def cores_back():
            for j in range(1, 4):
                l.arrived(region(j, l.h), self.sems, 6 + j)
                l.send(region(j, l.h), region(j, l.h), self.sems, 10 + j, (l.o, l.b))

        def done():
            for j in range(4):
                l.arrived(region(j, l.o), self.sems, 10 + j)

        return [cores, line, line_back, plane, cores_back, done]


def shard_of(h, chip):
    return h * CHIPS + chip


def centre(stream):
    average = jnp.mean(stream, axis=-1, keepdims=True)
    centred = stream - average
    variance = jnp.mean(centred * centred, axis=-1, keepdims=True)
    scale = lax.rsqrt(variance + EPSILON)
    return centred * scale, scale


def norm_back(stream, gain, grad):
    hat, scale = centre(stream)
    q = grad * gain
    return scale * (
        q - jnp.mean(q, axis=-1, keepdims=True) - hat * jnp.mean(q * hat, axis=-1, keepdims=True)
    )


def gelu_parts(u):
    cubic = 0.044715 * u * u
    slope = math.sqrt(2.0 / math.pi)
    t = jnp.tanh(slope * u * (1.0 + cubic))
    grown = 0.5 * (1.0 + t)
    return u * grown, grown + 0.5 * u * (1.0 - t * t) * slope * (1.0 + 3.0 * cubic)


PIECES = 5
MIXER_D, MIXER_U, EXPAND_D, REDUCE_U, TRIPLE_D, TRIPLE_U, SLICES, COLUMNS = (
    0, 1024, 2048, 3072, 4096, 5120, 8192, 16384,
)

INPUTS = (
    "hidden", "cot", "index", "small_sh", "triple_sh", "mixer_sh", "reduce_sh", "expand_sh",
    "down_t", "up_t", "down_m", "up_m", "down_e", "up_e", "down_r", "up_r",
)
OUTPUTS = {"layer_out": ((128, 1024), BF), "hidden_grad": ((128, 1024), BF), "g": ((128, COLUMNS), BF)}
SCRATCH = {
    "wt": ((1024, 3072), BF), "wm": ((1024, 1024), BF), "wr": ((1024, 1024), BF), "we": ((1024, 1024), BF),
    "e_in": ((32, 4096), BF), "e_stage": ((128, 1024), BF), "up_es": ((128, 1024), BF), "down_rs": ((128, 1024), BF), "bias_es": ((1, 1024), F4),
    "sel": ((128, 128), F4), "small": ((512, 128), BF), "vecs": ((16, 1024), F4), "bias_t": ((1, 3072), F4), "bias_e": ((1, 4096), F4),
    "fn": ((128, 1024), BF), "rank_t": ((128, 128), BF), "kv": ((4096, 128), BF), "q": ((2048, 128), BF),
    "attden": ((2048, 128), F4), "attended": ((128, 1024), BF), "ones_v": ((4096, 128), BF),
    "send_kv": ((2048, 128), BF), "send_q": ((1024, 128), BF), "recv_q": ((1024, 128), BF),
    "send_a": ((1024, 128), BF), "recv_a": ((1024, 128), BF),
    "residual": ((128, 1024), F4), "sn_all": ((512, 1152), BF), "cot_all": ((512, 1152), BF),
    "act": ((512, 1024), BF), "agrad": ((512, 1024), BF), "ng_part": ((512, 1152), BF), "ng_recv": ((512, 1152), BF),
    "red_part": ((512, 1152), BF), "red_recv": ((512, 1152), BF),
    "send_g": ((1024, 128), BF), "recv_g": ((1024, 128), BF),
    "qd": ((2048, 128), BF), "dz": ((2048, 128), BF), "vz": ((4096, 128), BF),
    "k_t": ((64, 4096), BF), "ddrow": ((1, 2048), F4), "dq_t": ((128, 2048), F4), "part": ((4096, 128), F4),
    "recv_part": ((2048, 128), F4), "send_dkv": ((2048, 128), BF), "send_dq": ((1024, 128), BF),
    "recv_dkv": ((2048, 128), BF), "recv_dq": ((1024, 128), BF), "jg": ((128, 3072), BF),
"gp": ((128, SLICES), BF), "gs": ((128, 2048), BF), "slice_c": ((128, 1024), BF), "slice_l": ((3, 128, 256), BF),
    "early_c": ((128, 2048), BF), "early_1": ((2, 128, 512), BF), "early_2": ((2, 128, 256), BF), "early_3": ((3, 128, 128), BF),
    "late_c": ((2, 64, 2048), BF), "late_1": ((2, 2, 64, 512), BF), "late_2": ((2, 2, 64, 256), BF), "late_3": ((2, 3, 64, 128), BF),
}
SEMS = {
    "z": (PIECES, 4), "x": (PIECES, 4), "y": (PIECES, 4), "d": (PIECES, 4), "c": (PIECES, 16),
    "kv": (16,), "q": (16,), "f": (16,), "a": (16,), "g": (16,), "e": (16,), "dkv": (16,), "dq": (16,),
    "early": (16,), "late": (16,), "late_two": (16,), "slice": (16,),
    "rz": (4,), "rc": (4,), "ep": (4,), "ez": (4, 4), "ec": (4, 4), "ct": (2, 4), "sn": (2, 4), "ng": (2, 4), "rd": (2, 4),
}


def layer_kernel(*refs):
    names = list(INPUTS) + list(OUTPUTS) + list(SCRATCH)
    r = types.SimpleNamespace(**dict(zip(names, refs)))
    rest = refs[len(names) :]
    local_sem = rest[0]
    sems = {name: (rest[1 + 2 * n], rest[2 + 2 * n]) for n, name in enumerate(SEMS)}
    l = Links()
    low, low64 = half_mask(128), half_mask(64)
    mine = shard_of(l.h, l.b)
    local_copies = [
        pltpu.make_async_copy(r.small_sh, rows_at(r.small, mine * 16, 16), local_sem.at[0]),
        pltpu.make_async_copy(r.triple_sh, rows_at(r.wt, mine * 32, 32), local_sem.at[1]),
        pltpu.make_async_copy(r.mixer_sh, rows_at(r.wm, mine * 32, 32), local_sem.at[2]),
        pltpu.make_async_copy(r.reduce_sh, rows_at(r.wr, (l.h * 4 + l.z) * 128, 128), local_sem.at[3]),
        pltpu.make_async_copy(r.expand_sh, r.e_in, local_sem.at[4]),
    ]
    for copy in local_copies:
        copy.start()
    l.greet()
    adapter_of = lax.broadcasted_iota(jnp.int32, (128, 128), 0) // RANK
    r.sel[...] = jnp.where(adapter_of == r.index[...], 1.0, 0.0).T

    def columns(ref, at):
        return lambda h, chip: ref.at[
            pl.ds(pl.multiple_of(shard_of(h, chip) * 32, 32), 32), at : at + 1024
        ]

    slots = [lambda h, chip: rows_at(r.small, shard_of(h, chip) * 16, 16)]
    slots += [columns(r.wt, m * 1024) for m in range(3)]
    slots += [columns(r.wm, 0)]
    pieces = [Gather(l, n, slot, sems) for n, slot in enumerate(slots)]
    pieces.append(RowSlice(l, r.wr, (sems["rz"], sems["rc"])))
    pieces.append(ColumnSlice(l, r.we, r.e_stage, (sems["ep"], sems["ez"], sems["ec"])))
    places = [lax.rem(chip, 4) for chip in (l.b, l.xb, l.yb, l.db)]

    def block(j, i):
        return pl.ds(pl.multiple_of((i // 4 * 16 + places[j] + i % 4 * 4) * 128, 128), 128)

    for i in range(8):
        here = slice(i * 128, (i + 1) * 128)
        r.up_es[:, here] = r.up_e[:, block(0, i)]
        r.down_rs[:, here] = r.down_r[:, block(0, i)]
    for copy in local_copies:
        copy.wait()
    for i in range(8):
        here = slice(i * 128, (i + 1) * 128)
        r.we[pl.ds(pl.multiple_of(mine * 32, 32), 32), here] = r.e_in[:, block(0, i)]
        for j in range(1, 4):
            r.e_stage[j * 32 : (j + 1) * 32, here] = r.e_in[:, block(j, i)]
    l.met()
    stages = [piece.stages() for piece in pieces]
    events = [event for n in (0, 1, 2, 3, 6) for event in stages[n].pop(0)]
    stages[2][1] += stages[5].pop(0)
    events += ordered(stages[:4], 1)
    ends = {n: len(events) for n in range(4)}
    events += stages[4].pop(0)
    begun = len(events)
    events += stages[6].pop(0)
    crossed = len(events) + 8
    events += [event for stage in stages[4] for event in stage]
    ends[4] = len(events)
    events += [event for stage in stages[5] for event in stage]
    ends[5] = len(events)
    events += [event for stage in stages[6] for event in stage]
    ends[6] = len(events)
    state = [0]

    def pump(count):
        until(state[0] + count)

    def until(end):
        end = min(end, len(events))
        while state[0] < end:
            events[state[0]]()
            state[0] += 1

    def need(first, last):
        until(ends[last])
        for n in range(first, last + 1):
            pieces[n].whole()

    until(ends[3] - 4)
    pieces[0].whole()
    for g in range(8):
        tile = jnp.zeros((16, 128), F4)
        for n in range(4):
            at = (4 * g + n) * 16
            tile = tile + r.small[at : at + 16, :].astype(F4)
        r.vecs[:, g * 128 : (g + 1) * 128] = tile
        for n in range(3):
            at = (g * 3 + n) * 128
            r.bias_t[0:1, at : at + 128] = tile[6 + n : 7 + n, :]
        for n in range(4):
            at = (g * 4 + n) * 128
            r.bias_e[0:1, at : at + 128] = tile[9 + n : 10 + n, :]
    gain_one, bias_one, bias_m, gain_two, bias_two, bias_r = [
        (lambda n=n: r.vecs[n : n + 1, :]) for n in range(6)
    ]
    hat, _ = centre(r.hidden[...].astype(F4))
    r.fn[...] = (hat * gain_one() + bias_one()).astype(BF)

    def rank(source, down):
        return (r.sel[...] * by_transpose(source, down)).astype(BF)

    r.rank_t[...] = rank(r.fn[...], r.down_t[...])
    need(1, 3)
    until(begun)

    own = l.b * 256 + l.h * 128

    def kv_at(chip, h):
        return rows_at(r.kv, chip * 256 + h * 128, 128)

    kv_out = Exchange(l, r.send_kv, r.kv, 128, sems["kv"], lambda chip: kv_at(chip, l.h))
    q_out = Exchange(l, r.send_q, r.recv_q, 64, sems["q"])
    for step in range(4):
        plane = lax.rem(l.z + 1 + step, 4)

        def joint(part):
            at = pl.ds(pl.multiple_of(part * 1024 + plane * 256, 256), 256)
            tile = (
                product(r.fn[...], r.wt[:, at]) + r.bias_t[0:1, at] + product(r.rank_t[...], r.up_t[:, at])
            )
            return tile[:, :128], tile[:, 128:]

        for n, (qt, kt, vt) in enumerate(zip(joint(0), joint(1), joint(2))):
            c = plane * 4 + n * 2
            send_kv, send_q = rows_at(r.send_kv, c * 128, 256), rows_at(r.send_q, c * 64, 128)
            send_kv[0:128, :] = jnp.where(low, kt, swap(vt)).astype(BF)
            send_kv[128:256, :] = jnp.where(low, swap(kt), vt).astype(BF)
            qt = qt.astype(BF).astype(F4) * 0.125
            turned = swap(qt)
            send_q[0:64, :] = jnp.where(low64, qt[:64], turned[64:]).astype(BF)
            send_q[64:128, :] = jnp.where(low64, turned[:64], qt[64:]).astype(BF)
        for n in range(4):
            kv_out.send(plane * 4 + n)
            q_out.send(plane * 4 + n)
    kv_out.own()
    q_out.own()
    until(crossed)
    rank_grad_r = rank(r.cot[...], r.up_r[...])
    for i in range(8):
        r.bias_es[0:1, i * 128 : (i + 1) * 128] = r.bias_e[0:1, block(0, i)]

    def to_plane(source, target, name, half, own):
        for j, chip in ((3, l.db), (1, l.xb), (2, l.yb)):
            part = rows_at(source, half * 256 + (0 if own else j * 64), 64)
            l.send(part, rows_at(target, half * 256 + j * 64, 64), sems[name], (half, j), (l.h, chip))

    def from_plane(target, name, half):
        for j in range(1, 4):
            l.arrived(rows_at(target, half * 256 + j * 64, 64), sems[name], (half, j))

    def keep_own(target, at, tile):
        target[0:64, at] = tile[:64]
        target[256:320, at] = tile[64:]

    all_columns, ranks = slice(0, 1024), slice(1024, 1152)
    keep_own(r.cot_all, all_columns, r.cot[...])
    keep_own(r.cot_all, ranks, rank_grad_r)
    l.send(kv_at(l.b, l.h), kv_at(l.b, l.h), sems["f"], 0, (l.o, l.b))
    for k in range(1, CHIPS):
        kv_out.wait(k)
        c = l.behind(k)
        l.send(kv_at(c, l.h), kv_at(c, l.h), sems["f"], k, (l.o, l.b))
        until(min(state[0] + 1, ends[4]))
    to_plane(r.cot_all, r.cot_all, "ct", 0, True)
    to_plane(r.cot_all, r.cot_all, "ct", 1, True)
    until(ends[5])
    for k in range(1, CHIPS):
        q_out.wait(k)
    for k in range(CHIPS):
        l.arrived(kv_at(l.behind(k), l.o), sems["f"], k)

    for n in range(CHIPS):
        tile = r.recv_q[n * 64 : n * 64 + 64, :].astype(F4)
        r.q[n * 128 : n * 128 + 64, :] = jnp.where(low64, tile, 0.0).astype(BF)
        r.q[n * 128 + 64 : n * 128 + 128, :] = jnp.where(low64, swap(tile), 0.0).astype(BF)
        tile = r.kv[n * 256 : n * 256 + 256, :].astype(F4)
        r.ones_v[n * 256 : n * 256 + 256, :] = jnp.where(half_mask(256), 1.0, tile).astype(BF)
    a_out = Exchange(l, r.send_a, r.recv_a, 64, sems["a"])
    for i in (7, 0, 6, 1, 5, 2, 4, 3):
        queries = r.q[i * 256 : (i + 1) * 256, :]

        def fold(jj, total, masked=False):
            at = pl.ds(pl.multiple_of(jj * 512, 512), 512)
            powers = jnp.exp(by_transpose(queries, r.kv[at, :]))
            if masked:
                row = lax.broadcasted_iota(jnp.int32, (256, 512), 0)
                column = lax.broadcasted_iota(jnp.int32, (256, 512), 1)
                powers = jnp.where((row >= 128) | (column < 256), powers, 0.0)
            return total + product(powers.astype(BF), r.ones_v[at, :])

        total = fold(i, jnp.zeros((256, 128), F4), True)
        if i:
            total = lax.fori_loop(0, i, fold, total)
        share = total / swap(total)
        r.attden[i * 256 : (i + 1) * 256, :] = jnp.where(half_mask(256), total, share)
        for n in range(2):
            t = 2 * i + n
            part = share[n * 128 : n * 128 + 128]
            packed = jnp.where(low64, swap(part[64:]), part[:64]).astype(BF)
            r.send_a[t * 64 : t * 64 + 64, :] = packed
            a_out.send(t)
    a_out.own()
    until(ends[6])
    need(4, 4)
    for k in range(1, CHIPS):
        a_out.wait(k)
    for p in range(8):
        one = r.recv_a[p * 128 : p * 128 + 64, :].astype(F4)
        two = r.recv_a[p * 128 + 64 : p * 128 + 128, :].astype(F4)
        at = p * 128
        r.attended[0:64, at : at + 128] = jnp.where(low64, swap(one), two).astype(BF)
        r.attended[64:128, at : at + 128] = jnp.where(low64, one, swap(two)).astype(BF)

    rank_m = rank(r.attended[...], r.down_m[...])
    r.residual[...] = (
        r.hidden[...].astype(F4)
        + product(r.attended[...], r.wm[...])
        + bias_m()
        + product(rank_m, r.up_m[...])
    )
    hat, _ = centre(r.residual[...])
    second_normed = (hat * gain_two() + bias_two()).astype(BF)
    rank_e = rank(second_normed, r.down_e[...])
    keep_own(r.sn_all, all_columns, second_normed)
    keep_own(r.sn_all, ranks, rank_e)
    to_plane(r.sn_all, r.sn_all, "sn", 0, True)
    to_plane(r.sn_all, r.sn_all, "sn", 1, True)

    def tile_at(n, width):
        return pl.ds(pl.multiple_of(n * width, width), width)

    need(5, 6)
    from_plane(r.cot_all, "ct", 0)
    from_plane(r.cot_all, "ct", 1)

    def grad_tile(n, carry):
        at = tile_at(n, 256)
        r.agrad[:, at] = (
            by_transpose(r.cot_all[:, :1024], r.wr[at, :]) + product(r.cot_all[:, 1024:], r.down_rs[:, at])
        ).astype(BF)
        return carry

    lax.fori_loop(0, 4, grad_tile, 0)
    for half in range(2):
        from_plane(r.sn_all, "sn", half)
        these = slice(half * 256, half * 256 + 256)

        def inner_tile(n, carry):
            at = tile_at(n, 256)
            expanded = (
                product(r.sn_all[these, :1024], r.we[:, at])
                + r.bias_es[0:1, at]
                + product(r.sn_all[these, 1024:], r.up_es[:, at])
            )
            value, slope = gelu_parts(expanded)
            r.act[these, at] = value.astype(BF)
            r.agrad[these, at] = (r.agrad[these, at].astype(F4) * slope).astype(BF)
            return carry

        lax.fori_loop(0, 4, inner_tile, 0)

        def normed_tile(n, carry):
            at = tile_at(n, 256)
            r.ng_part[these, at] = by_transpose(r.agrad[these, :], r.we[at, :]).astype(BF)
            return carry

        lax.fori_loop(0, 4, normed_tile, 0)
        r.ng_part[these, 1024:] = by_transpose(r.agrad[these, :], r.up_es[...]).astype(BF)
        to_plane(r.ng_part, r.ng_recv, "ng", half, False)
    def flipped(tile):
        return tile.astype(F4).T.astype(BF)

    def reduce_tile(n, carry):
        at = tile_at(n, 256)
        r.red_part[:, at] = product(r.act[...], r.wr[:, at]).astype(BF)
        return carry

    lax.fori_loop(0, 4, reduce_tile, 0)
    r.red_part[:, 1024:] = by_transpose(r.act[...], r.down_rs[...]).astype(BF)
    rank_e_t, rank_grad_r_t = flipped(r.sn_all[:, 1024:]), flipped(r.cot_all[:, 1024:])
    for n in range(4):
        at = slice(n * 256, (n + 1) * 256)
        for kind, tile in enumerate((product(rank_e_t, r.agrad[:, at]), product(rank_grad_r_t, r.act[:, at]))):
            for m in range(2):
                to = (n * 2 + m) * 256 + kind * 128
                r.gs[:, to : to + 128] = tile[:, m * 128 : (m + 1) * 128].astype(BF)
    sliced = SliceReduce(l, r.gs, r.g, SLICES, (r.slice_c, r.slice_l), sems["slice"]).steps()
    sliced.pop(0)()
    from_plane(r.ng_recv, "ng", 0)
    from_plane(r.ng_recv, "ng", 1)

    def plane_sum(part, received, at):
        halves = []
        for start in (0, 256):
            total = part[start : start + 64, at].astype(F4)
            for j in range(1, 4):
                total = total + received[start + j * 64 : start + j * 64 + 64, at].astype(F4)
            halves.append(total)
        return jnp.concatenate(halves, axis=0)

    rank_grad_e = (r.sel[...] * plane_sum(r.ng_part, r.ng_recv, ranks)).astype(BF)
    normed_grad = plane_sum(r.ng_part, r.ng_recv, all_columns) + product(rank_grad_e, r.down_e[...])
    back_two = norm_back(r.residual[...], gain_two(), normed_grad)
    residual_grad = r.cot[...].astype(F4) + back_two
    mixed_grad = residual_grad.astype(BF)
    rank_grad_m = rank(mixed_grad, r.up_m[...])
    g_out = Exchange(l, r.send_g, r.recv_g, 64, sems["g"])
    for step in range(4):
        plane = lax.rem(l.z + 1 + step, 4)
        at = pl.ds(pl.multiple_of(plane * 256, 256), 256)
        both = by_transpose(mixed_grad, r.wm[at, :]) + product(rank_grad_m, r.down_m[:, at])
        for n in range(2):
            tile = both[:, n * 128 : n * 128 + 128]
            turned = swap(tile)
            send_g = rows_at(r.send_g, (plane * 4 + n * 2) * 64, 128)
            send_g[0:64, :] = jnp.where(low64, tile[64:], turned[:64]).astype(BF)
            send_g[64:128, :] = jnp.where(low64, turned[64:], tile[:64]).astype(BF)
        for n in range(4):
            g_out.send(plane * 4 + n)
    g_out.own()

    to_plane(r.red_part, r.red_recv, "rd", 0, False)
    to_plane(r.red_part, r.red_recv, "rd", 1, False)

    def adapter(at, left, right, width):
        for n in range(width // 512):
            r.gp[:, at + n * 512 : at + (n + 1) * 512] = product(left, right[:, n * 512 : (n + 1) * 512]).astype(BF)

    adapter(MIXER_D, flipped(rank_grad_m), r.attended, 1024)
    adapter(MIXER_U, flipped(rank_m), mixed_grad, 1024)
    adapter(EXPAND_D, flipped(rank_grad_e), second_normed, 1024)
    early = Reduce(l, r.gp, r.g, 0, TRIPLE_D, (r.early_c, r.early_1, r.early_2, r.early_3), sems["early"]).steps()

    def finish_output():
        from_plane(r.red_recv, "rd", 0)
        from_plane(r.red_recv, "rd", 1)
        rank_r = (r.sel[...] * plane_sum(r.red_part, r.red_recv, ranks)).astype(BF)
        reduced = plane_sum(r.red_part, r.red_recv, all_columns)
        r.layer_out[...] = (r.residual[...] + reduced + bias_r() + product(rank_r, r.up_r[...])).astype(BF)
        adapter(REDUCE_U, flipped(rank_r), r.cot, 1024)
        r.residual[...] = residual_grad
        early.pop(0)()

    for n in range(CHIPS):
        tile = r.kv[n * 256 : n * 256 + 256, :].astype(F4)
        wide = half_mask(256)
        r.ones_v[n * 256 : n * 256 + 256, :] = jnp.where(wide, tile, 0.0).astype(BF)
        r.vz[n * 256 : n * 256 + 256, :] = jnp.where(wide, 0.0, tile).astype(BF)
        r.k_t[:, n * 256 : n * 256 + 256] = tile.T[:64, :].astype(BF)
    r.dq_t[...] = jnp.zeros((128, 2048), F4)
    for k in range(1, CHIPS):
        g_out.wait(k)
    for n in range(CHIPS):
        at = n * 128
        g = r.recv_g[n * 64 : n * 64 + 64, :].astype(F4)
        both = r.attden[at : at + 128, :]
        grad = jnp.concatenate([g, swap(g)], axis=0)
        numer = jnp.where(low, 0.0, grad / swap(both))
        numer_low = numer.astype(BF)
        r.dz[at : at + 128, :] = numer_low
        r.qd[at : at + 128, :] = jnp.where(
            low, r.q[at : at + 128, :].astype(F4), numer_low.astype(F4)
        ).astype(BF)
        term = jnp.where(low, 0.0, numer * both)
        row = -jnp.sum(term.T, axis=0, keepdims=True)
        r.ddrow[0:1, at : at + 128] = row.astype(BF).astype(F4)
    dkv_out = Exchange(l, r.send_dkv, r.recv_dkv, 128, sems["dkv"])
    dq_out = Exchange(l, r.send_dq, r.recv_dq, 64, sems["dq"])

    def exchange(jj):
        for n in range(2):
            t = 2 * jj + n
            l.send(rows_at(r.part, t * 256 + l.o * 128, 128), rows_at(r.recv_part, t * 128, 128), sems["e"], t, (l.o, l.b))

    def finish(jj):
        for n in range(2):
            t = 2 * jj + n
            l.arrived(rows_at(r.recv_part, t * 128, 128), sems["e"], t)
            here = r.part[pl.ds(pl.multiple_of(t * 256 + l.h * 128, 128), 128), :]
            r.send_dkv[t * 128 : t * 128 + 128, :] = (here + r.recv_part[t * 128 : t * 128 + 128, :]).astype(BF)
            dkv_out.send(t)

    def finish_queries(i):
        for t in (2 * i, 2 * i + 1):
            y = r.dq_t[:, t * 128 : t * 128 + 128].T * 0.125
            r.send_dq[t * 64 : t * 64 + 64, :] = jnp.where(low64, y[:64], swap(y[64:])).astype(BF)
            dq_out.send(t)

    order = (4, 0, 5, 1, 6, 2, 7, 3)
    queries_sent = 0
    for place, jj in enumerate(order):
        keys = slice(jj * 512, jj * 512 + 512)

        def fold_back(i, total, masked=False):
            at = tile_at(i, 256)
            both = r.qd[at, :]
            powers = jnp.exp(by_transpose(r.ones_v[keys, :], both))
            if masked:
                row = lax.broadcasted_iota(jnp.int32, (512, 256), 0)
                column = lax.broadcasted_iota(jnp.int32, (512, 256), 1)
                powers = jnp.where((row < 256) | (column >= 128), powers, 0.0)
            prob = by_transpose(r.vz[keys, :], both) + r.ddrow[0:1, at]
            score = (powers * prob).astype(BF)
            r.dq_t[0:64, at] += product(r.k_t[:, keys], score)
            return total + product(score, r.q[at, :]) + product(powers.astype(BF), r.dz[at, :])

        total = fold_back(jj, jnp.zeros((512, 128), F4), True)
        if jj < 7:
            total = lax.fori_loop(jj + 1, 8, fold_back, total)
        r.part[keys, :] = total
        exchange(jj)
        if place:
            finish(order[place - 1])
        while queries_sent < 8 and all(n in order[: place + 1] for n in range(queries_sent + 1)):
            finish_queries(queries_sent)
            queries_sent += 1
        if place == 1:
            finish_output()
        for steps in {0: [sliced], 2: [sliced, early], 4: [early], 5: [sliced], 7: [early]}.get(place, []):
            steps.pop(0)()
    finish(order[-1])
    dkv_out.own()
    dq_out.own()
    for k in range(1, CHIPS):
        dkv_out.wait(k)
        dq_out.wait(k)
    for p in range(8):
        at = p * 128
        one = r.recv_dq[p * 128 : p * 128 + 64, :].astype(F4)
        two = r.recv_dq[p * 128 + 64 : p * 128 + 128, :].astype(F4)
        r.jg[0:64, at : at + 128] = jnp.where(low64, one, swap(two)).astype(BF)
        r.jg[64:128, at : at + 128] = jnp.where(low64, swap(one), two).astype(BF)
        one = r.recv_dkv[p * 256 : p * 256 + 128, :].astype(F4)
        two = r.recv_dkv[p * 256 + 128 : p * 256 + 256, :].astype(F4)
        r.jg[:, 1024 + at : 1152 + at] = jnp.where(low, one, swap(two)).astype(BF)
        r.jg[:, 2048 + at : 2176 + at] = jnp.where(low, swap(one), two).astype(BF)

    rank_grad_t = rank(r.jg[...], r.up_t[...])
    adapter(TRIPLE_D, flipped(rank_grad_t), r.fn, 1024)
    adapter(TRIPLE_U, flipped(r.rank_t[...]), r.jg, 3072)
    halves = [
        Reduce(
            l, r.gp, r.g, TRIPLE_D, SLICES - TRIPLE_D,
            [buf.at[n] for buf in (r.late_c, r.late_1, r.late_2, r.late_3)],
            sems[("late", "late_two")[n]], slice(n * 64, n * 64 + 64),
        ).steps()
        for n in range(2)
    ]
    late = [step for pair in zip(*halves) for step in pair]
    for _ in range(4):
        late.pop(0)()

    def triple_tile(n, carry):
        at = tile_at(n, 512)
        return carry + by_transpose(r.jg[:, at], r.wt[:, at])

    normed_grad = lax.fori_loop(0, 6, triple_tile, product(rank_grad_t, r.down_t[...]))
    back_one = norm_back(r.hidden[...].astype(F4), gain_one(), normed_grad)
    r.hidden_grad[...] = (r.residual[...] + back_one).astype(BF)
    while late or early or sliced:
        for rest in (late, late, early, sliced):
            if rest:
                rest.pop(0)()
    for out in (kv_out, q_out, a_out, g_out, dkv_out, dq_out):
        out.settle()
    l.settle()


def layer(*arrays):
    vmem = pl.BlockSpec(memory_space=pltpu.VMEM)
    hbm = pl.BlockSpec(memory_space=pl.ANY)
    dma = pltpu.SemaphoreType.DMA
    return pl.pallas_call(
        layer_kernel,
        name="layer",
        in_specs=[hbm if name.endswith("_sh") else vmem for name in INPUTS],
        out_shape=[jax.ShapeDtypeStruct(*OUTPUTS[name]) for name in OUTPUTS],
        out_specs=[vmem] * len(OUTPUTS),
        scratch_shapes=[pltpu.VMEM(*SCRATCH[name]) for name in SCRATCH]
        + [dma((5,))]
        + [dma(SEMS[name]) for name in SEMS for _ in range(2)],
        compiler_params=pltpu.CompilerParams(
            collective_id=0, has_side_effects=True, vmem_limit_bytes=LIMIT
        ),
    )(*arrays)


WRITTEN = (1024, 3072, 1024, 1024, 1024, 4096, 4096, 1024)


def write_kernel(layer_in, hidden_in, g, layer_out, hidden_out, td, tu, md, mu, ed, eu, rd, ru, low, high, in_sem, out_sem):
    passed = [
        pltpu.make_async_copy(layer_in, layer_out, out_sem.at[0]),
        pltpu.make_async_copy(hidden_in, hidden_out, out_sem.at[1]),
    ]
    reads = [
        pltpu.make_async_copy(
            g.at[:, n * 2048 : (n + 1) * 2048], low.at[:, n * 2048 : (n + 1) * 2048], in_sem.at[n]
        )
        for n in range(8)
    ]
    for copy in reads + passed:
        copy.start()
    writes = []

    def write(start, width, target, at):
        copy = pltpu.make_async_copy(
            high.at[:, start : start + width], target.at[:, at : at + width], out_sem.at[2 + len(writes)]
        )
        copy.start()
        writes.append(copy)

    whole = (
        (MIXER_D, 1024, md, 0), (MIXER_U, 1024, mu, 0), (EXPAND_D, 1024, ed, 0), (REDUCE_U, 1024, ru, 0),
        (TRIPLE_D, 1024, td, 0), (TRIPLE_U, 1024, tu, 0), (TRIPLE_U + 1024, 2048, tu, 1024),
    )
    done = 0
    for start, width, target, at in whole:
        while done * 2048 < start + width:
            reads[done].wait()
            done += 1
        high[:, start : start + width] = low[:, start : start + width].astype(F4)
        write(start, width, target, at)
    for n in range(done, 8):
        reads[n].wait()
    for h in range(2):
        for kind, target in enumerate((eu, rd)):
            to = SLICES + (h * 2 + kind) * 2048
            for z in range(4):
                for p in range(4):
                    source = SLICES + p * 2048 + h * 1024 + z * 256 + kind * 128
                    here = to + (z * 4 + p) * 128
                    high[:, here : here + 128] = low[:, source : source + 128].astype(F4)
            write(to, 2048, target, h * 2048)
    for copy in passed + writes:
        copy.wait()


def written(layer_out, hidden_grad, g):
    hbm = pl.BlockSpec(memory_space=pl.ANY)
    dma = pltpu.SemaphoreType.DMA
    return pl.pallas_call(
        write_kernel,
        name="written",
        in_specs=[hbm] * 3,
        out_shape=[jax.ShapeDtypeStruct((128, 1024), BF)] * 2 + [jax.ShapeDtypeStruct((128, width), F4) for width in WRITTEN],
        out_specs=[hbm] * 10,
        scratch_shapes=[pltpu.VMEM((128, COLUMNS), BF), pltpu.VMEM((128, COLUMNS), F4), dma((8,)), dma((16,))],
        compiler_params=pltpu.CompilerParams(vmem_limit_bytes=20 * 1024 * 1024),
    )(layer_out, hidden_grad, g)


def small_block(blocks, triple_bias, expand_bias):
    place = lax.rem(shard_of(lax.axis_index("head"), lax.axis_index("blk")), 4)
    lane = jnp.arange(128, dtype=jnp.int32)[None, :]
    six = jnp.where(lane // 32 == place, jnp.tile(jnp.stack(blocks), (1, 4)), 0)
    wide = jnp.arange(384, dtype=jnp.int32)
    three = jnp.where(wide // 96 == place, jnp.tile(triple_bias, 4), 0).reshape(3, 128)
    row = jnp.arange(4, dtype=jnp.int32)[:, None]
    four = jnp.where(row == place, expand_bias[None, :], 0)
    return jnp.concatenate([six, three, four, jnp.zeros((3, 128), BF)], axis=0).astype(BF)


def local_fast(
    hidden, adapter_index, first_gain, first_bias, triple_weight, triple_bias, mixer_weight, mixer_bias,
    second_gain, second_bias, expand_weight, expand_bias, reduce_weight, reduce_bias, triple_down, triple_up,
    mixer_down, mixer_up, expand_down, expand_up, reduce_down, reduce_up, cotangent,
):
    def turned(factor):
        return jnp.transpose(factor, (0, 2, 1)).reshape(ADAPTERS * RANK, factor.shape[1])

    small_sh = small_block(
        [first_gain, first_bias, mixer_bias, second_gain, second_bias, reduce_bias], triple_bias, expand_bias
    )
    layer_out, hidden_grad, g = layer(
        hidden, cotangent, adapter_index.reshape(1, 128), small_sh, triple_weight, mixer_weight, reduce_weight, expand_weight,
        turned(triple_down), flat_up(triple_up), turned(mixer_down), flat_up(mixer_up),
        turned(expand_down), flat_up(expand_up), turned(reduce_down), flat_up(reduce_up),
    )
    layer_out, hidden_grad, *grads = written(layer_out, hidden_grad, g)

    def down_out(part):
        return jnp.transpose(part.reshape(ADAPTERS, RANK, part.shape[1]), (0, 2, 1))

    def up_out(part):
        return part.reshape(ADAPTERS, RANK, part.shape[1])

    shaped = [down_out, up_out, down_out, up_out, down_out, up_out, down_out, up_out]
    return (layer_out, hidden_grad) + tuple(shape(part) for shape, part in zip(shaped, grads))


def solution(mesh):
    placed = (
        P(("blk", "head"), None),
        P(("blk", "head")),
        P(("head", "blk")),
        P(("head", "blk")),
        P(("head", "blk"), None),
        P(("head", "blk")),
        P(("head", "blk"), None),
        P(("head", "blk")),
        P(("head", "blk")),
        P(("head", "blk")),
        P(("head", "blk"), None),
        P(("head", "blk")),
        P(("head", "blk"), None),
        P(("head", "blk")),
        P(),
        P(),
        P(),
        P(),
        P(),
        P(),
        P(),
        P(),
        P(("blk", "head"), None),
    )
    fits = tuple(mesh.shape[name] for name in ("head", "blk")) == (2, CHIPS)
    return jax.shard_map(
        local_fast if fits else local,
        mesh=mesh,
        in_specs=placed,
        out_specs=(
            P(("blk", "head"), None),
            P(("blk", "head"), None),
            P(),
            P(),
            P(),
            P(),
            P(),
            P(),
            P(),
            P(),
        ),
        check_vma=False,
    )
```

```python
import functools
import math
import types

import jax
import jax.numpy as jnp
from jax import lax
from jax.experimental import pallas as pl
from jax.experimental.pallas import tpu as pltpu
from jax.sharding import PartitionSpec as P

WIDTH = 1024
HEADS = 16
HEAD_DIM = 64
RANK = 16
ADAPTERS = 8
BLOCK = 256


EPSILON = 1e-05


def product(left, right):
    return jnp.dot(left, right, preferred_element_type=jnp.float32)


def by_transpose(left, right):
    return lax.dot_general(
        left, right, (((1,), (1,)), ((), ())), preferred_element_type=jnp.float32
    )


def transpose_by(left, right):
    return lax.dot_general(
        left, right, (((0,), (0,)), ((), ())), preferred_element_type=jnp.float32
    )


def layer_norm(stream, scales, offset):
    average = jnp.mean(stream, axis=-1, keepdims=True)
    centred = stream - average
    variance = jnp.mean(centred * centred, axis=-1, keepdims=True)
    return centred * lax.rsqrt(variance + EPSILON) * scales + offset


def selector(adapter_index):
    column = jnp.arange(ADAPTERS * RANK, dtype=jnp.int32) // RANK
    return (adapter_index[:, None] == column[None, :]).astype(jnp.float32)


def flat_down(factor):
    return jnp.transpose(factor, (1, 0, 2)).reshape(factor.shape[1], ADAPTERS * RANK)


def flat_up(factor):
    return factor.reshape(ADAPTERS * RANK, factor.shape[2])


def unflat_down(gradient):
    return jnp.transpose(gradient.reshape(gradient.shape[0], ADAPTERS, RANK), (1, 0, 2))


def unflat_up(gradient):
    return gradient.reshape(ADAPTERS, RANK, gradient.shape[1])


def projected(source, weight, offset, down_flat, up_flat, selection):
    low_rank = (selection * product(source, down_flat)).astype(jnp.bfloat16)
    return (
        product(source, weight) + offset.astype(jnp.float32) + product(low_rank, up_flat),
        low_rank,
    )


def adapter_grads(source, low_rank, out_grad, down_flat, up_flat, selection):
    rank_grad = (selection * by_transpose(out_grad, up_flat)).astype(jnp.bfloat16)
    down_grad = transpose_by(source, rank_grad)
    up_grad = transpose_by(low_rank, out_grad)
    return (down_grad, up_grad, by_transpose(rank_grad, down_flat))


def score_block(queries, keys_block):
    return jnp.einsum("qhd,khd->qhk", queries, keys_block, preferred_element_type=jnp.float32) * (
        1.0 / math.sqrt(HEAD_DIM)
    )


def cut_rows(arrays, trailing):
    length = arrays[0].shape[0]
    block_rows = math.gcd(length, 512)
    repeats = length // block_rows
    shaped = tuple(
        (
            array.reshape((repeats, block_rows) + shape_tail)
            for array, shape_tail in zip(arrays, trailing)
        )
    )
    firsts = jnp.arange(repeats, dtype=jnp.int32) * block_rows
    return (shaped, firsts, block_rows)


def forward_fold(queries, query_places, locate, totals, portion):
    head_count = queries.shape[1]
    query_block = query_places // BLOCK
    last_block = jnp.max(query_block)
    shaped, firsts, block_rows = cut_rows(portion, ((head_count, HEAD_DIM), (head_count, HEAD_DIM)))

    def forward_visiting(carried, packet):
        keys_block, values_block, first_row = packet
        key_places = locate(first_row, block_rows)

        def forward_compute(running):
            numerator, denominator = running
            allowed = (key_places // BLOCK)[None, None, :] <= query_block[:, None, None]
            powers = jnp.where(allowed, jnp.exp(score_block(queries, keys_block)), 0.0)
            numerator = numerator + jnp.einsum(
                "qhk,khd->qhd",
                powers.astype(jnp.bfloat16),
                values_block,
                preferred_element_type=jnp.float32,
            )
            return (numerator, denominator + jnp.sum(powers, axis=-1))

        skipped = jnp.min(key_places) // BLOCK > last_block
        return (lax.cond(skipped, lambda running: running, forward_compute, carried), None)

    return lax.scan(forward_visiting, totals, shaped + (firsts,))[0]


def query_grad_fold(queries, query_places, locate, numer_grad, denom_grad, totals, portion):
    head_count = queries.shape[1]
    query_block = query_places // BLOCK
    last_block = jnp.max(query_block)
    shaped, firsts, block_rows = cut_rows(portion, ((head_count, HEAD_DIM), (head_count, HEAD_DIM)))

    def query_visiting(carried, packet):
        keys_block, values_block, first_row = packet
        key_places = locate(first_row, block_rows)

        def query_compute(running):
            allowed = (key_places // BLOCK)[None, None, :] <= query_block[:, None, None]
            powers = jnp.where(allowed, jnp.exp(score_block(queries, keys_block)), 0.0)
            prob_grad = jnp.einsum(
                "qhd,khd->qhk", numer_grad, values_block, preferred_element_type=jnp.float32
            )
            score_grad = (powers * (prob_grad + denom_grad[:, :, None])).astype(jnp.bfloat16)
            return running + jnp.einsum(
                "qhk,khd->qhd", score_grad, keys_block, preferred_element_type=jnp.float32
            )

        skipped = jnp.min(key_places) // BLOCK > last_block
        return (lax.cond(skipped, lambda running: running, query_compute, carried), None)

    return lax.scan(query_visiting, totals, shaped + (firsts,))[0]


def key_grad_fold(keys_here, values_here, key_places, locate, totals, portion):
    head_count = keys_here.shape[1]
    key_block = key_places // BLOCK
    first_block = jnp.min(key_block)
    shaped, firsts, block_rows = cut_rows(
        portion, ((head_count, HEAD_DIM), (head_count, HEAD_DIM), (head_count,))
    )

    def key_visiting(carried, packet):
        query_rows, numer_rows, denom_rows, first_row = packet
        query_places = locate(first_row, block_rows)

        def key_compute(running):
            keys_grad, values_grad = running
            allowed = key_block[None, None, :] <= (query_places // BLOCK)[:, None, None]
            powers = jnp.where(allowed, jnp.exp(score_block(query_rows, keys_here)), 0.0)
            prob_grad = jnp.einsum(
                "qhd,khd->qhk", numer_rows, values_here, preferred_element_type=jnp.float32
            )
            score_grad = (powers * (prob_grad + denom_rows.astype(jnp.float32)[:, :, None])).astype(
                jnp.bfloat16
            )
            keys_grad = keys_grad + jnp.einsum(
                "qhk,qhd->khd", score_grad, query_rows, preferred_element_type=jnp.float32
            )
            values_grad = values_grad + jnp.einsum(
                "qhk,qhd->khd",
                powers.astype(jnp.bfloat16),
                numer_rows,
                preferred_element_type=jnp.float32,
            )
            return (keys_grad, values_grad)

        skipped = jnp.max(query_places) // BLOCK < first_block
        return (lax.cond(skipped, lambda running: running, key_compute, carried), None)

    return lax.scan(key_visiting, totals, shaped + (firsts,))[0]


def local(
    hidden,
    adapter_index,
    first_gain,
    first_bias,
    triple_weight,
    triple_bias,
    mixer_weight,
    mixer_bias,
    second_gain,
    second_bias,
    expand_weight,
    expand_bias,
    reduce_weight,
    reduce_bias,
    triple_down,
    triple_up,
    mixer_down,
    mixer_up,
    expand_down,
    expand_up,
    reduce_down,
    reduce_up,
    cotangent,
):
    gathered = (
        lax.all_gather(first_gain, ("head", "blk"), axis=0, tiled=True),
        lax.all_gather(first_bias, ("head", "blk"), axis=0, tiled=True),
        lax.all_gather(triple_weight, ("head", "blk"), axis=0, tiled=True),
        lax.all_gather(triple_bias, ("head", "blk"), axis=0, tiled=True),
        lax.all_gather(mixer_weight, ("head", "blk"), axis=0, tiled=True),
        lax.all_gather(mixer_bias, ("head", "blk"), axis=0, tiled=True),
        lax.all_gather(second_gain, ("head", "blk"), axis=0, tiled=True),
        lax.all_gather(second_bias, ("head", "blk"), axis=0, tiled=True),
        lax.all_gather(expand_weight, ("head", "blk"), axis=0, tiled=True),
        lax.all_gather(expand_bias, ("head", "blk"), axis=0, tiled=True),
        lax.all_gather(reduce_weight, ("head", "blk"), axis=0, tiled=True),
        lax.all_gather(reduce_bias, ("head", "blk"), axis=0, tiled=True),
    )
    (
        gain_one,
        bias_one,
        weight_triple,
        bias_triple,
        weight_mixer,
        bias_mixer,
        gain_two,
        bias_two,
        weight_expand,
        bias_expand,
        weight_reduce,
        bias_reduce,
    ) = gathered
    token_count = hidden.shape[0]
    head_ways = lax.axis_size("head")
    cycle_ways = lax.axis_size("blk")
    selection = selector(adapter_index)
    down_triple = flat_down(triple_down)
    upward_triple = flat_up(triple_up)
    down_mixer = flat_down(mixer_down)
    upward_mixer = flat_up(mixer_up)
    down_expand = flat_down(expand_down)
    upward_expand = flat_up(expand_up)
    down_reduce = flat_down(reduce_down)
    upward_reduce = flat_up(reduce_up)
    stream = hidden.astype(jnp.float32)

    def first_norm(values_in):
        return layer_norm(values_in, gain_one.astype(jnp.float32), bias_one.astype(jnp.float32))

    def second_norm(values_in):
        return layer_norm(values_in, gain_two.astype(jnp.float32), bias_two.astype(jnp.float32))

    first_normed = first_norm(stream).astype(jnp.bfloat16)
    joint, rank_triple = projected(
        first_normed, weight_triple, bias_triple, down_triple, upward_triple, selection
    )
    joint = joint.astype(jnp.bfloat16)
    parts = joint.reshape(token_count, 3, HEADS, HEAD_DIM)
    own_shard = lax.axis_index("blk") * head_ways + lax.axis_index("head")
    query_places = own_shard * token_count + jnp.arange(token_count, dtype=jnp.int32)

    def locate(first_row, length):
        rows_here = first_row + jnp.arange(length, dtype=jnp.int32)
        shard_index = rows_here // token_count
        return (
            shard_index % cycle_ways * head_ways + shard_index // cycle_ways
        ) * token_count + rows_here % token_count

    queries = parts[:, 0]
    keys_here = parts[:, 1]
    values_here = parts[:, 2]
    head_count = queries.shape[1]
    flat_keys = keys_here.reshape(token_count, head_count * HEAD_DIM)
    flat_values = values_here.reshape(token_count, head_count * HEAD_DIM)
    zeros_rows = jnp.zeros((token_count, head_count, HEAD_DIM), jnp.float32)
    payload = (flat_keys, flat_values)
    numerator, denominator = forward_fold(
        queries,
        query_places,
        locate,
        (zeros_rows, jnp.zeros((token_count, head_count), jnp.float32)),
        (
            lax.all_gather(payload[0], ("head", "blk"), axis=0, tiled=True),
            lax.all_gather(payload[1], ("head", "blk"), axis=0, tiled=True),
        ),
    )
    attended = numerator / denominator[:, :, None]
    attended_low = attended.astype(jnp.bfloat16).reshape(token_count, WIDTH)
    mixed, rank_mixer = projected(
        attended_low, weight_mixer, bias_mixer, down_mixer, upward_mixer, selection
    )
    residual = stream + mixed
    second_normed = second_norm(residual).astype(jnp.bfloat16)
    expanded, rank_expand = projected(
        second_normed, weight_expand, bias_expand, down_expand, upward_expand, selection
    )
    activated = jax.nn.gelu(expanded, approximate=True).astype(jnp.bfloat16)
    reduced, rank_reduce = projected(
        activated, weight_reduce, bias_reduce, down_reduce, upward_reduce, selection
    )
    layer_out = (residual + reduced).astype(jnp.bfloat16)
    reduce_down_grad, reduce_up_grad, through_reduce = adapter_grads(
        activated, rank_reduce, cotangent, down_reduce, upward_reduce, selection
    )
    activated_grad = (by_transpose(cotangent, weight_reduce) + through_reduce).astype(jnp.bfloat16)
    gelu_back = jax.vjp(lambda values_in: jax.nn.gelu(values_in, approximate=True), expanded)[1]
    expanded_grad = gelu_back(activated_grad.astype(jnp.float32))[0].astype(jnp.bfloat16)
    expand_down_grad, expand_up_grad, through_expand = adapter_grads(
        second_normed, rank_expand, expanded_grad, down_expand, upward_expand, selection
    )
    normed_grad = by_transpose(expanded_grad, weight_expand) + through_expand
    second_back = jax.vjp(second_norm, residual)[1]
    residual_grad = cotangent.astype(jnp.float32) + second_back(normed_grad)[0]
    mixed_grad = residual_grad.astype(jnp.bfloat16)
    mixer_down_grad, mixer_up_grad, through_mixer = adapter_grads(
        attended_low, rank_mixer, mixed_grad, down_mixer, upward_mixer, selection
    )
    attended_grad = (by_transpose(mixed_grad, weight_mixer) + through_mixer).astype(jnp.bfloat16)
    output_grad = attended_grad.reshape(token_count, HEADS, HEAD_DIM).astype(jnp.float32)
    numer_grad = (output_grad / denominator[:, :, None]).astype(jnp.bfloat16)
    denom_grad = (-jnp.sum(output_grad * attended, axis=-1) / denominator).astype(jnp.bfloat16)
    payload = (flat_keys, flat_values)
    query_grad = query_grad_fold(
        queries,
        query_places,
        locate,
        numer_grad,
        denom_grad.astype(jnp.float32),
        zeros_rows,
        (
            lax.all_gather(payload[0], ("head", "blk"), axis=0, tiled=True),
            lax.all_gather(payload[1], ("head", "blk"), axis=0, tiled=True),
        ),
    )
    payload = (
        queries.reshape(token_count, head_count * HEAD_DIM),
        numer_grad.reshape(token_count, head_count * HEAD_DIM),
        denom_grad,
    )
    keys_grad, values_grad = key_grad_fold(
        keys_here,
        values_here,
        query_places,
        locate,
        (zeros_rows, zeros_rows),
        (
            lax.all_gather(payload[0], ("head", "blk"), axis=0, tiled=True),
            lax.all_gather(payload[1], ("head", "blk"), axis=0, tiled=True),
            lax.all_gather(payload[2], ("head", "blk"), axis=0, tiled=True),
        ),
    )
    factor = 1.0 / math.sqrt(HEAD_DIM)
    joint_grad = jnp.stack([query_grad * factor, keys_grad * factor, values_grad], axis=1).astype(
        jnp.bfloat16
    )
    joint_tokens = joint_grad.reshape(token_count, 3 * WIDTH)
    triple_down_grad, triple_up_grad, through_triple = adapter_grads(
        first_normed, rank_triple, joint_tokens, down_triple, upward_triple, selection
    )
    normed_one_grad = by_transpose(joint_tokens, weight_triple) + through_triple
    first_back = jax.vjp(first_norm, stream)[1]
    hidden_grad = (residual_grad + first_back(normed_one_grad)[0]).astype(jnp.bfloat16)
    summed = lax.psum(
        (
            triple_down_grad,
            triple_up_grad,
            mixer_down_grad,
            mixer_up_grad,
            expand_down_grad,
            expand_up_grad,
            reduce_down_grad,
            reduce_up_grad,
        ),
        ("head", "blk"),
    )
    return (
        layer_out,
        hidden_grad,
        unflat_down(summed[0]),
        unflat_up(summed[1]),
        unflat_down(summed[2]),
        unflat_up(summed[3]),
        unflat_down(summed[4]),
        unflat_up(summed[5]),
        unflat_down(summed[6]),
        unflat_up(summed[7]),
    )


MESH = pl.DeviceIdType.MESH
CHIPS = 16
LIMIT = 62 * 1024 * 1024 - 512 * 1024
BF = jnp.bfloat16
F4 = jnp.float32


ALONG = ((0, 1, 2, 3), (1, 0, 2, 3), (2, 1, 3, 0), (3, 2, 1, 0))


class Links:
    def __init__(self):
        self.h = lax.axis_index("head")
        self.b = lax.axis_index("blk")
        self.o = 1 - self.h
        self.sent = []
        self.x = lax.rem(self.b, 2)
        self.y = lax.rem(self.b // 2, 2)
        self.z = self.b // 4
        self.xb = self.b + 1 - 2 * self.x
        self.yb = self.b + 2 - 4 * self.y
        self.db = self.xb + 2 - 4 * self.y
        self.columns = [lax.rem(chip, 4) for chip in (self.b, self.xb, self.yb, self.db)]

    def nth(self, n):
        return sum(jnp.where(self.z == z, table[n], 0) for z, table in enumerate(ALONG))

    def at_line(self, z):
        return lax.rem(self.b, 4) + 4 * z

    def along(self, piece, sems, index):
        for k, wanted in ((1, self.z < 3), (3, self.z > 0), (2, None)):
            where = (piece, piece, sems, index + (self.z,), (self.h, self.ahead(4 * k)))
            if wanted is None:
                self.send(*where)
            else:
                self.send_if(wanted, *where)

    def pass_on(self, piece, z, sems, index):
        wanted = (self.z == 2) & (z == 0) | (self.z == 1) & (z == 3)
        chip = self.columns[0] + 4 * (3 - z)
        self.send_if(wanted, piece, piece, sems, index + (z,), (self.h, chip))

    def ahead(self, k):
        return lax.rem(self.b + k, CHIPS)

    def behind(self, k):
        return lax.rem(self.b + CHIPS - k, CHIPS)

    def greet(self):
        barrier = pltpu.get_barrier_semaphore()
        for k in range(1, CHIPS):
            pl.semaphore_signal(
                barrier, 1, device_id=(self.h, self.ahead(k)), device_id_type=MESH
            )
        pl.semaphore_signal(barrier, 1, device_id=(self.o, self.b), device_id_type=MESH)

    def met(self):
        pl.semaphore_wait(pltpu.get_barrier_semaphore(), CHIPS)

    def copy(self, source, target, sems, at, device):
        return pltpu.make_async_remote_copy(
            src_ref=source,
            dst_ref=target,
            send_sem=sems[0].at[at],
            recv_sem=sems[1].at[at],
            device_id=device,
            device_id_type=MESH,
        )

    def send(self, source, target, sems, at, device):
        copy = self.copy(source, target, sems, at, device)
        copy.start()
        self.sent.append((None, copy))

    def send_if(self, wanted, *where):
        copy = self.copy(*where)
        pl.when(wanted)(copy.start)
        self.sent.append((wanted, copy))

    def arrived(self, target, sems, at):
        self.copy(target, target, sems, at, (self.o, self.b)).wait_recv()

    def settle(self):
        for wanted, copy in self.sent:
            if wanted is None:
                copy.wait_send()
            else:
                pl.when(wanted)(copy.wait_send)
        self.sent = []


class Exchange:
    def __init__(self, links, source, target, rows, sems, slot=None):
        self.links, self.source, self.target = links, source, target
        self.rows, self.sems = rows, sems
        self.slot = slot or (lambda chip: rows_at(target, chip * rows, rows))

    def send(self, t):
        l = self.links

        @pl.when(l.b != t)
        def _():
            l.copy(
                rows_at(self.source, t * self.rows, self.rows),
                self.slot(l.b), self.sems, lax.rem(t + CHIPS - l.b, CHIPS), (l.h, t),
            ).start()

    def own(self):
        l = self.links
        copy = pltpu.make_async_copy(
            rows_at(self.source, l.b * self.rows, self.rows), self.slot(l.b), self.sems[0].at[0]
        )
        copy.start()
        copy.wait()

    def wait(self, k):
        self.links.arrived(self.slot(self.links.behind(k)), self.sems, k)

    def settle(self):
        for k in range(1, CHIPS):
            l = self.links
            part = rows_at(self.source, l.ahead(k) * self.rows, self.rows)
            l.copy(part, part, self.sems, k, (l.h, l.ahead(k))).wait_send()


def half_mask(rows):
    return lax.broadcasted_iota(jnp.int32, (rows, 128), 1) < 64


def swap(tile):
    return pltpu.roll(tile, 64, 1)


def rows_at(ref, start, count):
    return ref.at[pl.ds(pl.multiple_of(start, 16), count), :]


class Gather:
    def __init__(self, links, number, slot, sems):
        self.links, self.p, self.slot = links, number, slot
        self.sems = sems

    def send(self, axis, n, chip, device):
        piece = self.slot(self.links.h, chip)
        self.links.send(piece, piece, self.sems[axis], (self.p, n), device)

    def chip(self, side, n):
        return side + 4 * self.links.nth(n)

    def own(self, n):
        l = self.links
        chip = self.chip(l.columns[0], n)
        if n:
            l.pass_on(self.slot(l.h, chip), l.nth(n), self.sems["z"], (self.p,))
        else:
            l.along(self.slot(l.h, chip), self.sems["z"], (self.p,))
        self.send("x", n, chip, (l.h, l.xb))
        self.send("y", n, chip, (l.h, l.yb))
        self.send("c", n, chip, (l.o, l.b))

    def from_line(self, n):
        l = self.links
        chip = self.chip(l.columns[0], n)
        l.arrived(self.slot(l.h, chip), self.sems["z"], (self.p, l.nth(n)))
        self.own(n)

    def arrived(self, axis, n, chip):
        self.links.arrived(self.slot(self.links.h, chip), self.sems[axis], (self.p, n))

    def from_side(self, axis, n):
        l = self.links
        chip = self.chip(l.columns[1 if axis == "x" else 2], n)
        self.arrived(axis, n, chip)
        if (n % 2 == 0) == (axis == "x"):
            self.send("d", n, chip, (l.h, l.yb if axis == "x" else l.xb))
        self.send("c", (4 if axis == "x" else 8) + n, chip, (l.o, l.b))

    def from_corner(self, n):
        l = self.links
        chip = self.chip(l.columns[3], n)
        self.arrived("d", n, chip)
        self.send("c", 12 + n, chip, (l.o, l.b))

    def stages(self):
        part = functools.partial
        return [
            [part(self.own, 0)],
            [part(self.from_line, 1), part(self.from_side, "x", 0), part(self.from_side, "y", 0), part(self.from_line, 2)],
            [part(self.from_side, axis, 1) for axis in "xy"]
            + [part(self.from_line, 3)]
            + [part(self.from_side, axis, n) for n in (2, 3) for axis in "xy"],
            [part(self.from_corner, n) for n in range(4)],
        ]

    def whole(self):
        l = self.links
        for number in range(16):
            chip = self.chip(l.columns[number // 4], number % 4)
            l.arrived(self.slot(l.o, chip), self.sems["c"], (self.p, number))


class RowSlice:
    def __init__(self, links, ref, sems):
        self.links, self.ref = links, ref
        self.line_sems, self.core_sems = sems

    def slot(self, h, z):
        return rows_at(self.ref, (h * 4 + z) * 128, 128)

    def core(self, k, z):
        l = self.links
        l.send(self.slot(l.h, z), self.slot(l.h, z), self.core_sems, k, (l.o, l.b))

    def own(self, n):
        l = self.links
        z = l.nth(n)
        if n:
            l.pass_on(self.slot(l.h, z), z, self.line_sems, ())
        else:
            l.along(self.slot(l.h, z), self.line_sems, ())
        self.core(n, z)

    def from_line(self, n):
        l = self.links
        z = l.nth(n)
        l.arrived(self.slot(l.h, z), self.line_sems, (z,))
        self.own(n)

    def stages(self):
        part = functools.partial
        return [[part(self.own, 0)], [part(self.from_line, 1)], [part(self.from_line, 2)], [part(self.from_line, 3)]]

    def whole(self):
        l = self.links
        for n in range(4):
            l.arrived(self.slot(l.o, l.nth(n)), self.core_sems, n)


class ColumnSlice:
    def __init__(self, links, ref, stage, sems):
        self.links, self.ref, self.stage = links, ref, stage
        self.plane_sems, self.line_sems, self.core_sems = sems

    def chip(self, j, n):
        return self.links.columns[j] + 4 * self.links.nth(n)

    def slot(self, h, chip):
        return rows_at(self.ref, shard_of(h, chip) * 32, 32)

    def own(self, j, n):
        l = self.links
        piece = self.slot(l.h, self.chip(j, n))
        if n:
            l.pass_on(piece, l.nth(n), self.line_sems, (j,))
        else:
            l.along(piece, self.line_sems, (j,))
        l.send(piece, piece, self.core_sems, (j, n), (l.o, l.b))

    def start(self):
        l = self.links
        for j, chip in enumerate((l.b, l.xb, l.yb, l.db)):
            if j:
                l.send(rows_at(self.stage, j * 32, 32), self.slot(l.h, l.b), self.plane_sems, j, (l.h, chip))

    def from_plane(self, j):
        self.links.arrived(self.slot(self.links.h, self.chip(j, 0)), self.plane_sems, j)
        self.own(j, 0)

    def from_line(self, j, n):
        l = self.links
        l.arrived(self.slot(l.h, self.chip(j, n)), self.line_sems, (j, l.nth(n)))
        self.own(j, n)

    def stages(self):
        part = functools.partial
        return [
            [self.start],
            [part(self.own, 0, 0)] + [part(self.from_plane, j) for j in range(1, 4)],
            [part(self.from_line, j, n) for n in range(1, 4) for j in range(4)],
        ]

    def whole(self):
        l = self.links
        for j in range(4):
            for n in range(4):
                l.arrived(self.slot(l.o, self.chip(j, n)), self.core_sems, (j, n))


def ordered(stages, lag):
    events = []
    deepest = max(len(stage) for stage in stages)
    for tick in range(len(stages) * lag + deepest):
        for n, stage in enumerate(stages):
            if 0 <= tick - n * lag < len(stage):
                events += stage[tick - n * lag]
    return events


class Reduce:
    def __init__(self, links, g, out, base, width, bufs, sems, rows=slice(0, 128)):
        self.l, self.g, self.out, self.base, self.sems = links, g, out, base, sems
        self.by_core, self.by_side, self.by_turn, self.by_line = bufs
        self.half, self.p, self.rows = width // 2, width // 4, rows
        l = links
        self.mine = base + l.h * self.half
        p = self.p
        self.keep1 = (self.mine + l.x * (p // 2), self.mine + p + l.y * (p // 2))
        self.give1 = (self.mine + (1 - l.x) * (p // 2), self.mine + p + (1 - l.y) * (p // 2))
        self.keep2 = (self.keep1[0] + l.y * (p // 4), self.keep1[1] + l.x * (p // 4))
        self.give2 = (self.keep1[0] + (1 - l.y) * (p // 4), self.keep1[1] + (1 - l.x) * (p // 4))

    def at(self, start, width):
        return self.g.at[self.rows, pl.ds(pl.multiple_of(start, 128), width)]

    def out_at(self, start, width):
        return self.out.at[self.rows, pl.ds(pl.multiple_of(start, 128), width)]

    def chunk(self, z):
        first, second = self.keep2
        return first * (1 - z // 2) + second * (z // 2) + lax.rem(z, 2) * (self.p // 8)

    def add(self, start, width, others, final=False):
        tile = 384 if width % 384 == 0 else 128
        for n in range(width // tile):
            here = pl.ds(pl.multiple_of(start + n * tile, 128), tile)
            total = self.g[self.rows, here].astype(F4)
            for other in others:
                total = total + other[:, n * tile : (n + 1) * tile].astype(F4)
            (self.out if final else self.g)[self.rows, here] = total.astype(BF)

    def steps(self):
        l, p = self.l, self.p
        sides, turns = (l.xb, l.yb), (l.yb, l.xb)

        def cores():
            away = self.base + l.o * self.half
            l.send(self.at(away, self.half), self.by_core, self.sems, 0, (l.o, l.b))

        def side():
            l.arrived(self.by_core, self.sems, 0)
            for n in range(2):
                self.add(self.give1[n], p // 2, [self.by_core.at[:, pl.ds(pl.multiple_of(self.give1[n] - self.mine, 128), p // 2)]])
                l.send(self.at(self.give1[n], p // 2), self.by_side.at[n], self.sems, 1 + n, (l.h, sides[n]))
            for n in range(2):
                self.add(self.keep1[n], p // 2, [self.by_core.at[:, pl.ds(pl.multiple_of(self.keep1[n] - self.mine, 128), p // 2)]])

        def turn():
            for n in range(2):
                l.arrived(self.by_side.at[n], self.sems, 1 + n)
                self.add(self.keep1[n], p // 2, [self.by_side.at[n]])
                l.send(self.at(self.give2[n], p // 4), self.by_turn.at[n], self.sems, 3 + n, (l.h, turns[n]))

        def line():
            for n in range(2):
                l.arrived(self.by_turn.at[n], self.sems, 3 + n)
                self.add(self.keep2[n], p // 4, [self.by_turn.at[n]])
            for k in range(1, 4):
                away = self.chunk(lax.rem(l.z + k, 4))
                l.send(self.at(away, p // 8), self.by_line.at[k - 1], self.sems, 4 + k, (l.h, l.ahead(4 * k)))

        def line_back():
            for k in range(1, 4):
                l.arrived(self.by_line.at[k - 1], self.sems, 4 + k)
            self.add(self.chunk(l.z), p // 8, [self.by_line.at[k] for k in range(3)], True)
            here = self.out_at(self.chunk(l.z), p // 8)
            for k in range(1, 4):
                l.send(here, here, self.sems, 7 + k, (l.h, l.ahead(4 * k)))

        def turn_back():
            for k in range(1, 4):
                l.arrived(self.out_at(self.chunk(lax.rem(l.z + 4 - k, 4)), p // 8), self.sems, 7 + k)
            for n in range(2):
                here = self.out_at(self.keep2[n], p // 4)
                l.send(here, here, self.sems, 11 + n, (l.h, turns[n]))

        def side_back():
            for n in range(2):
                l.arrived(self.out_at(self.give2[n], p // 4), self.sems, 11 + n)
                here = self.out_at(self.keep1[n], p // 2)
                l.send(here, here, self.sems, 13 + n, (l.h, sides[n]))

        def cores_back():
            for n in range(2):
                l.arrived(self.out_at(self.give1[n], p // 2), self.sems, 13 + n)
            here = self.out_at(self.mine, self.half)
            l.send(here, here, self.sems, 15, (l.o, l.b))

        def done():
            l.arrived(self.out_at(self.base + l.o * self.half, self.half), self.sems, 15)

        return [cores, side, turn, line, line_back, turn_back, side_back, cores_back, done]


class SliceReduce:
    def __init__(self, links, g, out, base, bufs, sems):
        self.l, self.g, self.out, self.base, self.sems = links, g, out, base, sems
        self.by_core, self.by_line = bufs

    def at(self, ref, start, width):
        return ref.at[:, pl.ds(pl.multiple_of(start, 128), width)]

    def steps(self):
        l = self.l
        chips = (l.b, l.xb, l.yb, l.db)
        places = [
            self.base + 2048 * (lax.rem(chip, 4)) for chip in chips
        ]

        def region(j, h, z=None):
            if z is None:
                return self.at(self.out, places[j] + h * 1024, 1024)
            return self.at(self.out, places[j] + h * 1024 + z * 256, 256)

        def cores():
            l.send(self.at(self.g, l.o * 1024, 1024), self.by_core, self.sems, 0, (l.o, l.b))

        def line():
            l.arrived(self.by_core, self.sems, 0)
            for n in range(4):
                here = pl.ds(pl.multiple_of(l.h * 1024 + n * 256, 128), 256)
                total = self.g[:, here].astype(F4) + self.by_core[:, n * 256 : (n + 1) * 256].astype(F4)
                self.g[:, here] = total.astype(BF)
            for k in range(1, 4):
                z = lax.rem(l.z + k, 4)
                l.send(self.at(self.g, l.h * 1024 + z * 256, 256), self.by_line.at[k - 1], self.sems, k, (l.h, l.ahead(4 * k)))

        def line_back():
            total = self.g[:, pl.ds(pl.multiple_of(l.h * 1024 + l.z * 256, 128), 256)].astype(F4)
            for k in range(1, 4):
                l.arrived(self.by_line.at[k - 1], self.sems, k)
                total = total + self.by_line[k - 1].astype(F4)
            self.out[:, pl.ds(pl.multiple_of(places[0] + l.h * 1024 + l.z * 256, 128), 256)] = total.astype(BF)
            for k in range(1, 4):
                l.send(region(0, l.h, l.z), region(0, l.h, l.z), self.sems, 3 + k, (l.h, l.ahead(4 * k)))

        def plane():
            for k in range(1, 4):
                l.arrived(region(0, l.h, lax.rem(l.z + 4 - k, 4)), self.sems, 3 + k)
            for j in range(1, 4):
                l.send(region(0, l.h), region(0, l.h), self.sems, 6 + j, (l.h, chips[j]))
            l.send(region(0, l.h), region(0, l.h), self.sems, 10, (l.o, l.b))

        def cores_back():
            for j in range(1, 4):
                l.arrived(region(j, l.h), self.sems, 6 + j)
                l.send(region(j, l.h), region(j, l.h), self.sems, 10 + j, (l.o, l.b))

        def done():
            for j in range(4):
                l.arrived(region(j, l.o), self.sems, 10 + j)

        return [cores, line, line_back, plane, cores_back, done]


def shard_of(h, chip):
    return h * CHIPS + chip


def centre(stream):
    average = jnp.mean(stream, axis=-1, keepdims=True)
    centred = stream - average
    variance = jnp.mean(centred * centred, axis=-1, keepdims=True)
    scale = lax.rsqrt(variance + EPSILON)
    return centred * scale, scale


def norm_back(stream, gain, grad):
    hat, scale = centre(stream)
    q = grad * gain
    return scale * (
        q - jnp.mean(q, axis=-1, keepdims=True) - hat * jnp.mean(q * hat, axis=-1, keepdims=True)
    )


def gelu_parts(u):
    cubic = 0.044715 * u * u
    slope = math.sqrt(2.0 / math.pi)
    t = jnp.tanh(slope * u * (1.0 + cubic))
    grown = 0.5 * (1.0 + t)
    return u * grown, grown + 0.5 * u * (1.0 - t * t) * slope * (1.0 + 3.0 * cubic)


PIECES = 5
MIXER_D, MIXER_U, EXPAND_D, REDUCE_U, TRIPLE_D, TRIPLE_U, SLICES, COLUMNS = (
    0, 1024, 2048, 3072, 4096, 5120, 8192, 16384,
)

INPUTS = (
    "hidden", "cot", "index", "small_sh", "triple_sh", "mixer_sh", "reduce_sh", "expand_sh",
    "down_t", "up_t", "down_m", "up_m", "down_e", "up_e", "down_r", "up_r",
)
OUTPUTS = {"layer_out": ((128, 1024), BF), "hidden_grad": ((128, 1024), BF), "g": ((128, COLUMNS), BF)}
SCRATCH = {
    "wt": ((1024, 3072), BF), "wm": ((1024, 1024), BF), "wr": ((1024, 1024), BF), "we": ((1024, 1024), BF),
    "e_in": ((32, 4096), BF), "e_stage": ((128, 1024), BF), "up_es": ((128, 1024), BF), "down_rs": ((128, 1024), BF), "bias_es": ((1, 1024), F4),
    "sel": ((128, 128), F4), "small": ((512, 128), BF), "vecs": ((16, 1024), F4), "bias_t": ((1, 3072), F4), "bias_e": ((1, 4096), F4),
    "fn": ((128, 1024), BF), "rank_t": ((128, 128), BF), "kv": ((4096, 128), BF), "q": ((2048, 128), BF),
    "attden": ((2048, 128), F4), "attended": ((128, 1024), BF), "ones_v": ((4096, 128), BF),
    "send_kv": ((2048, 128), BF), "send_q": ((1024, 128), BF), "recv_q": ((1024, 128), BF),
    "send_a": ((1024, 128), BF), "recv_a": ((1024, 128), BF),
    "residual": ((128, 1024), F4), "sn_all": ((512, 1152), BF), "cot_all": ((512, 1152), BF),
    "act": ((512, 1024), BF), "agrad": ((512, 1024), BF), "ng_part": ((512, 1152), BF), "ng_recv": ((512, 1152), BF),
    "red_part": ((512, 1152), BF), "red_recv": ((512, 1152), BF),
    "send_g": ((1024, 128), BF), "recv_g": ((1024, 128), BF),
    "qd": ((2048, 128), BF), "dz": ((2048, 128), BF), "vz": ((4096, 128), BF),
    "k_t": ((64, 4096), BF), "ddrow": ((1, 2048), F4), "dq_t": ((128, 2048), F4), "part": ((4096, 128), F4),
    "recv_part": ((2048, 128), F4), "send_dkv": ((2048, 128), BF), "send_dq": ((1024, 128), BF),
    "recv_dkv": ((2048, 128), BF), "recv_dq": ((1024, 128), BF), "jg": ((128, 3072), BF),
"gp": ((128, SLICES), BF), "gs": ((128, 2048), BF), "slice_c": ((128, 1024), BF), "slice_l": ((3, 128, 256), BF),
    "early_c": ((128, 2048), BF), "early_1": ((2, 128, 512), BF), "early_2": ((2, 128, 256), BF), "early_3": ((3, 128, 128), BF),
    "late_c": ((2, 64, 2048), BF), "late_1": ((2, 2, 64, 512), BF), "late_2": ((2, 2, 64, 256), BF), "late_3": ((2, 3, 64, 128), BF),
}
SEMS = {
    "z": (PIECES, 4), "x": (PIECES, 4), "y": (PIECES, 4), "d": (PIECES, 4), "c": (PIECES, 16),
    "kv": (16,), "q": (16,), "f": (16,), "a": (16,), "g": (16,), "e": (16,), "dkv": (16,), "dq": (16,),
    "early": (16,), "late": (16,), "late_two": (16,), "slice": (16,),
    "rz": (4,), "rc": (4,), "ep": (4,), "ez": (4, 4), "ec": (4, 4), "ct": (2, 4), "sn": (2, 4), "ng": (2, 4), "rd": (2, 4),
}


def layer_kernel(*refs):
    names = list(INPUTS) + list(OUTPUTS) + list(SCRATCH)
    r = types.SimpleNamespace(**dict(zip(names, refs)))
    rest = refs[len(names) :]
    local_sem = rest[0]
    sems = {name: (rest[1 + 2 * n], rest[2 + 2 * n]) for n, name in enumerate(SEMS)}
    l = Links()
    low, low64 = half_mask(128), half_mask(64)
    mine = shard_of(l.h, l.b)
    local_copies = [
        pltpu.make_async_copy(r.small_sh, rows_at(r.small, mine * 16, 16), local_sem.at[0]),
        pltpu.make_async_copy(r.triple_sh, rows_at(r.wt, mine * 32, 32), local_sem.at[1]),
        pltpu.make_async_copy(r.mixer_sh, rows_at(r.wm, mine * 32, 32), local_sem.at[2]),
        pltpu.make_async_copy(r.reduce_sh, rows_at(r.wr, (l.h * 4 + l.z) * 128, 128), local_sem.at[3]),
        pltpu.make_async_copy(r.expand_sh, r.e_in, local_sem.at[4]),
    ]
    for copy in local_copies:
        copy.start()
    l.greet()
    adapter_of = lax.broadcasted_iota(jnp.int32, (128, 128), 0) // RANK
    r.sel[...] = jnp.where(adapter_of == r.index[...], 1.0, 0.0).T

    def columns(ref, at):
        return lambda h, chip: ref.at[
            pl.ds(pl.multiple_of(shard_of(h, chip) * 32, 32), 32), at : at + 1024
        ]

    slots = [lambda h, chip: rows_at(r.small, shard_of(h, chip) * 16, 16)]
    slots += [columns(r.wt, m * 1024) for m in range(3)]
    slots += [columns(r.wm, 0)]
    pieces = [Gather(l, n, slot, sems) for n, slot in enumerate(slots)]
    pieces.append(RowSlice(l, r.wr, (sems["rz"], sems["rc"])))
    pieces.append(ColumnSlice(l, r.we, r.e_stage, (sems["ep"], sems["ez"], sems["ec"])))
    places = [lax.rem(chip, 4) for chip in (l.b, l.xb, l.yb, l.db)]

    def block(j, i):
        return pl.ds(pl.multiple_of((i // 4 * 16 + places[j] + i % 4 * 4) * 128, 128), 128)

    for i in range(8):
        here = slice(i * 128, (i + 1) * 128)
        r.up_es[:, here] = r.up_e[:, block(0, i)]
        r.down_rs[:, here] = r.down_r[:, block(0, i)]
    for copy in local_copies:
        copy.wait()
    for i in range(8):
        here = slice(i * 128, (i + 1) * 128)
        r.we[pl.ds(pl.multiple_of(mine * 32, 32), 32), here] = r.e_in[:, block(0, i)]
        for j in range(1, 4):
            r.e_stage[j * 32 : (j + 1) * 32, here] = r.e_in[:, block(j, i)]
    l.met()
    stages = [piece.stages() for piece in pieces]
    events = [event for n in (0, 1, 2, 3, 6) for event in stages[n].pop(0)]
    stages[2][1] += stages[5].pop(0)
    events += ordered(stages[:4], 1)
    ends = {n: len(events) for n in range(4)}
    events += stages[4].pop(0)
    begun = len(events)
    events += stages[6].pop(0)
    crossed = len(events) + 8
    events += [event for stage in stages[4] for event in stage]
    ends[4] = len(events)
    events += [event for stage in stages[5] for event in stage]
    ends[5] = len(events)
    events += [event for stage in stages[6] for event in stage]
    ends[6] = len(events)
    state = [0]

    def pump(count):
        until(state[0] + count)

    def until(end):
        end = min(end, len(events))
        while state[0] < end:
            events[state[0]]()
            state[0] += 1

    def need(first, last):
        until(ends[last])
        for n in range(first, last + 1):
            pieces[n].whole()

    until(ends[3] - 4)
    pieces[0].whole()
    for g in range(8):
        tile = jnp.zeros((16, 128), F4)
        for n in range(4):
            at = (4 * g + n) * 16
            tile = tile + r.small[at : at + 16, :].astype(F4)
        r.vecs[:, g * 128 : (g + 1) * 128] = tile
        for n in range(3):
            at = (g * 3 + n) * 128
            r.bias_t[0:1, at : at + 128] = tile[6 + n : 7 + n, :]
        for n in range(4):
            at = (g * 4 + n) * 128
            r.bias_e[0:1, at : at + 128] = tile[9 + n : 10 + n, :]
    gain_one, bias_one, bias_m, gain_two, bias_two, bias_r = [
        (lambda n=n: r.vecs[n : n + 1, :]) for n in range(6)
    ]
    hat, _ = centre(r.hidden[...].astype(F4))
    r.fn[...] = (hat * gain_one() + bias_one()).astype(BF)

    def rank(source, down):
        return (r.sel[...] * by_transpose(source, down)).astype(BF)

    r.rank_t[...] = rank(r.fn[...], r.down_t[...])
    need(1, 3)
    until(begun)

    own = l.b * 256 + l.h * 128

    def kv_at(chip, h):
        return rows_at(r.kv, chip * 256 + h * 128, 128)

    kv_out = Exchange(l, r.send_kv, r.kv, 128, sems["kv"], lambda chip: kv_at(chip, l.h))
    q_out = Exchange(l, r.send_q, r.recv_q, 64, sems["q"])
    for step in range(4):
        plane = lax.rem(l.z + 1 + step, 4)

        def joint(part):
            at = pl.ds(pl.multiple_of(part * 1024 + plane * 256, 256), 256)
            tile = (
                product(r.fn[...], r.wt[:, at]) + r.bias_t[0:1, at] + product(r.rank_t[...], r.up_t[:, at])
            )
            return tile[:, :128], tile[:, 128:]

        for n, (qt, kt, vt) in enumerate(zip(joint(0), joint(1), joint(2))):
            c = plane * 4 + n * 2
            send_kv, send_q = rows_at(r.send_kv, c * 128, 256), rows_at(r.send_q, c * 64, 128)
            send_kv[0:128, :] = jnp.where(low, kt, swap(vt)).astype(BF)
            send_kv[128:256, :] = jnp.where(low, swap(kt), vt).astype(BF)
            qt = qt.astype(BF).astype(F4) * 0.125
            turned = swap(qt)
            send_q[0:64, :] = jnp.where(low64, qt[:64], turned[64:]).astype(BF)
            send_q[64:128, :] = jnp.where(low64, turned[:64], qt[64:]).astype(BF)
        for n in range(4):
            kv_out.send(plane * 4 + n)
            q_out.send(plane * 4 + n)
    kv_out.own()
    q_out.own()
    until(crossed)
    rank_grad_r = rank(r.cot[...], r.up_r[...])
    for i in range(8):
        r.bias_es[0:1, i * 128 : (i + 1) * 128] = r.bias_e[0:1, block(0, i)]

    def to_plane(source, target, name, half, own):
        for j, chip in ((3, l.db), (1, l.xb), (2, l.yb)):
            part = rows_at(source, half * 256 + (0 if own else j * 64), 64)
            l.send(part, rows_at(target, half * 256 + j * 64, 64), sems[name], (half, j), (l.h, chip))

    def from_plane(target, name, half):
        for j in range(1, 4):
            l.arrived(rows_at(target, half * 256 + j * 64, 64), sems[name], (half, j))

    def keep_own(target, at, tile):
        target[0:64, at] = tile[:64]
        target[256:320, at] = tile[64:]

    all_columns, ranks = slice(0, 1024), slice(1024, 1152)
    keep_own(r.cot_all, all_columns, r.cot[...])
    keep_own(r.cot_all, ranks, rank_grad_r)
    l.send(kv_at(l.b, l.h), kv_at(l.b, l.h), sems["f"], 0, (l.o, l.b))
    for k in range(1, CHIPS):
        kv_out.wait(k)
        c = l.behind(k)
        l.send(kv_at(c, l.h), kv_at(c, l.h), sems["f"], k, (l.o, l.b))
        until(min(state[0] + 1, ends[4]))
    to_plane(r.cot_all, r.cot_all, "ct", 0, True)
    to_plane(r.cot_all, r.cot_all, "ct", 1, True)
    until(ends[5])
    for k in range(1, CHIPS):
        q_out.wait(k)
    for k in range(CHIPS):
        l.arrived(kv_at(l.behind(k), l.o), sems["f"], k)

    for n in range(CHIPS):
        tile = r.recv_q[n * 64 : n * 64 + 64, :].astype(F4)
        r.q[n * 128 : n * 128 + 64, :] = jnp.where(low64, tile, 0.0).astype(BF)
        r.q[n * 128 + 64 : n * 128 + 128, :] = jnp.where(low64, swap(tile), 0.0).astype(BF)
        tile = r.kv[n * 256 : n * 256 + 256, :].astype(F4)
        r.ones_v[n * 256 : n * 256 + 256, :] = jnp.where(half_mask(256), 1.0, tile).astype(BF)
    a_out = Exchange(l, r.send_a, r.recv_a, 64, sems["a"])
    for i in (7, 0, 6, 1, 5, 2, 4, 3):
        queries = r.q[i * 256 : (i + 1) * 256, :]

        def fold(jj, total, masked=False):
            at = pl.ds(pl.multiple_of(jj * 512, 512), 512)
            powers = jnp.exp(by_transpose(queries, r.kv[at, :]))
            if masked:
                row = lax.broadcasted_iota(jnp.int32, (256, 512), 0)
                column = lax.broadcasted_iota(jnp.int32, (256, 512), 1)
                powers = jnp.where((row >= 128) | (column < 256), powers, 0.0)
            return total + product(powers.astype(BF), r.ones_v[at, :])

        total = fold(i, jnp.zeros((256, 128), F4), True)
        if i:
            total = lax.fori_loop(0, i, fold, total)
        share = total / swap(total)
        r.attden[i * 256 : (i + 1) * 256, :] = jnp.where(half_mask(256), total, share)
        for n in range(2):
            t = 2 * i + n
            part = share[n * 128 : n * 128 + 128]
            packed = jnp.where(low64, swap(part[64:]), part[:64]).astype(BF)
            r.send_a[t * 64 : t * 64 + 64, :] = packed
            a_out.send(t)
    a_out.own()
    until(ends[6])
    need(4, 4)
    for k in range(1, CHIPS):
        a_out.wait(k)
    for p in range(8):
        one = r.recv_a[p * 128 : p * 128 + 64, :].astype(F4)
        two = r.recv_a[p * 128 + 64 : p * 128 + 128, :].astype(F4)
        at = p * 128
        r.attended[0:64, at : at + 128] = jnp.where(low64, swap(one), two).astype(BF)
        r.attended[64:128, at : at + 128] = jnp.where(low64, one, swap(two)).astype(BF)

    rank_m = rank(r.attended[...], r.down_m[...])
    r.residual[...] = (
        r.hidden[...].astype(F4)
        + product(r.attended[...], r.wm[...])
        + bias_m()
        + product(rank_m, r.up_m[...])
    )
    hat, _ = centre(r.residual[...])
    second_normed = (hat * gain_two() + bias_two()).astype(BF)
    rank_e = rank(second_normed, r.down_e[...])
    keep_own(r.sn_all, all_columns, second_normed)
    keep_own(r.sn_all, ranks, rank_e)
    to_plane(r.sn_all, r.sn_all, "sn", 0, True)
    to_plane(r.sn_all, r.sn_all, "sn", 1, True)

    def tile_at(n, width):
        return pl.ds(pl.multiple_of(n * width, width), width)

    need(5, 6)
    from_plane(r.cot_all, "ct", 0)
    from_plane(r.cot_all, "ct", 1)

    def grad_tile(n, carry):
        at = tile_at(n, 256)
        r.agrad[:, at] = (
            by_transpose(r.cot_all[:, :1024], r.wr[at, :]) + product(r.cot_all[:, 1024:], r.down_rs[:, at])
        ).astype(BF)
        return carry

    lax.fori_loop(0, 4, grad_tile, 0)
    for half in range(2):
        from_plane(r.sn_all, "sn", half)
        these = slice(half * 256, half * 256 + 256)

        def inner_tile(n, carry):
            at = tile_at(n, 256)
            expanded = (
                product(r.sn_all[these, :1024], r.we[:, at])
                + r.bias_es[0:1, at]
                + product(r.sn_all[these, 1024:], r.up_es[:, at])
            )
            value, slope = gelu_parts(expanded)
            r.act[these, at] = value.astype(BF)
            r.agrad[these, at] = (r.agrad[these, at].astype(F4) * slope).astype(BF)
            return carry

        lax.fori_loop(0, 4, inner_tile, 0)

        def normed_tile(n, carry):
            at = tile_at(n, 256)
            r.ng_part[these, at] = by_transpose(r.agrad[these, :], r.we[at, :]).astype(BF)
            return carry

        lax.fori_loop(0, 4, normed_tile, 0)
        r.ng_part[these, 1024:] = by_transpose(r.agrad[these, :], r.up_es[...]).astype(BF)
        to_plane(r.ng_part, r.ng_recv, "ng", half, False)
    def flipped(tile):
        return tile.astype(F4).T.astype(BF)

    def reduce_tile(n, carry):
        at = tile_at(n, 256)
        r.red_part[:, at] = product(r.act[...], r.wr[:, at]).astype(BF)
        return carry

    lax.fori_loop(0, 4, reduce_tile, 0)
    r.red_part[:, 1024:] = by_transpose(r.act[...], r.down_rs[...]).astype(BF)
    rank_e_t, rank_grad_r_t = flipped(r.sn_all[:, 1024:]), flipped(r.cot_all[:, 1024:])
    for n in range(4):
        at = slice(n * 256, (n + 1) * 256)
        for kind, tile in enumerate((product(rank_e_t, r.agrad[:, at]), product(rank_grad_r_t, r.act[:, at]))):
            for m in range(2):
                to = (n * 2 + m) * 256 + kind * 128
                r.gs[:, to : to + 128] = tile[:, m * 128 : (m + 1) * 128].astype(BF)
    sliced = SliceReduce(l, r.gs, r.g, SLICES, (r.slice_c, r.slice_l), sems["slice"]).steps()
    sliced.pop(0)()
    from_plane(r.ng_recv, "ng", 0)
    from_plane(r.ng_recv, "ng", 1)

    def plane_sum(part, received, at):
        halves = []
        for start in (0, 256):
            total = part[start : start + 64, at].astype(F4)
            for j in range(1, 4):
                total = total + received[start + j * 64 : start + j * 64 + 64, at].astype(F4)
            halves.append(total)
        return jnp.concatenate(halves, axis=0)

    rank_grad_e = (r.sel[...] * plane_sum(r.ng_part, r.ng_recv, ranks)).astype(BF)
    normed_grad = plane_sum(r.ng_part, r.ng_recv, all_columns) + product(rank_grad_e, r.down_e[...])
    back_two = norm_back(r.residual[...], gain_two(), normed_grad)
    residual_grad = r.cot[...].astype(F4) + back_two
    mixed_grad = residual_grad.astype(BF)
    rank_grad_m = rank(mixed_grad, r.up_m[...])
    g_out = Exchange(l, r.send_g, r.recv_g, 64, sems["g"])
    for step in range(4):
        plane = lax.rem(l.z + 1 + step, 4)
        at = pl.ds(pl.multiple_of(plane * 256, 256), 256)
        both = by_transpose(mixed_grad, r.wm[at, :]) + product(rank_grad_m, r.down_m[:, at])
        for n in range(2):
            tile = both[:, n * 128 : n * 128 + 128]
            turned = swap(tile)
            send_g = rows_at(r.send_g, (plane * 4 + n * 2) * 64, 128)
            send_g[0:64, :] = jnp.where(low64, tile[64:], turned[:64]).astype(BF)
            send_g[64:128, :] = jnp.where(low64, turned[64:], tile[:64]).astype(BF)
        for n in range(4):
            g_out.send(plane * 4 + n)
    g_out.own()

    to_plane(r.red_part, r.red_recv, "rd", 0, False)
    to_plane(r.red_part, r.red_recv, "rd", 1, False)

    def adapter(at, left, right, width):
        for n in range(width // 512):
            r.gp[:, at + n * 512 : at + (n + 1) * 512] = product(left, right[:, n * 512 : (n + 1) * 512]).astype(BF)

    adapter(MIXER_D, flipped(rank_grad_m), r.attended, 1024)
    adapter(MIXER_U, flipped(rank_m), mixed_grad, 1024)
    adapter(EXPAND_D, flipped(rank_grad_e), second_normed, 1024)
    early = Reduce(l, r.gp, r.g, 0, TRIPLE_D, (r.early_c, r.early_1, r.early_2, r.early_3), sems["early"]).steps()

    def finish_output():
        from_plane(r.red_recv, "rd", 0)
        from_plane(r.red_recv, "rd", 1)
        rank_r = (r.sel[...] * plane_sum(r.red_part, r.red_recv, ranks)).astype(BF)
        reduced = plane_sum(r.red_part, r.red_recv, all_columns)
        r.layer_out[...] = (r.residual[...] + reduced + bias_r() + product(rank_r, r.up_r[...])).astype(BF)
        adapter(REDUCE_U, flipped(rank_r), r.cot, 1024)
        r.residual[...] = residual_grad
        early.pop(0)()

    for n in range(CHIPS):
        tile = r.kv[n * 256 : n * 256 + 256, :].astype(F4)
        wide = half_mask(256)
        r.ones_v[n * 256 : n * 256 + 256, :] = jnp.where(wide, tile, 0.0).astype(BF)
        r.vz[n * 256 : n * 256 + 256, :] = jnp.where(wide, 0.0, tile).astype(BF)
        r.k_t[:, n * 256 : n * 256 + 256] = tile.T[:64, :].astype(BF)
    r.dq_t[...] = jnp.zeros((128, 2048), F4)
    for k in range(1, CHIPS):
        g_out.wait(k)
    for n in range(CHIPS):
        at = n * 128
        g = r.recv_g[n * 64 : n * 64 + 64, :].astype(F4)
        both = r.attden[at : at + 128, :]
        grad = jnp.concatenate([g, swap(g)], axis=0)
        numer = jnp.where(low, 0.0, grad / swap(both))
        numer_low = numer.astype(BF)
        r.dz[at : at + 128, :] = numer_low
        r.qd[at : at + 128, :] = jnp.where(
            low, r.q[at : at + 128, :].astype(F4), numer_low.astype(F4)
        ).astype(BF)
        term = jnp.where(low, 0.0, numer * both)
        row = -jnp.sum(term.T, axis=0, keepdims=True)
        r.ddrow[0:1, at : at + 128] = row.astype(BF).astype(F4)
    dkv_out = Exchange(l, r.send_dkv, r.recv_dkv, 128, sems["dkv"])
    dq_out = Exchange(l, r.send_dq, r.recv_dq, 64, sems["dq"])

    def exchange(jj):
        for n in range(2):
            t = 2 * jj + n
            l.send(rows_at(r.part, t * 256 + l.o * 128, 128), rows_at(r.recv_part, t * 128, 128), sems["e"], t, (l.o, l.b))

    def finish(jj):
        for n in range(2):
            t = 2 * jj + n
            l.arrived(rows_at(r.recv_part, t * 128, 128), sems["e"], t)
            here = r.part[pl.ds(pl.multiple_of(t * 256 + l.h * 128, 128), 128), :]
            r.send_dkv[t * 128 : t * 128 + 128, :] = (here + r.recv_part[t * 128 : t * 128 + 128, :]).astype(BF)
            dkv_out.send(t)

    def finish_queries(i):
        for t in (2 * i, 2 * i + 1):
            y = r.dq_t[:, t * 128 : t * 128 + 128].T * 0.125
            r.send_dq[t * 64 : t * 64 + 64, :] = jnp.where(low64, y[:64], swap(y[64:])).astype(BF)
            dq_out.send(t)

    order = (4, 0, 5, 1, 6, 2, 7, 3)
    queries_sent = 0
    for place, jj in enumerate(order):
        keys = slice(jj * 512, jj * 512 + 512)

        def fold_back(i, total, masked=False):
            at = tile_at(i, 256)
            both = r.qd[at, :]
            powers = jnp.exp(by_transpose(r.ones_v[keys, :], both))
            if masked:
                row = lax.broadcasted_iota(jnp.int32, (512, 256), 0)
                column = lax.broadcasted_iota(jnp.int32, (512, 256), 1)
                powers = jnp.where((row < 256) | (column >= 128), powers, 0.0)
            prob = by_transpose(r.vz[keys, :], both) + r.ddrow[0:1, at]
            score = (powers * prob).astype(BF)
            r.dq_t[0:64, at] += product(r.k_t[:, keys], score)
            return total + product(score, r.q[at, :]) + product(powers.astype(BF), r.dz[at, :])

        total = fold_back(jj, jnp.zeros((512, 128), F4), True)
        if jj < 7:
            total = lax.fori_loop(jj + 1, 8, fold_back, total)
        r.part[keys, :] = total
        exchange(jj)
        if place:
            finish(order[place - 1])
        while queries_sent < 8 and all(n in order[: place + 1] for n in range(queries_sent + 1)):
            finish_queries(queries_sent)
            queries_sent += 1
        if place == 1:
            finish_output()
        for steps in {0: [sliced], 2: [sliced, early], 4: [early], 5: [sliced], 7: [early]}.get(place, []):
            steps.pop(0)()
    finish(order[-1])
    dkv_out.own()
    dq_out.own()
    for k in range(1, CHIPS):
        dkv_out.wait(k)
        dq_out.wait(k)
    early.pop(0)()
    sliced.pop(0)()
    for p in range(8):
        at = p * 128
        one = r.recv_dq[p * 128 : p * 128 + 64, :].astype(F4)
        two = r.recv_dq[p * 128 + 64 : p * 128 + 128, :].astype(F4)
        r.jg[0:64, at : at + 128] = jnp.where(low64, one, swap(two)).astype(BF)
        r.jg[64:128, at : at + 128] = jnp.where(low64, swap(one), two).astype(BF)
        one = r.recv_dkv[p * 256 : p * 256 + 128, :].astype(F4)
        two = r.recv_dkv[p * 256 + 128 : p * 256 + 256, :].astype(F4)
        r.jg[:, 1024 + at : 1152 + at] = jnp.where(low, one, swap(two)).astype(BF)
        r.jg[:, 2048 + at : 2176 + at] = jnp.where(low, swap(one), two).astype(BF)

    rank_grad_t = rank(r.jg[...], r.up_t[...])
    adapter(TRIPLE_D, flipped(rank_grad_t), r.fn, 1024)
    adapter(TRIPLE_U, flipped(r.rank_t[...]), r.jg, 3072)
    halves = [
        Reduce(
            l, r.gp, r.g, TRIPLE_D, SLICES - TRIPLE_D,
            [buf.at[n] for buf in (r.late_c, r.late_1, r.late_2, r.late_3)],
            sems[("late", "late_two")[n]], slice(n * 64, n * 64 + 64),
        ).steps()
        for n in range(2)
    ]
    late = [step for pair in zip(*halves) for step in pair]
    for _ in range(4):
        late.pop(0)()

    def triple_tile(n, carry):
        at = tile_at(n, 512)
        return carry + by_transpose(r.jg[:, at], r.wt[:, at])

    normed_grad = lax.fori_loop(0, 6, triple_tile, product(rank_grad_t, r.down_t[...]))
    back_one = norm_back(r.hidden[...].astype(F4), gain_one(), normed_grad)
    r.hidden_grad[...] = (r.residual[...] + back_one).astype(BF)
    while late or early or sliced:
        for rest in (late, late, early, sliced):
            if rest:
                rest.pop(0)()
    for out in (kv_out, q_out, a_out, g_out, dkv_out, dq_out):
        out.settle()
    l.settle()


def layer(*arrays):
    vmem = pl.BlockSpec(memory_space=pltpu.VMEM)
    hbm = pl.BlockSpec(memory_space=pl.ANY)
    dma = pltpu.SemaphoreType.DMA
    return pl.pallas_call(
        layer_kernel,
        name="layer",
        in_specs=[hbm if name.endswith("_sh") else vmem for name in INPUTS],
        out_shape=[jax.ShapeDtypeStruct(*OUTPUTS[name]) for name in OUTPUTS],
        out_specs=[vmem] * len(OUTPUTS),
        scratch_shapes=[pltpu.VMEM(*SCRATCH[name]) for name in SCRATCH]
        + [dma((5,))]
        + [dma(SEMS[name]) for name in SEMS for _ in range(2)],
        compiler_params=pltpu.CompilerParams(
            collective_id=0, has_side_effects=True, vmem_limit_bytes=LIMIT
        ),
    )(*arrays)


WRITTEN = (1024, 3072, 1024, 1024, 1024, 4096, 4096, 1024)


def write_kernel(layer_in, hidden_in, g, layer_out, hidden_out, td, tu, md, mu, ed, eu, rd, ru, low, high, in_sem, out_sem):
    passed = [
        pltpu.make_async_copy(layer_in, layer_out, out_sem.at[0]),
        pltpu.make_async_copy(hidden_in, hidden_out, out_sem.at[1]),
    ]
    reads = [
        pltpu.make_async_copy(
            g.at[:, n * 2048 : (n + 1) * 2048], low.at[:, n * 2048 : (n + 1) * 2048], in_sem.at[n]
        )
        for n in range(8)
    ]
    for copy in reads + passed:
        copy.start()
    writes = []

    def write(start, width, target, at):
        copy = pltpu.make_async_copy(
            high.at[:, start : start + width], target.at[:, at : at + width], out_sem.at[2 + len(writes)]
        )
        copy.start()
        writes.append(copy)

    whole = (
        (MIXER_D, 1024, md, 0), (MIXER_U, 1024, mu, 0), (EXPAND_D, 1024, ed, 0), (REDUCE_U, 1024, ru, 0),
        (TRIPLE_D, 1024, td, 0), (TRIPLE_U, 1024, tu, 0), (TRIPLE_U + 1024, 2048, tu, 1024),
    )
    done = 0
    for start, width, target, at in whole:
        while done * 2048 < start + width:
            reads[done].wait()
            done += 1
        high[:, start : start + width] = low[:, start : start + width].astype(F4)
        write(start, width, target, at)
    for n in range(done, 8):
        reads[n].wait()
    for h in range(2):
        for kind, target in enumerate((eu, rd)):
            to = SLICES + (h * 2 + kind) * 2048
            for z in range(4):
                for p in range(4):
                    source = SLICES + p * 2048 + h * 1024 + z * 256 + kind * 128
                    here = to + (z * 4 + p) * 128
                    high[:, here : here + 128] = low[:, source : source + 128].astype(F4)
            write(to, 2048, target, h * 2048)
    for copy in passed + writes:
        copy.wait()


def written(layer_out, hidden_grad, g):
    hbm = pl.BlockSpec(memory_space=pl.ANY)
    dma = pltpu.SemaphoreType.DMA
    return pl.pallas_call(
        write_kernel,
        name="written",
        in_specs=[hbm] * 3,
        out_shape=[jax.ShapeDtypeStruct((128, 1024), BF)] * 2 + [jax.ShapeDtypeStruct((128, width), F4) for width in WRITTEN],
        out_specs=[hbm] * 10,
        scratch_shapes=[pltpu.VMEM((128, COLUMNS), BF), pltpu.VMEM((128, COLUMNS), F4), dma((8,)), dma((16,))],
        compiler_params=pltpu.CompilerParams(vmem_limit_bytes=20 * 1024 * 1024),
    )(layer_out, hidden_grad, g)


def small_block(blocks, triple_bias, expand_bias):
    place = lax.rem(shard_of(lax.axis_index("head"), lax.axis_index("blk")), 4)
    lane = jnp.arange(128, dtype=jnp.int32)[None, :]
    six = jnp.where(lane // 32 == place, jnp.tile(jnp.stack(blocks), (1, 4)), 0)
    wide = jnp.arange(384, dtype=jnp.int32)
    three = jnp.where(wide // 96 == place, jnp.tile(triple_bias, 4), 0).reshape(3, 128)
    row = jnp.arange(4, dtype=jnp.int32)[:, None]
    four = jnp.where(row == place, expand_bias[None, :], 0)
    return jnp.concatenate([six, three, four, jnp.zeros((3, 128), BF)], axis=0).astype(BF)


def local_fast(
    hidden, adapter_index, first_gain, first_bias, triple_weight, triple_bias, mixer_weight, mixer_bias,
    second_gain, second_bias, expand_weight, expand_bias, reduce_weight, reduce_bias, triple_down, triple_up,
    mixer_down, mixer_up, expand_down, expand_up, reduce_down, reduce_up, cotangent,
):
    def turned(factor):
        return jnp.transpose(factor, (0, 2, 1)).reshape(ADAPTERS * RANK, factor.shape[1])

    small_sh = small_block(
        [first_gain, first_bias, mixer_bias, second_gain, second_bias, reduce_bias], triple_bias, expand_bias
    )
    layer_out, hidden_grad, g = layer(
        hidden, cotangent, adapter_index.reshape(1, 128), small_sh, triple_weight, mixer_weight, reduce_weight, expand_weight,
        turned(triple_down), flat_up(triple_up), turned(mixer_down), flat_up(mixer_up),
        turned(expand_down), flat_up(expand_up), turned(reduce_down), flat_up(reduce_up),
    )
    layer_out, hidden_grad, *grads = written(layer_out, hidden_grad, g)

    def down_out(part):
        return jnp.transpose(part.reshape(ADAPTERS, RANK, part.shape[1]), (0, 2, 1))

    def up_out(part):
        return part.reshape(ADAPTERS, RANK, part.shape[1])

    shaped = [down_out, up_out, down_out, up_out, down_out, up_out, down_out, up_out]
    return (layer_out, hidden_grad) + tuple(shape(part) for shape, part in zip(shaped, grads))


def solution(mesh):
    placed = (
        P(("blk", "head"), None),
        P(("blk", "head")),
        P(("head", "blk")),
        P(("head", "blk")),
        P(("head", "blk"), None),
        P(("head", "blk")),
        P(("head", "blk"), None),
        P(("head", "blk")),
        P(("head", "blk")),
        P(("head", "blk")),
        P(("head", "blk"), None),
        P(("head", "blk")),
        P(("head", "blk"), None),
        P(("head", "blk")),
        P(),
        P(),
        P(),
        P(),
        P(),
        P(),
        P(),
        P(),
        P(("blk", "head"), None),
    )
    fits = tuple(mesh.shape[name] for name in ("head", "blk")) == (2, CHIPS)
    return jax.shard_map(
        local_fast if fits else local,
        mesh=mesh,
        in_specs=placed,
        out_specs=(
            P(("blk", "head"), None),
            P(("blk", "head"), None),
            P(),
            P(),
            P(),
            P(),
            P(),
            P(),
            P(),
            P(),
        ),
        check_vma=False,
    )
```
